32 devices in a mesh: wide: 8 (over z, x), narrow: 4 (over y, core).
Axes of the slice: x: 2, y: 2, z: 4, core: 2. Of those that a mesh axis runs over, the one named last changes fastest.
Arguments:
- inputs: bfloat16 [64, 1024, 768], P(('wide', 'narrow')), may hold values from -6 to 6
- tok_landmark: int32 [64, 1024], P(('wide', 'narrow')), may hold values from 0 to 63, never falling along the last dimension, each value on 1 to 32 neighbouring positions
- landmark_doc: int32 [64, 64], P(('wide', 'narrow')), may hold values from 0 to 3, never falling along the last dimension, each value on 1 to 48 neighbouring positions
- w_query: bfloat16 [768, 768], P(None, ('wide', 'narrow')), may hold values from -0.75 to 0.75
- b_query: bfloat16 [768], P(('wide', 'narrow')), may hold values from -4 to 4
- w_key: bfloat16 [768, 768], P(None, ('wide', 'narrow')), may hold values from -0.75 to 0.75
- w_value: bfloat16 [768, 768], P(None, ('wide', 'narrow')), may hold values from -0.21875 to 0.21875
- b_value: bfloat16 [768], P(('wide', 'narrow')), may hold values from -3 to 3
- conv_weight: bfloat16 [33, 768], P(None, ('wide', 'narrow')), may hold values from -0.5 to 0.5
- w_out: bfloat16 [768, 768], P(None, ('wide', 'narrow')), may hold values from -0.4375 to 0.4375
- b_out: bfloat16 [768], P(('wide', 'narrow')), may hold values from -3 to 3
- gain_one: bfloat16 [768], P(('wide', 'narrow')), may hold values from 0.5 to 1.5
- shift_one: bfloat16 [768], P(('wide', 'narrow')), may hold values from -3 to 3
- w_up: bfloat16 [768, 3072], P(None, ('wide', 'narrow')), may hold values from -0.21875 to 0.21875
- b_up: bfloat16 [3072], P(('wide', 'narrow')), may hold values from -3 to 3
- w_down: bfloat16 [3072, 768], P(None, ('wide', 'narrow')), may hold values from -0.15625 to 0.15625
- b_down: bfloat16 [768], P(('wide', 'narrow')), may hold values from -3 to 3
- gain_two: bfloat16 [768], P(('wide', 'narrow')), may hold values from 0.5 to 1.5
- shift_two: bfloat16 [768], P(('wide', 'narrow')), may hold values from -3 to 3
- cotangent: bfloat16 [64, 1024, 768], P(('wide', 'narrow')), may hold values from -6 to 6
Outputs:
- layer_out: bfloat16 [64, 1024, 768], P(('wide', 'narrow'))
- input_grad: float32 [64, 1024, 768], P(('wide', 'narrow'))
- grad_w_query: float32 [768, 768], P(None, ('wide', 'narrow'))
- grad_b_query: float32 [768], P(('wide', 'narrow'))
- grad_w_key: float32 [768, 768], P(None, ('wide', 'narrow'))
- grad_w_value: float32 [768, 768], P(None, ('wide', 'narrow'))
- grad_b_value: float32 [768], P(('wide', 'narrow'))
- grad_conv: float32 [33, 768], P(None, ('wide', 'narrow'))
- grad_w_out: float32 [768, 768], P(None, ('wide', 'narrow'))
- grad_b_out: float32 [768], P(('wide', 'narrow'))
- grad_gain_one: float32 [768], P(('wide', 'narrow'))
- grad_shift_one: float32 [768], P(('wide', 'narrow'))
- grad_w_up: float32 [768, 3072], P(None, ('wide', 'narrow'))
- grad_b_up: float32 [3072], P(('wide', 'narrow'))
- grad_w_down: float32 [3072, 768], P(None, ('wide', 'narrow'))
- grad_b_down: float32 [768], P(('wide', 'narrow'))
- grad_gain_two: float32 [768], P(('wide', 'narrow'))
- grad_shift_two: float32 [768], P(('wide', 'narrow'))
The draws below stay inside these ranges and needn't reach their ends.
Inputs may be any that keep to these rules, and one draw needn't show every extreme that they name: `tok_landmark`: in each sequence the landmark numbers never fall along the tokens and each of the 64 landmarks holds 1 to 32 tokens. `landmark_doc`: in each sequence the document numbers never fall along the landmarks and each of the 4 documents holds 1 to 48 landmarks.
All inputs are finite; a program needn't handle non-finite values.
Results may differ from the reference program's by a relative error of at most 0.0095.
Values may be sent and summed in bfloat16 or wider, within the bound.
No kernel may reach another device: no remote copies, remote signals or barrier semaphores. Data moves between devices by JAX's collectives and lax.ppermute only.
A program may use at most 576 MiB of HBM per device.

```python
import math
import jax
import jax.numpy as jnp
import numpy as np
from jax import lax

D = 768
HEAD_COUNT = 12
HEAD_WIDTH = 64
FF = 3072
LANDMARKS = 64
KW = 33
NEWTON = 6
DOCS = 4
L = 1024
ROWS = 64


def strengthened(values, key, source, target, parts, factor):
    def block_of(position):
        return (jnp.arange(values.shape[position]) // (values.shape[position] // parts)).reshape((-1,) + (1,) * (values.ndim - 1 - position))

    near = jax.random.permutation(key, parts)[block_of(target)]
    second = (block_of(target) + parts // 2) % parts
    return jnp.where((block_of(source) == near) | (block_of(source) == second), factor * values, values)


def block_levels(rng, dims, split, least, largest):
    factor_of = 1.0
    for axis_at, parts in split:
        steps = jax.random.uniform(jax.random.fold_in(jax.random.fold_in(rng, 6), axis_at), (parts,), jnp.float32, least / len(split), largest / len(split))
        factor_of = factor_of * jnp.repeat(jnp.exp(steps), dims[axis_at] // parts).reshape((-1,) + (1,) * (len(dims) - 1 - axis_at))
    return factor_of


def length_profile(number_of, total, bound, lean):
    weights = [(1 << 20) // math.isqrt(grade ** lean) + 1 for grade in range(2, number_of + 1)]
    surplus, given = total - bound - (number_of - 1), [1] * (number_of - 1)
    while surplus > 0:
        candidates = [i for i in range(number_of - 1) if given[i] < bound]
        pool, left = sum([weights[i] for i in candidates]), surplus
        for i in candidates:
            addition = min(bound - given[i], max(1, left * weights[i] // pool), surplus)
            given[i] = given[i] + addition
            surplus = surplus - addition
    return np.array([bound] + given)


def uneven_parts(own_key, count, total, limit, skew):
    if count == 2:
        one = jax.random.randint(own_key, (), max(1, total - limit), min(limit, total - 1) + 1)
        return jnp.stack([one, total - one])
    tallies = jnp.asarray(length_profile(count, total, limit, skew), jnp.int32)
    pairs = (count - 1) // 2
    source_of, sink = tallies[1:1 + 2 * pairs:2], tallies[2:2 + 2 * pairs:2]
    margin = jnp.minimum(source_of - 1, limit - sink)
    passed = jax.random.randint(jax.random.fold_in(own_key, 1), (pairs,), 0, 1 << 20) % (margin + 1)
    tallies = tallies.at[1:1 + 2 * pairs:2].set(source_of - passed).at[2:2 + 2 * pairs:2].set(sink + passed)
    return tallies[jax.random.permutation(jax.random.fold_in(own_key, 2), count)]


def centred(own_key, extent, deviation, bound, split=(), kind=jnp.bfloat16):
    level = block_levels(own_key, extent, split, -0.22, 0.18) if split else 1.0
    entries = jax.random.normal(own_key, extent, jnp.float32) * deviation * level
    return jnp.minimum(jnp.maximum(entries, -bound), bound).astype(kind)


def gaussian_with(key, extent, deviation, bound, split, heavy, held_as=jnp.bfloat16):
    array = deviation * jax.random.normal(key, extent, jnp.float32)
    if split:
        array = array * block_levels(key, extent, split, -0.22, 0.18)
    return jnp.clip(strengthened(array, jax.random.fold_in(key, 3), *heavy), -bound, bound).astype(held_as)


def setup_inputs(seed: int = 0) -> dict:
    arg_keys = jax.random.split(jax.random.key(seed), 21)
    return {
        "inputs": centred(arg_keys[0], (ROWS, L, D), 1.0, 6.0, ((0, 32),)),
        "tok_landmark": jax.vmap(lambda own: jnp.searchsorted(jnp.cumsum(uneven_parts(own, LANDMARKS, L, 2 * L // LANDMARKS, 1)), jnp.arange(L), side="right"))(jax.random.split(arg_keys[1], ROWS)).reshape((ROWS, L)).astype(jnp.int32),
        "landmark_doc": jax.vmap(lambda own: jnp.searchsorted(jnp.cumsum(uneven_parts(own, DOCS, LANDMARKS, 3 * LANDMARKS // 4, 1)), jnp.arange(LANDMARKS), side="right"))(jax.random.split(arg_keys[2], ROWS)).reshape((ROWS, LANDMARKS)).astype(jnp.int32),
        "w_query": centred(arg_keys[3], (D, D), (D // 12) ** -0.5, 0.75, ((1, 32),)),
        "b_query": centred(arg_keys[4], (D,), 1.0, 4.0, ((0, 32),)),
        "w_key": centred(arg_keys[5], (D, D), (D // 12) ** -0.5, 0.75, ((1, 32),)),
        "w_value": centred(arg_keys[6], (D, D), D ** -0.5, 0.21875, ((1, 32),)),
        "b_value": centred(arg_keys[7], (D,), 0.5, 3.0, ((0, 32),)),
        "conv_weight": centred(arg_keys[8], (KW, D), (4 * KW) ** -0.5, 0.5, ((1, 32),)),
        "w_out": centred(arg_keys[9], (D, D), (D // 4) ** -0.5, 0.4375, ((1, 32),)),
        "b_out": centred(arg_keys[10], (D,), 0.5, 3.0, ((0, 32),)),
        "gain_one": jnp.clip(1.0 + 0.1 * jax.random.normal(arg_keys[11], (D,), jnp.float32), 0.5, 1.5).astype(jnp.bfloat16),
        "shift_one": centred(arg_keys[12], (D,), 0.5, 3.0, ((0, 32),)),
        "w_up": centred(arg_keys[13], (D, FF), D ** -0.5, 0.21875, ((1, 32),)),
        "b_up": centred(arg_keys[14], (FF,), 0.5, 3.0, ((0, 32),)),
        "w_down": centred(arg_keys[15], (FF, D), (FF // 2) ** -0.5, 0.15625, ((1, 32),)),
        "b_down": centred(arg_keys[16], (D,), 0.5, 3.0, ((0, 32),)),
        "gain_two": jnp.clip(1.0 + 0.1 * jax.random.normal(arg_keys[17], (D,), jnp.float32), 0.5, 1.5).astype(jnp.bfloat16),
        "shift_two": centred(arg_keys[18], (D,), 0.5, 3.0, ((0, 32),)),
        "cotangent": gaussian_with(arg_keys[19], (ROWS, L, D), 1.0, 6.0, ((0, 32),), (0, 2, 32, 2.75)),
    }


@jax.custom_vjp
def low(v):
    return lax.optimization_barrier(v.astype(jnp.bfloat16)).astype(jnp.float32)

@jax.custom_vjp
def low_back(v):
    return v

def low_keep(v):
    return (low(v), None)

def low_pass(kept, grad):
    return (grad,)

def back_keep(v):
    return (v, None)

def back_low(kept, grad):
    return (low(grad),)
low.defvjp(low_keep, low_pass)
low_back.defvjp(back_keep, back_low)
HIGHEST = lax.Precision.HIGHEST

def batch_mapped(left_side, right_side, form):
    return jnp.einsum(form, left_side, right_side, precision=HIGHEST)

def hdot(left_side, right_side):
    return jnp.dot(left_side, right_side, precision=HIGHEST, preferred_element_type=jnp.float32)

def softmax_with_mask(scores, allowed):
    held_scores = jnp.where(allowed, scores, -1e+30)
    row_top = lax.optimization_barrier(jnp.max(held_scores, axis=-1, keepdims=True))
    raised = jnp.where(allowed, jnp.exp(held_scores - row_top), 0.0)
    return raised / lax.optimization_barrier(jnp.sum(raised, axis=-1, keepdims=True))

def newton_inverse(kernel):
    identity = jnp.eye(kernel.shape[-1], dtype=kernel.dtype)
    approx = jnp.swapaxes(kernel, 1, 2) / lax.optimization_barrier(jnp.sum(kernel * kernel, axis=(1, 2), keepdims=True))
    for iteration in range(NEWTON):
        product = batch_mapped(kernel, approx, 'hij,hjk->hik')
        inner_term = 7.0 * identity - product
        inner_term = 15.0 * identity - batch_mapped(product, inner_term, 'hij,hjk->hik')
        outer_term = 13.0 * identity - batch_mapped(product, inner_term, 'hij,hjk->hik')
        approx = 0.25 * batch_mapped(approx, outer_term, 'hij,hjk->hik')
    return approx

def nystrom(query_rows, key_rows, value_rows, conv_weight, tok_landmark, landmark_doc):
    sequence_length = query_rows.shape[0]
    membership = tok_landmark[:, None] == jnp.arange(LANDMARKS, dtype=jnp.int32)[None, :]
    document_indicator = membership.astype(query_rows.dtype)
    landmark_counts = lax.optimization_barrier(jnp.sum(document_indicator, axis=0))
    doc_tok = lax.optimization_barrier(jnp.sum(jnp.where(membership, landmark_doc[None, :], 0), axis=1))
    first_document_mask = doc_tok[:, None] == landmark_doc[None, :]
    second_document_mask = landmark_doc[:, None] == landmark_doc[None, :]
    scaling = HEAD_WIDTH ** (-0.25)
    query_heads = (query_rows * scaling).reshape(sequence_length, HEAD_COUNT, HEAD_WIDTH)
    key_heads = (key_rows * scaling).reshape(sequence_length, HEAD_COUNT, HEAD_WIDTH)
    value_heads = value_rows.reshape(sequence_length, HEAD_COUNT, HEAD_WIDTH)
    landmark_queries = batch_mapped(document_indicator, query_heads, 'kp,ksz->spz') / landmark_counts[None, :, None]
    landmark_keys = batch_mapped(document_indicator, key_heads, 'kp,ksz->spz') / landmark_counts[None, :, None]
    first_kernel = softmax_with_mask(batch_mapped(query_heads, landmark_keys, 'kxs,xfs->xkf'), first_document_mask[None])
    middle_kernel = softmax_with_mask(batch_mapped(landmark_queries, landmark_keys, 'cfo,cto->cft'), second_document_mask[None])
    third_kernel = softmax_with_mask(batch_mapped(landmark_queries, key_heads, 'ryx,srx->rys'), first_document_mask.T[None])
    carry_state = batch_mapped(third_kernel, value_heads, 'cyn,ncr->cyr')
    carry_state = batch_mapped(newton_inverse(middle_kernel), carry_state, 'otz,ozu->otu')
    mixed_context = batch_mapped(first_kernel, carry_state, 'fve,feg->vfg').reshape(sequence_length, HEAD_COUNT * HEAD_WIDTH)
    half_width = KW // 2
    padded = jnp.pad(value_rows, ((half_width, half_width), (0, 0)))
    padded_doc = jnp.pad(doc_tok, (half_width, half_width), constant_values=-1)
    for offset in range(KW):
        inside = (padded_doc[offset:offset + sequence_length] == doc_tok)[:, None]
        mixed_context = mixed_context + jnp.where(inside, conv_weight[offset][None, :] * padded[offset:offset + sequence_length], 0.0)
    return mixed_context

def norm_apply(values, gain_vec, shift_vec):
    row_mean = lax.optimization_barrier(jnp.mean(values, axis=-1, keepdims=True))
    centered = values - row_mean
    variance = lax.optimization_barrier(jnp.mean(centered * centered, axis=-1, keepdims=True))
    return centered * lax.rsqrt(variance + 1e-05) * gain_vec + shift_vec

def layer_one(params, rows_in, tok_landmark, landmark_doc):
    w_query, b_query, w_key, w_value, b_value, conv_weight, w_out, b_out, gain_one, shift_one, w_up, b_up, w_down, b_down, gain_two, shift_two = params
    query_rows = low_back(hdot(rows_in, w_query) + b_query)
    key_rows = low_back(hdot(rows_in, w_key))
    value_rows = low_back(hdot(rows_in, w_value) + b_value)
    mixed_context = low(nystrom(query_rows, key_rows, value_rows, conv_weight, tok_landmark, landmark_doc))
    attended = low_back(hdot(mixed_context, w_out) + b_out)
    normed = norm_apply(rows_in + attended, gain_one, shift_one)
    up_pre = low_back(hdot(low(normed), w_up) + b_up)
    hidden = low(jax.nn.gelu(up_pre, approximate=False))
    down_out = low_back(hdot(hidden, w_down) + b_down)
    return norm_apply(normed + down_out, gain_two, shift_two)

def reference(inputs, tok_landmark, landmark_doc, w_query, b_query, w_key, w_value, b_value, conv_weight, w_out, b_out, gain_one, shift_one, w_up, b_up, w_down, b_down, gain_two, shift_two, cotangent):
    params = tuple((weight.astype(jnp.float32) for weight in (w_query, b_query, w_key, w_value, b_value, conv_weight, w_out, b_out, gain_one, shift_one, w_up, b_up, w_down, b_down, gain_two, shift_two)))

    def forward(weights, rows_all):

        def one_sequence(packed):
            return layer_one(weights, packed[0], packed[1], packed[2])
        return lax.map(jax.checkpoint(one_sequence), (rows_all, tok_landmark, landmark_doc))
    outputs, pullback = jax.vjp(forward, params, inputs.astype(jnp.float32))
    gradients, input_grad = pullback(cotangent.astype(jnp.float32))
    return (outputs.astype(jnp.bfloat16), input_grad, gradients[0], gradients[1], gradients[2], gradients[3], gradients[4], gradients[5], gradients[6], gradients[7], gradients[8], gradients[9], gradients[10], gradients[11], gradients[12], gradients[13], gradients[14], gradients[15])
```

```python
import jax
import jax.numpy as jnp
from jax import lax
from jax.sharding import PartitionSpec as P

HEAD_COUNT = 12
HEAD_WIDTH = 64
LANDMARKS = 64
KW = 33
NEWTON = 6


HIGHEST = lax.Precision.HIGHEST


def batch_mapped(left_side, right_side, form):
    return jnp.einsum(form, left_side, right_side, precision=HIGHEST)


def softmax_with_mask(scores, allowed):
    held_scores = jnp.where(allowed, scores, -1e30)
    row_top = jnp.max(held_scores, axis=-1, keepdims=True)
    raised = jnp.where(allowed, jnp.exp(held_scores - row_top), 0.0)
    return raised / jnp.sum(raised, axis=-1, keepdims=True)


def newton_inverse(kernel):
    identity = jnp.eye(kernel.shape[-1], dtype=kernel.dtype)
    approx = jnp.swapaxes(kernel, 1, 2) / jnp.sum(kernel * kernel, axis=(1, 2), keepdims=True)
    for iteration in range(NEWTON):
        product = batch_mapped(kernel, approx, "hij,hjk->hik")
        inner_term = 7.0 * identity - product
        inner_term = 15.0 * identity - batch_mapped(product, inner_term, "hij,hjk->hik")
        outer_term = 13.0 * identity - batch_mapped(product, inner_term, "hij,hjk->hik")
        approx = 0.25 * batch_mapped(approx, outer_term, "hij,hjk->hik")
    return approx


def nystrom(query_rows, key_rows, value_rows, conv_weight, tok_landmark, landmark_doc):
    sequence_length = query_rows.shape[0]
    membership = tok_landmark[:, None] == jnp.arange(LANDMARKS, dtype=jnp.int32)[None, :]
    document_indicator = membership.astype(query_rows.dtype)
    landmark_counts = jnp.sum(document_indicator, axis=0)
    doc_tok = jnp.sum(jnp.where(membership, landmark_doc[None, :], 0), axis=1)
    first_document_mask = doc_tok[:, None] == landmark_doc[None, :]
    second_document_mask = landmark_doc[:, None] == landmark_doc[None, :]
    scaling = HEAD_WIDTH ** (-0.25)
    query_heads = (query_rows * scaling).reshape(sequence_length, HEAD_COUNT, HEAD_WIDTH)
    key_heads = (key_rows * scaling).reshape(sequence_length, HEAD_COUNT, HEAD_WIDTH)
    value_heads = value_rows.reshape(sequence_length, HEAD_COUNT, HEAD_WIDTH)
    landmark_queries = (
        batch_mapped(document_indicator, query_heads, "kp,ksz->spz")
        / landmark_counts[None, :, None]
    )
    landmark_keys = (
        batch_mapped(document_indicator, key_heads, "kp,ksz->spz") / landmark_counts[None, :, None]
    )
    first_kernel = softmax_with_mask(
        batch_mapped(query_heads, landmark_keys, "kxs,xfs->xkf"), first_document_mask[None]
    )
    middle_kernel = softmax_with_mask(
        batch_mapped(landmark_queries, landmark_keys, "cfo,cto->cft"), second_document_mask[None]
    )
    third_kernel = softmax_with_mask(
        batch_mapped(landmark_queries, key_heads, "ryx,srx->rys"), first_document_mask.T[None]
    )
    carry_state = batch_mapped(third_kernel, value_heads, "cyn,ncr->cyr")
    carry_state = batch_mapped(newton_inverse(middle_kernel), carry_state, "otz,ozu->otu")
    mixed_context = batch_mapped(first_kernel, carry_state, "fve,feg->vfg").reshape(
        sequence_length, HEAD_COUNT * HEAD_WIDTH
    )
    half_width = KW // 2
    padded = jnp.pad(value_rows, ((half_width, half_width), (0, 0)))
    padded_doc = jnp.pad(doc_tok, (half_width, half_width), constant_values=-1)
    for offset in range(KW):
        inside = (padded_doc[offset : offset + sequence_length] == doc_tok)[:, None]
        mixed_context = mixed_context + jnp.where(
            inside, conv_weight[offset][None, :] * padded[offset : offset + sequence_length], 0.0
        )
    return mixed_context


def normalize(values):
    row_mean = jnp.mean(values, axis=-1, keepdims=True)
    centered = values - row_mean
    inv_std = lax.rsqrt(jnp.mean(centered * centered, axis=-1, keepdims=True) + 1e-05)
    return (centered * inv_std, inv_std)


def norm_back(upstream, normal, inv_std, gain_vec):
    scaled = upstream * gain_vec
    inner_mean = jnp.mean(scaled, axis=-1, keepdims=True)
    cross_mean = jnp.mean(scaled * normal, axis=-1, keepdims=True)
    return (
        inv_std * (scaled - inner_mean - normal * cross_mean),
        jnp.sum(upstream * normal, axis=0),
        jnp.sum(upstream, axis=0),
    )


def forward_dot(left_side, right_side):
    return jnp.dot(left_side, right_side, preferred_element_type=jnp.float32)


def across_rows(left_side, right_side):
    return lax.dot_general(
        left_side, right_side, (((0,), (0,)), ((), ())), preferred_element_type=jnp.float32
    )


def against_cols(left_side, right_side):
    return lax.dot_general(
        left_side, right_side, (((1,), (1,)), ((), ())), preferred_element_type=jnp.float32
    )


def column_sums(values):
    return jnp.sum(values.astype(jnp.float32), axis=0)


def gelu_exact(values):
    return jax.nn.gelu(values, approximate=False)


def digits():
    found = []
    for axis in ("wide", "narrow"):
        stride = lax.axis_size(axis) // 2
        while stride >= 1:
            found.append((axis, stride))
            stride //= 2
    return found


def stage_orders():
    count = len(digits())
    if lax.axis_size("wide") == 8 and lax.axis_size("narrow") == 4:
        return [(4, 2, 3, 1, 0), (4, 3, 1, 2, 0), (4, 1, 2, 3, 0)]
    return [tuple(range(count - 1, -1, -1))] * 3


def exchange(values, axis, stride):
    return lax.ppermute(values, axis, [(i, i ^ stride) for i in range(lax.axis_size(axis))])


def digit_of(axis, stride):
    return (lax.axis_index(axis) // stride) % 2


def gather_rows(shard):
    rows, columns = shard.shape
    places = digits()
    width = columns // 3
    parts = []
    for number, order in enumerate(stage_orders()):
        held = shard[:, number * width : (number + 1) * width]
        held = held.reshape((1,) * len(places) + (rows, width))
        for dim in order[::-1]:
            mine = digit_of(*places[dim])
            got = exchange(held, *places[dim])
            first = jnp.where(mine == 0, held, got)
            second = jnp.where(mine == 0, got, held)
            held = jnp.concatenate([first, second], dim)
        parts.append(held.reshape(-1, rows, width))
    return jnp.concatenate(parts, 2)


def scatter_rows(whole):
    _, rows, columns = whole.shape
    places = digits()
    width = columns // 3
    parts = []
    for number, order in enumerate(stage_orders()):
        held = whole[:, :, number * width : (number + 1) * width]
        held = held.reshape((2,) * len(places) + (rows, width))
        for dim in order:
            mine = digit_of(*places[dim])
            keep = lax.dynamic_slice_in_dim(held, mine, 1, dim).astype(jnp.float32)
            send = lax.dynamic_slice_in_dim(held, 1 - mine, 1, dim).astype(jnp.bfloat16)
            held = keep + exchange(send, *places[dim]).astype(jnp.float32)
        parts.append(held.reshape(rows, width))
    return jnp.concatenate(parts, 1)


def pad_rows(flat, rows):
    count, length = flat.shape
    return jnp.pad(flat, ((0, 0), (0, rows * 768 - length))).reshape(count, rows, 768)


def shards(
    inputs,
    tok_landmark,
    landmark_doc,
    w_query,
    b_query,
    w_key,
    w_value,
    b_value,
    conv_weight,
    w_out,
    b_out,
    gain_one,
    shift_one,
    w_up,
    b_up,
    w_down,
    b_down,
    gain_two,
    shift_two,
    cotangent,
):
    batch_rows, sequence_length, feature_width = inputs.shape
    group_count = lax.axis_size("wide") * lax.axis_size("narrow")
    own = feature_width // group_count
    vectors = (b_query, b_value, b_out, gain_one, shift_one, b_down, gain_two, shift_two)
    flat = jnp.concatenate([conv_weight.T.reshape(-1)] + list(vectors) + [b_up])
    small_rows = -(-flat.shape[0] // 768)
    small = pad_rows(flat[None], small_rows)[0]
    bundle = jnp.concatenate([w_query.T, w_key.T, w_value.T, small], axis=0)
    gathered = gather_rows(bundle)
    w_q, w_k, w_v = [
        gathered[:, i * own : (i + 1) * own].reshape(feature_width, feature_width) for i in range(3)
    ]
    small = gathered[:, 3 * own :].reshape(group_count, -1)
    conv_full = small[:, : own * KW].reshape(feature_width, KW).T
    small = small[:, own * KW :]
    b_q, b_v, b_o, g_one, s_one, b_d, g_two, s_two = [
        small[:, i * own : (i + 1) * own].reshape(feature_width).astype(jnp.float32)
        for i in range(8)
    ]
    b_u = small[:, 8 * own : 8 * own + b_up.shape[0]].reshape(-1).astype(jnp.float32)
    later = lax.optimization_barrier((w_out.T, w_up.T, w_down.T, gathered))
    w_o, w_u, w_d = [
        lax.all_gather(shard, ("wide", "narrow"), axis=0, tiled=True) for shard in later[:3]
    ]
    rows_low = inputs.reshape(batch_rows * sequence_length, feature_width)
    rows_in = rows_low.astype(jnp.float32)
    query_rows = against_cols(rows_low, w_q) + b_q
    key_rows = against_cols(rows_low, w_k)
    value_rows = against_cols(rows_low, w_v) + b_v

    def attend(query_part, key_part, value_part, conv_part):
        shaped = (batch_rows, sequence_length, feature_width)
        mixed = jax.vmap(nystrom, in_axes=(0, 0, 0, None, 0, 0))(
            query_part.reshape(shaped),
            key_part.reshape(shaped),
            value_part.reshape(shaped),
            conv_part,
            tok_landmark,
            landmark_doc,
        )
        return mixed.reshape(batch_rows * sequence_length, feature_width)

    conv_taps = conv_full.astype(jnp.float32)
    mixed_context = attend(query_rows, key_rows, value_rows, conv_taps)
    context_low = mixed_context.astype(jnp.bfloat16)
    attended = against_cols(context_low, w_o) + b_o
    normal_one, inv_one = normalize(rows_in + attended)
    normed = normal_one * g_one + s_one
    normed_low = normed.astype(jnp.bfloat16)
    up_pre = against_cols(normed_low, w_u) + b_u
    hidden = gelu_exact(up_pre).astype(jnp.bfloat16)
    down_out = against_cols(hidden, w_d) + b_d
    normal_two, inv_two = normalize(normed + down_out)
    layer_out = (normal_two * g_two + s_two).astype(jnp.bfloat16)
    upstream = cotangent.reshape(batch_rows * sequence_length, feature_width).astype(jnp.float32)
    grad_two, grad_gain_two, grad_shift_two = norm_back(upstream, normal_two, inv_two, g_two)
    down_low = grad_two.astype(jnp.bfloat16)
    grad_w_down = across_rows(down_low, hidden)
    grad_b_down = column_sums(down_low)
    hidden_grad = forward_dot(down_low, w_d)
    up_low = jax.vjp(gelu_exact, up_pre)[1](hidden_grad)[0].astype(jnp.bfloat16)
    grad_w_up = across_rows(up_low, normed_low)
    grad_b_up = column_sums(up_low)
    normed_grad = grad_two + forward_dot(up_low, w_u)
    grad_one, grad_gain_one, grad_shift_one = norm_back(normed_grad, normal_one, inv_one, g_one)
    attended_low = grad_one.astype(jnp.bfloat16)
    grad_w_out = across_rows(attended_low, context_low)
    grad_b_out = column_sums(attended_low)
    context_grad = forward_dot(attended_low, w_o)

    def by_device(values):
        return values.reshape((group_count, -1) + values.shape[1:])

    early_vectors = (
        grad_b_out,
        grad_gain_one,
        grad_shift_one,
        grad_b_down,
        grad_gain_two,
        grad_shift_two,
        grad_b_up,
    )
    early = jnp.concatenate([by_device(v) for v in early_vectors], axis=1)
    early_rows = -(-early.shape[1] // 768)
    share_up = scatter_rows(by_device(grad_w_up))
    share_down = scatter_rows(by_device(grad_w_down))
    share_out = scatter_rows(
        jnp.concatenate([by_device(grad_w_out), pad_rows(early, early_rows)], axis=1)
    )
    pullback = jax.vjp(attend, query_rows, key_rows, value_rows, conv_taps)[1]
    query_grad, key_grad, value_grad, grad_conv = pullback(context_grad)
    query_low = query_grad.astype(jnp.bfloat16)
    key_low = key_grad.astype(jnp.bfloat16)
    value_low = value_grad.astype(jnp.bfloat16)
    late = jnp.concatenate(
        [
            by_device(grad_conv.T).reshape(group_count, -1),
            by_device(column_sums(query_low)),
            by_device(column_sums(value_low)),
        ],
        axis=1,
    )
    late_rows = -(-late.shape[1] // 768)
    share_late = scatter_rows(
        jnp.concatenate(
            [
                by_device(across_rows(query_low, rows_low)),
                by_device(across_rows(key_low, rows_low)),
                by_device(across_rows(value_low, rows_low)),
                pad_rows(late, late_rows),
            ],
            axis=1,
        )
    )
    input_grad = (
        grad_one
        + forward_dot(query_low, w_q)
        + forward_dot(key_low, w_k)
        + forward_dot(value_low, w_v)
    )
    early = share_out[own:].reshape(-1)
    late = share_late[3 * own :].reshape(-1)
    shaped_out = (batch_rows, sequence_length, feature_width)
    return (
        layer_out.reshape(shaped_out),
        input_grad.reshape(shaped_out),
        share_late[:own].T,
        late[own * KW : own * KW + own],
        share_late[own : 2 * own].T,
        share_late[2 * own : 3 * own].T,
        late[own * KW + own : own * KW + 2 * own],
        late[: own * KW].reshape(own, KW).T,
        share_out[:own].T,
        early[:own],
        early[own : 2 * own],
        early[2 * own : 3 * own],
        share_up.T,
        early[6 * own : 6 * own + b_up.shape[0]],
        share_down.T,
        early[3 * own : 4 * own],
        early[4 * own : 5 * own],
        early[5 * own : 6 * own],
    )


def solution(mesh):
    return jax.shard_map(
        shards,
        mesh=mesh,
        in_specs=(
            P(("wide", "narrow"), None, None),
            P(("wide", "narrow"), None),
            P(("wide", "narrow"), None),
            P(None, ("wide", "narrow")),
            P(("wide", "narrow")),
            P(None, ("wide", "narrow")),
            P(None, ("wide", "narrow")),
            P(("wide", "narrow")),
            P(None, ("wide", "narrow")),
            P(None, ("wide", "narrow")),
            P(("wide", "narrow")),
            P(("wide", "narrow")),
            P(("wide", "narrow")),
            P(None, ("wide", "narrow")),
            P(("wide", "narrow")),
            P(None, ("wide", "narrow")),
            P(("wide", "narrow")),
            P(("wide", "narrow")),
            P(("wide", "narrow")),
            P(("wide", "narrow"), None, None),
        ),
        out_specs=(
            P(("wide", "narrow"), None, None),
            P(("wide", "narrow"), None, None),
            P(None, ("wide", "narrow")),
            P(("wide", "narrow")),
            P(None, ("wide", "narrow")),
            P(None, ("wide", "narrow")),
            P(("wide", "narrow")),
            P(None, ("wide", "narrow")),
            P(None, ("wide", "narrow")),
            P(("wide", "narrow")),
            P(("wide", "narrow")),
            P(("wide", "narrow")),
            P(None, ("wide", "narrow")),
            P(("wide", "narrow")),
            P(None, ("wide", "narrow")),
            P(("wide", "narrow")),
            P(("wide", "narrow")),
            P(("wide", "narrow")),
        ),
        check_vma=False,
    )
```

```python
import functools

import jax
import jax.numpy as jnp
from jax import lax
from jax.experimental import pallas as pl
from jax.experimental.pallas import tpu as pltpu
from jax.sharding import PartitionSpec as P

BF = jnp.bfloat16
F32 = jnp.float32
KW=33; HALF=16; DOCS=4; GAP=16
def spread(dst, get, bounds, length, step):
    total=length+GAP*(DOCS+1)
    ids=lax.broadcasted_iota(jnp.int32,(step,128),0)
    for p0 in range(0,total,step):
        size=min(step,total-p0)
        acc=None
        for d in range(DOCS):
            s0=p0-GAP*(d+1)
            lo=max(s0,0); hi=min(s0+size,length)
            if hi<=lo: continue
            row=ids[:hi-lo]+lo
            inside=(row>=bounds[d])&(row<bounds[d+1])
            part=jnp.where(inside,get(lo,hi-lo),0.0)
            pads=[]
            if lo>s0: pads.append(jnp.zeros((lo-s0,128),F32))
            pads.append(part)
            if s0+size>hi: pads.append(jnp.zeros((s0+size-hi,128),F32))
            part=jnp.concatenate(pads,0) if len(pads)>1 else part
            acc=part if acc is None else acc+part
        if acc is None: acc=jnp.zeros((size,128),F32)
        dst[HALF+p0:HALF+p0+size,:]=acc
def collect(src, bounds, lo, size):
    row=lax.broadcasted_iota(jnp.int32,(size,128),0)+lo
    acc=None
    for d in range(DOCS):
        part=src[lo+GAP*(d+1):lo+GAP*(d+1)+size,:]
        acc=part if acc is None else jnp.where(row>=bounds[d],part,acc)
    return acc
BLOCK=64
def taps(ref, base, weight, sign):
    acc=None
    for r in range(8):
        win=ref[pl.ds(base+r,BLOCK+32),:] if r==0 else ref[pl.ds(base+r,BLOCK+24),:]
        for a in range(5 if r==0 else 4):
            o=8*a+r
            t=weight(o if sign>0 else 2*HALF-o)*win[8*a:8*a+BLOCK]
            acc=t if acc is None else acc+t
    return acc
def conv_fwd_kernel(bounds_ref, v_ref, w_ref, out_ref, pad_ref, res_ref):
    b=pl.program_id(0)
    bounds=[bounds_ref[b,d] for d in range(DOCS+1)]
    length=v_ref.shape[1]; total=length+GAP*(DOCS+1)
    zeros=jnp.zeros((HALF,128),F32)
    pad_ref[0:HALF,:]=zeros; pad_ref[HALF+total:,:]=jnp.zeros((pad_ref.shape[0]-HALF-total,128),F32)
    spread(pad_ref, lambda lo,n: v_ref[0,lo:lo+n,:], bounds, length, BLOCK)
    def block(i,c):
        base=pl.multiple_of(i*BLOCK,BLOCK)
        res_ref[pl.ds(base,BLOCK),:]=taps(pad_ref, base, lambda s: w_ref[s:s+1,:], 1)
        return c
    lax.fori_loop(0,-(-total//BLOCK),block,0)
    for lo in range(0,length,BLOCK):
        out_ref[0,lo:lo+BLOCK,:]=collect(res_ref,bounds,lo,BLOCK)
def padded_rows(length):
    total=length+GAP*(DOCS+1)
    return -(-total//BLOCK)*BLOCK
def conv_fwd(bounds, v, w):
    B,L,D=v.shape
    rows=padded_rows(L)
    return pl.pallas_call(conv_fwd_kernel,grid_spec=pltpu.PrefetchScalarGridSpec(num_scalar_prefetch=1,grid=(B,D//128),
        in_specs=[pl.BlockSpec((1,L,128),lambda b,c,_:(b,0,c)),pl.BlockSpec((KW,128),lambda b,c,_:(0,c))],
        out_specs=pl.BlockSpec((1,L,128),lambda b,c,_:(b,0,c)),
        scratch_shapes=[pltpu.VMEM((rows+2*HALF+8,128),F32),pltpu.VMEM((rows,128),F32)]),
        out_shape=jax.ShapeDtypeStruct((B,L,D),F32),
        compiler_params=pltpu.CompilerParams(vmem_limit_bytes=32*2**20))(bounds,v,w)
def conv_bwd_kernel(bounds_ref, v_ref, g_ref, w_ref, dv_ref, dw_ref, vpad_ref, gpad_ref, res_ref, acc_ref):
    b=pl.program_id(1)
    bounds=[bounds_ref[b,d] for d in range(DOCS+1)]
    length=v_ref.shape[1]; total=length+GAP*(DOCS+1)
    for ref in (vpad_ref,gpad_ref):
        ref[0:HALF,:]=jnp.zeros((HALF,128),F32)
        ref[HALF+total:,:]=jnp.zeros((ref.shape[0]-HALF-total,128),F32)
    spread(vpad_ref, lambda lo,n: v_ref[0,lo:lo+n,:], bounds, length, BLOCK)
    spread(gpad_ref, lambda lo,n: g_ref[0,lo:lo+n,:], bounds, length, BLOCK)
    @pl.when(b==0)
    def _(): acc_ref[...]=jnp.zeros_like(acc_ref)
    def block(i,c):
        base=pl.multiple_of(i*BLOCK,BLOCK)
        here=vpad_ref[pl.ds(base+HALF,BLOCK),:]
        acc=None
        for r in range(8):
            n=5 if r==0 else 4
            win=gpad_ref[pl.ds(base+r,BLOCK+8*(n-1)),:]
            for a in range(n):
                s=2*HALF-(8*a+r)
                x=win[8*a:8*a+BLOCK]
                t=w_ref[s:s+1,:]*x
                acc=t if acc is None else acc+t
                p=(here*x).reshape(BLOCK//8,8,128)
                acc_ref[s]+=jnp.sum(p,axis=0)
        res_ref[pl.ds(base,BLOCK),:]=acc
        return c
    lax.fori_loop(0,-(-total//BLOCK),block,0)
    for lo in range(0,length,BLOCK):
        dv_ref[0,lo:lo+BLOCK,:]=collect(res_ref,bounds,lo,BLOCK)
    @pl.when(b==pl.num_programs(1)-1)
    def _():
        for s in range(KW):
            dw_ref[s:s+1,:]=jnp.sum(acc_ref[s],axis=0,keepdims=True)
def conv_bwd(bounds, v, g, w):
    B,L,D=v.shape
    rows=padded_rows(L)
    slab=pl.BlockSpec((1,L,128),lambda c,b,_:(b,0,c)); tapsp=pl.BlockSpec((KW,128),lambda c,b,_:(0,c))
    return pl.pallas_call(conv_bwd_kernel,grid_spec=pltpu.PrefetchScalarGridSpec(num_scalar_prefetch=1,grid=(D//128,B),
        in_specs=[slab,slab,tapsp],out_specs=[slab,tapsp],
        scratch_shapes=[pltpu.VMEM((rows+2*HALF+8,128),F32)]*2+[pltpu.VMEM((rows,128),F32),pltpu.VMEM((KW,8,128),F32)]),
        out_shape=[jax.ShapeDtypeStruct((B,L,D),F32),jax.ShapeDtypeStruct((KW,D),F32)],
        compiler_params=pltpu.CompilerParams(vmem_limit_bytes=32*2**20))(bounds,v,g,w)

HW=64; LM=64; NEWTON=6; GH=4; GW=GH*HW
STASH=4*NEWTON
def nt(a,b): return lax.dot_general(a,b,(((1,),(1,)),((),())),preferred_element_type=F32)
def nn(a,b): return lax.dot_general(a,b,(((1,),(0,)),((),())),preferred_element_type=F32)
def split(a):
    hi=a.astype(BF); return hi,(a-hi.astype(F32)).astype(BF)
def wide(a):
    hi,lo=split(a); return jnp.concatenate([hi,hi,lo],axis=1)
def tall(b):
    hi,lo=split(b); return jnp.concatenate([hi,lo,hi],axis=0)
def mm3(a,b): return nn(wide(a),tall(b))
def mm1(a,b): return nn(a.astype(BF),b.astype(BF))
def pair(a):
    hi,lo=split(a); return jnp.concatenate([hi,lo],axis=0)
def long3(a,b):
    full=nt(a,b); n=full.shape[0]//2
    return full[:n,:n]+(full[:n,n:]+full[n:,:n])
def eye(c):
    return jnp.where(lax.broadcasted_iota(jnp.int32,(LM,LM),0)==lax.broadcasted_iota(jnp.int32,(LM,LM),1),c,0.0)
def masks(tok_ref,ldc_ref,ldr_ref):
    tok=tok_ref[0]; ldc=ldc_ref[0]; ldr=ldr_ref[0]
    member=lax.broadcasted_iota(jnp.int32,(LM,tok.shape[1]),0)==tok
    doc=jnp.sum(jnp.where(member,ldc,0),axis=0,keepdims=True)
    return member, doc==ldc, ldc==ldr
def softmax(s,allowed,axis):
    held=jnp.where(allowed,s,-1e30)
    raised=jnp.exp(held-jnp.max(held,axis=axis,keepdims=True))
    raised=jnp.where(allowed,raised,0.0)
    return raised/jnp.sum(raised,axis=axis,keepdims=True)
def att_fwd_kernel(x_ref,wq_ref,wk_ref,wv_ref,bq_ref,bv_ref,tok_ref,ldc_ref,ldr_ref,conv_ref,
               q_ref,k_ref,v_ref,k1_ref,k3_ref,stash_ref,small_ref,ctx_ref):
    x=x_ref[0]
    member,allow1,allow2=masks(tok_ref,ldc_ref,ldr_ref)
    one_hot=jnp.where(member,1.0,0.0).astype(BF)
    count=nt(jnp.ones((8,x.shape[0]),BF),one_hot)[0:1]
    scale=HW**-0.25
    q=(nt(wq_ref[...],x)+bq_ref[...])*scale; q_ref[0]=q
    k=nt(wk_ref[...],x)*scale; k_ref[0]=k
    v=nt(wv_ref[...],x)+bv_ref[...]; v_ref[0]=v
    def land(a):
        hi,lo=split(a); return (nt(hi,one_hot)+nt(lo,one_hot))/count
    lqt,lkt=land(q),land(k)
    heads=range(GH)
    cut=lambda a,h: a[h*HW:(h+1)*HW]
    lq=[cut(lqt,h).T for h in heads]; lk=[cut(lkt,h).T for h in heads]
    k2=[softmax(mm3(lq[h],cut(lkt,h)),allow2,1) for h in heads]
    z=[k2[h].T*(1.0/jnp.sum(k2[h]*k2[h])) for h in heads]
    k2w=[wide(a) for a in k2]
    for n in range(NEWTON):
        p=[nn(k2w[h],tall(z[h])) for h in heads]
        pw=[wide(a) for a in p]
        b=[eye(15.0)-nn(pw[h],tall(eye(7.0)-p[h])) for h in heads]
        c=[eye(13.0)-nn(pw[h],tall(b[h])) for h in heads]
        for h in heads:
            stash_ref[0,h,4*n]=p[h].astype(BF); stash_ref[0,h,4*n+1]=b[h].astype(BF)
            stash_ref[0,h,4*n+2]=c[h].astype(BF); stash_ref[0,h,4*n+3]=z[h].T.astype(BF)
        z=[0.25*mm3(z[h],c[h]) for h in heads]
    outs=[]
    for h in heads:
        k1=softmax(mm3(lk[h],cut(q,h)),allow1,0); k1_ref[0,h*LM:(h+1)*LM]=k1
        k3=softmax(mm3(lq[h],cut(k,h)),allow1,1); k3_ref[0,h*LM:(h+1)*LM]=k3
        r=long3(pair(k3),pair(cut(v,h)))
        u=mm3(z[h],r)
        small_ref[0,h,0]=lq[h]; small_ref[0,h,1]=lk[h]; small_ref[0,h,2]=k2[h]; small_ref[0,h,3]=z[h]
        small_ref[0,h,4]=r; small_ref[0,h,5]=u
        outs.append(mm3(u.T,k1))
    ctx_ref[0]=(jnp.concatenate(outs,axis=0).T+conv_ref[0]).astype(BF)
def att_fwd(x,wq,wk,wv,bq,bv,tok,ld,conv):
    B,T,D=x.shape; G=D//GW; H=D//HW
    seq=lambda s: pl.BlockSpec((1,)+s,lambda g,b:(b,)+(0,)*len(s))
    wsp=pl.BlockSpec((GW,D),lambda g,b:(g,0)); bsp=pl.BlockSpec((GW,1),lambda g,b:(g,0))
    rows=pl.BlockSpec((1,GW,T),lambda g,b:(b,g,0)); cols=pl.BlockSpec((1,T,GW),lambda g,b:(b,0,g))
    sq=lambda n: pl.BlockSpec((1,GH,n,LM,LM),lambda g,b:(b,g,0,0,0))
    sd=jax.ShapeDtypeStruct; big=sd((B,D,T),F32)
    return pl.pallas_call(att_fwd_kernel,grid=(G,B),
        in_specs=[seq((T,D)),wsp,wsp,wsp,bsp,bsp,seq((1,T)),seq((LM,1)),seq((1,LM)),cols],
        out_specs=[rows]*5+[sq(STASH),sq(6),cols],
        out_shape=[big]*5+[sd((B,H,STASH,LM,LM),BF),sd((B,H,6,LM,LM),F32),sd((B,T,D),BF)],
        compiler_params=pltpu.CompilerParams(vmem_limit_bytes=60*2**20))(
            x,wq,wk,wv,bq,bv,tok[:,None,:],ld[:,:,None],ld[:,None,:],conv)
def att_bwd_kernel(x_ref,al_ref,wo_ref,q_ref,k_ref,v_ref,k1_ref,k3_ref,stash_ref,small_ref,tok_ref,ldc_ref,ldr_ref,conv_ref,
               dq_ref,dk_ref,dv_ref,gq_ref,gk_ref,gv_ref,sq_ref,sv_ref):
    x=x_ref[0]
    member,_,_=masks(tok_ref,ldc_ref,ldr_ref)
    one_hot=jnp.where(member,1.0,0.0).astype(BF)
    count=nt(jnp.ones((8,x.shape[0]),BF),one_hot)[0:1]
    per=1.0/count
    scale=HW**-0.25
    g=nt(wo_ref[...],al_ref[0])
    heads=range(GH)
    rows=lambda ref,h: ref[0,h*HW:(h+1)*HW]
    lq,lk,k2,z,r,u=[[small_ref[0,h,i] for h in heads] for i in range(6)]
    du=[];ds1=[];dlk=[]
    for h in heads:
        gh=g[h*HW:(h+1)*HW]; k1=rows(k1_ref,h)
        gp=pair(gh)
        dk1=nn(wide(u[h]),jnp.concatenate([gp,gp[:HW]],axis=0))
        du.append(long3(pair(k1),gp))
        d=k1*(dk1-jnp.sum(k1*dk1,axis=0,keepdims=True)); ds1.append(d)
        dlk.append(long3(pair(d),pair(rows(q_ref,h))))
    dr=[mm3(z[h].T,du[h]) for h in heads]
    dz=[mm3(du[h],r[h].T) for h in heads]
    dlq=[];ds3=[];dvs=[]
    for h in heads:
        k3=rows(k3_ref,h)
        dk3=mm3(dr[h],rows(v_ref,h))
        dvs.append(mm3(dr[h].T,k3))
        d=k3*(dk3-jnp.sum(k3*dk3,axis=1,keepdims=True)); ds3.append(d)
        dlq.append(long3(pair(d),pair(rows(k_ref,h))))
    dk2=[None]*GH
    k2t=[a.T for a in k2]; k2tb=[a.astype(BF) for a in k2t]
    for n in reversed(range(NEWTON)):
        P,Bm,C,ZT=[[stash_ref[0,h,4*n+i] for h in heads] for i in range(4)]
        A=[(eye(7.0)-P[h].astype(F32)).astype(BF) for h in heads]
        gz=[(0.25*dz[h]).astype(BF) for h in heads]
        dc=[nn(ZT[h],gz[h]).astype(BF) for h in heads]
        db=[nn(P[h],dc[h]).astype(BF) for h in heads]
        da=[nn(P[h],db[h]) for h in heads]
        dp=[(nn(db[h],A[h])-nn(dc[h],Bm[h])-da[h]).astype(BF) for h in heads]
        for h in heads:
            t=nn(dp[h],ZT[h]); dk2[h]=t if dk2[h] is None else dk2[h]+t
        dz=[nn(gz[h],C[h])+nn(k2tb[h],dp[h]) for h in heads]
    dqs=[];dks=[]
    for h in heads:
        inv=1.0/jnp.sum(k2[h]*k2[h])
        d=dk2[h]+inv*dz[h].T-k2[h]*(2.0*inv*inv*jnp.sum(dz[h]*k2t[h]))
        d=k2[h]*(d-jnp.sum(k2[h]*d,axis=1,keepdims=True))
        dlqh=dlq[h]+mm3(d,lk[h]); dlkh=dlk[h]+mm3(d.T,lq[h])
        def back(land,dscore,dland):
            ah,al=split(land.T); dh,dl=split(dscore); mh,ml=split(dland.T*per)
            return nn(jnp.concatenate([ah,ah,al,mh,ml],axis=1),jnp.concatenate([dh,dl,dh,one_hot,one_hot],axis=0))
        dqs.append(back(lk[h],ds1[h],dlqh)); dks.append(back(lq[h],ds3[h],dlkh))
    cat=lambda a: jnp.concatenate(a,axis=0)
    dq=(cat(dqs)*scale).astype(BF); dk=(cat(dks)*scale).astype(BF)
    dv=(cat(dvs)+conv_ref[0].T).astype(BF)
    dq_ref[0]=dq; dk_ref[0]=dk; dv_ref[0]=dv
    @pl.when(pl.program_id(1)==0)
    def _():
        for ref in (gq_ref,gk_ref,gv_ref,sq_ref,sv_ref): ref[...]=jnp.zeros_like(ref)
    gq_ref[...]+=nn(dq,x); gk_ref[...]+=nn(dk,x); gv_ref[...]+=nn(dv,x)
    sq_ref[...]+=jnp.sum(dq.astype(F32),axis=1,keepdims=True)
    sv_ref[...]+=jnp.sum(dv.astype(F32),axis=1,keepdims=True)
def att_bwd(x,al,wo,q,k,v,k1,k3,stash,small,tok,ld,conv):
    B,T,D=x.shape; G=D//GW; H=D//HW
    seq=lambda s: pl.BlockSpec((1,)+s,lambda g,b:(b,)+(0,)*len(s))
    wsp=pl.BlockSpec((GW,D),lambda g,b:(g,0)); bsp=pl.BlockSpec((GW,1),lambda g,b:(g,0))
    rows=pl.BlockSpec((1,GW,T),lambda g,b:(b,g,0)); cols=pl.BlockSpec((1,T,GW),lambda g,b:(b,0,g))
    sq=lambda n: pl.BlockSpec((1,GH,n,LM,LM),lambda g,b:(b,g,0,0,0))
    sd=jax.ShapeDtypeStruct; big=sd((B,D,T),BF)
    return pl.pallas_call(att_bwd_kernel,grid=(G,B),
        in_specs=[seq((T,D)),seq((T,D)),wsp]+[rows]*5+[sq(STASH),sq(6),seq((1,T)),seq((LM,1)),seq((1,LM)),cols],
        out_specs=[rows]*3+[wsp]*3+[bsp]*2,
        out_shape=[big]*3+[sd((D,D),F32)]*3+[sd((D,1),F32)]*2,
        compiler_params=pltpu.CompilerParams(vmem_limit_bytes=60*2**20))(
            x,al,wo,q,k,v,k1,k3,stash,small,tok[:,None,:],ld[:,:,None],ld[:,None,:],conv)

def gelu_parts(x):
    size=jnp.abs(x)
    density=jnp.exp(-0.5*x*x)*0.3989422804014327
    t=1.0/(1.0+0.2316419*size)
    tail=density*(t*(0.319381530+t*(-0.356563782+t*(1.781477937+t*(-1.821255978+t*1.330274429)))))
    dist=jnp.where(x<0.0,tail,1.0-tail)
    return dist, x*density
def norm(v):
    mean=jnp.mean(v,axis=-1,keepdims=True); c=v-mean
    r=lax.rsqrt(jnp.mean(c*c,axis=-1,keepdims=True)+1e-5)
    return c*r, r
def norm_back(up,n,r,g):
    e=up*g
    return r*(e-jnp.mean(e,axis=-1,keepdims=True)-n*jnp.mean(e*n,axis=-1,keepdims=True))
def ffn_kernel(chunks, ctx_ref,x_ref,cot_ref,wo_ref,wu_ref,wd_ref,vec_ref,bu_ref,
               out_ref,normed_ref,hidden_ref,down_ref,up_ref,one_ref,att_ref,sums_ref,sumu_ref,slope_ref):
    width=wu_ref.shape[0]//chunks
    @pl.when(pl.program_id(0)==0)
    def _():
        sums_ref[...]=jnp.zeros_like(sums_ref); sumu_ref[...]=jnp.zeros_like(sumu_ref)
    v=lambda i: vec_ref[i:i+1,:]
    b_o,g1,s1,b_d,g2,s2=[v(i) for i in range(6)]
    n1,r1=norm(x_ref[...].astype(F32)+(nt(ctx_ref[...],wo_ref[...])+b_o))
    normed=n1*g1+s1
    low=normed.astype(BF); normed_ref[...]=low
    down=None
    for k in range(chunks):
        part=slice(k*width,(k+1)*width)
        pre=nt(low,wu_ref[part,:])+bu_ref[:,part]
        dist,slope=gelu_parts(pre)
        slope_ref[:,part]=dist+slope
        hid=(pre*dist).astype(BF); hidden_ref[:,part]=hid
        add=nt(hid,wd_ref[:,part]); down=add if down is None else down+add
    n2,r2=norm(normed+(down+b_d))
    out_ref[...]=(n2*g2+s2).astype(BF)
    cot=cot_ref[...].astype(F32)
    g_two=norm_back(cot,n2,r2,g2)
    low2=g_two.astype(BF); down_ref[...]=low2
    back=g_two
    for k in range(chunks):
        part=slice(k*width,(k+1)*width)
        hg=nn(low2,wd_ref[:,part])
        upl=(hg*slope_ref[:,part]).astype(BF); up_ref[:,part]=upl
        sumu_ref[:,part]+=jnp.sum(upl.astype(F32),axis=0,keepdims=True)
        back=back+nn(upl,wu_ref[part,:])
    g_one=norm_back(back,n1,r1,g1)
    one_ref[...]=g_one
    al=g_one.astype(BF); att_ref[...]=al
    s=lambda a: jnp.sum(a,axis=0,keepdims=True)
    sums_ref[...]+=jnp.concatenate([s(al.astype(F32)),s(back*n1),s(back),s(low2.astype(F32)),s(cot*n2),s(cot),jnp.zeros((2,n1.shape[1]),F32)],axis=0)
def ffn(ctx,x,cot,wo,wu,wd,vec,bu,block=256,chunks=4):
    T,D=x.shape; F=wu.shape[0]
    row=lambda w: pl.BlockSpec((block,w),lambda i:(i,0))
    full=lambda a: pl.BlockSpec(a.shape,lambda i:(0,0),pipeline_mode=pl.Buffered(1))
    keep=lambda r,w: pl.BlockSpec((r,w),lambda i:(0,0))
    sd=jax.ShapeDtypeStruct
    return pl.pallas_call(functools.partial(ffn_kernel,chunks),grid=(T//block,),
        in_specs=[row(D),row(D),row(D),full(wo),full(wu),full(wd),full(vec),full(bu)],
        out_specs=[row(D),row(D),row(F),row(D),row(F),row(D),row(D),keep(8,D),keep(1,F)],
        out_shape=[sd((T,D),BF),sd((T,D),BF),sd((T,F),BF),sd((T,D),BF),sd((T,F),BF),sd((T,D),F32),sd((T,D),BF),sd((8,D),F32),sd((1,F),F32)],
        scratch_shapes=[pltpu.VMEM((block,F),F32)],
        compiler_params=pltpu.CompilerParams(vmem_limit_bytes=60*2**20,dimension_semantics=("arbitrary",)),
    )(ctx,x,cot,wo,wu,wd,vec,bu)


def digits():
    found = []
    for axis in ("wide", "narrow"):
        stride = lax.axis_size(axis) // 2
        while stride >= 1:
            found.append((axis, stride))
            stride //= 2
    return found


def link_order(number):
    count = len(digits())
    if lax.axis_size("wide") == 8 and lax.axis_size("narrow") == 4:
        return [(4, 2, 3, 1, 0), (4, 3, 1, 2, 0), (4, 1, 2, 3, 0)][number]
    return tuple(range(count - 1, -1, -1))


def exchange(values, axis, stride):
    return lax.ppermute(values, axis, [(i, i ^ stride) for i in range(lax.axis_size(axis))])


def digit_of(axis, stride):
    return (lax.axis_index(axis) // stride) % 2


def gather_rows(shard, number):
    places = digits()
    held = shard.reshape((1,) * len(places) + shard.shape)
    for dim in link_order(number)[::-1]:
        mine = digit_of(*places[dim])
        got = exchange(held, *places[dim])
        first = jnp.where(mine == 0, held, got)
        second = jnp.where(mine == 0, got, held)
        held = jnp.concatenate([first, second], dim)
    return held.reshape((-1,) + shard.shape)


def scatter_start(whole):
    return whole.reshape((2,) * len(digits()) + whole.shape[1:])


def scatter_step(held, number, step):
    places = digits()
    dim = link_order(number)[step]
    mine = digit_of(*places[dim])
    keep = lax.dynamic_slice_in_dim(held, mine, 1, dim).astype(F32)
    send = lax.dynamic_slice_in_dim(held, 1 - mine, 1, dim).astype(BF)
    return keep + exchange(send, *places[dim]).astype(F32)


def scatter_rest(held, number, step):
    for later in range(step, len(digits())):
        held = scatter_step(held, number, later)
    return held.reshape(held.shape[-2:])


def pad_rows(flat, rows):
    count, length = flat.shape
    return jnp.pad(flat, ((0, 0), (0, rows * 768 - length))).reshape(count, rows, 768)


def across_rows(left_side, right_side):
    return lax.dot_general(left_side, right_side, (((0,), (0,)), ((), ())), preferred_element_type=F32)


def shards(
    inputs,
    tok_landmark,
    landmark_doc,
    w_query,
    b_query,
    w_key,
    w_value,
    b_value,
    conv_weight,
    w_out,
    b_out,
    gain_one,
    shift_one,
    w_up,
    b_up,
    w_down,
    b_down,
    gain_two,
    shift_two,
    cotangent,
):
    batch_rows, sequence_length, feature_width = inputs.shape
    group_count = lax.axis_size("wide") * lax.axis_size("narrow")
    own = feature_width // group_count
    tokens = batch_rows * sequence_length
    vectors = (b_query, b_value, b_out, gain_one, shift_one, b_down, gain_two, shift_two)
    flat = jnp.concatenate([conv_weight.T.reshape(-1)] + list(vectors) + [b_up])
    small = pad_rows(flat[None], -(-flat.shape[0] // 768))[0]
    gathered_v = gather_rows(jnp.concatenate([w_value.T, small], axis=0), 0)
    w_q = gather_rows(w_query.T, 1).reshape(feature_width, feature_width)
    w_k = gather_rows(w_key.T, 2).reshape(feature_width, feature_width)
    w_v = gathered_v[:, :own].reshape(feature_width, feature_width)
    small = gathered_v[:, own:].reshape(group_count, -1).astype(F32)
    conv_taps = small[:, : own * KW].reshape(feature_width, KW).T
    small = small[:, own * KW :]
    b_q, b_v, b_o, g_one, s_one, b_d, g_two, s_two = [
        small[:, i * own : (i + 1) * own].reshape(feature_width) for i in range(8)
    ]
    b_u = small[:, 8 * own : 8 * own + b_up.shape[0]].reshape(1, -1)
    later = lax.optimization_barrier((w_out.T, w_up.T, w_down.T, gathered_v, w_q, w_k))
    w_o, w_u, w_d = [
        lax.all_gather(shard, ("wide", "narrow"), axis=0, tiled=True) for shard in later[:3]
    ]
    w_q, w_k = later[4:]
    doc = jnp.sum(
        jnp.where(tok_landmark[:, :, None] == jnp.arange(LM)[None, None], landmark_doc[:, None], 0), axis=2
    )
    bounds = jnp.sum(doc[:, None, :] < jnp.arange(DOCS + 1)[None, :, None], axis=2).astype(jnp.int32)
    rows_low = inputs.reshape(tokens, feature_width)
    value_rows = (nt(rows_low, w_v) + b_v).reshape(inputs.shape)
    conv_part = conv_fwd(bounds, value_rows, conv_taps)
    q, k, v, k1, k3, stash, landmarks, context = att_fwd(
        inputs, w_q, w_k, w_v, b_q[:, None], b_v[:, None], tok_landmark, landmark_doc, conv_part
    )
    context = context.reshape(tokens, feature_width)
    vec = jnp.concatenate([jnp.stack([b_o, g_one, s_one, b_d, g_two, s_two]), jnp.zeros((2, feature_width), F32)])
    layer_out, normed, hidden, down_low, up_low, grad_one, att_low, sums, sums_up = ffn(
        context, rows_low, cotangent.reshape(tokens, feature_width), w_o, w_u, w_d, vec, b_u
    )

    def by_device(values):
        return values.reshape((group_count, -1) + values.shape[1:])

    context_grad = nn(att_low, w_o).reshape(inputs.shape)
    early = jnp.concatenate([by_device(sums[i]) for i in range(6)] + [by_device(sums_up[0])], axis=1)
    grad_out = jnp.concatenate(
        [by_device(across_rows(att_low, context)), pad_rows(early, -(-early.shape[1] // 768))], axis=1
    )
    share_up = scatter_start(by_device(across_rows(up_low, normed)))
    share_down = scatter_start(by_device(across_rows(down_low, hidden)))
    share_out = scatter_start(grad_out)
    shares = [share_up, share_down, share_out]
    shares = [scatter_step(share, i, 0) for i, share in enumerate(shares)]
    context_grad, *shares = lax.optimization_barrier((context_grad, *shares))
    shares = [scatter_step(share, i, 1) for i, share in enumerate(shares)]
    conv_grad, taps_grad = conv_bwd(bounds, value_rows, context_grad, conv_taps)
    conv_grad, att_low, *shares = lax.optimization_barrier((conv_grad, att_low, *shares))
    shares = [scatter_step(share, i, 2) for i, share in enumerate(shares)]
    w_plain = w_o.T
    dq, dk, dv, grad_q, grad_k, grad_v, sum_q, sum_v = att_bwd(
        inputs, att_low.reshape(inputs.shape), w_plain, q, k, v, k1, k3, stash, landmarks, tok_landmark,
        landmark_doc, conv_grad,
    )
    dq, dk, dv, grad_q, grad_k, grad_v, *shares = lax.optimization_barrier(
        (dq, dk, dv, grad_q, grad_k, grad_v, *shares)
    )
    share_up, share_down, share_out = [scatter_rest(share, i, 3) for i, share in enumerate(shares)]
    late = jnp.concatenate(
        [by_device(taps_grad.T).reshape(group_count, -1), by_device(sum_q[:, 0]), by_device(sum_v[:, 0])], axis=1
    )
    grad_v = jnp.concatenate([by_device(grad_v), pad_rows(late, -(-late.shape[1] // 768))], axis=1)
    share_v = scatter_rest(scatter_start(grad_v), 0, 0)
    share_q = scatter_rest(scatter_start(by_device(grad_q)), 1, 0)
    share_k = scatter_rest(scatter_start(by_device(grad_k)), 2, 0)

    def through(grad, weight):
        return jnp.einsum("bot,oi->bti", grad, weight, preferred_element_type=F32)

    input_grad = grad_one.reshape(inputs.shape) + through(dq, w_q) + through(dk, w_k) + through(dv, w_v)
    early = share_out[own:].reshape(-1)
    late = share_v[own:].reshape(-1)
    return (
        layer_out.reshape(inputs.shape),
        input_grad,
        share_q.T,
        late[own * KW : own * KW + own],
        share_k.T,
        share_v[:own].T,
        late[own * KW + own : own * KW + 2 * own],
        late[: own * KW].reshape(own, KW).T,
        share_out[:own].T,
        early[:own],
        early[own : 2 * own],
        early[2 * own : 3 * own],
        share_up.T,
        early[6 * own : 6 * own + b_up.shape[0]],
        share_down.T,
        early[3 * own : 4 * own],
        early[4 * own : 5 * own],
        early[5 * own : 6 * own],
    )


def solution(mesh):
    return jax.shard_map(
        shards,
        mesh=mesh,
        in_specs=(
            P(("wide", "narrow"), None, None),
            P(("wide", "narrow"), None),
            P(("wide", "narrow"), None),
            P(None, ("wide", "narrow")),
            P(("wide", "narrow")),
            P(None, ("wide", "narrow")),
            P(None, ("wide", "narrow")),
            P(("wide", "narrow")),
            P(None, ("wide", "narrow")),
            P(None, ("wide", "narrow")),
            P(("wide", "narrow")),
            P(("wide", "narrow")),
            P(("wide", "narrow")),
            P(None, ("wide", "narrow")),
            P(("wide", "narrow")),
            P(None, ("wide", "narrow")),
            P(("wide", "narrow")),
            P(("wide", "narrow")),
            P(("wide", "narrow")),
            P(("wide", "narrow"), None, None),
        ),
        out_specs=(
            P(("wide", "narrow"), None, None),
            P(("wide", "narrow"), None, None),
            P(None, ("wide", "narrow")),
            P(("wide", "narrow")),
            P(None, ("wide", "narrow")),
            P(None, ("wide", "narrow")),
            P(("wide", "narrow")),
            P(None, ("wide", "narrow")),
            P(None, ("wide", "narrow")),
            P(("wide", "narrow")),
            P(("wide", "narrow")),
            P(("wide", "narrow")),
            P(None, ("wide", "narrow")),
            P(("wide", "narrow")),
            P(None, ("wide", "narrow")),
            P(("wide", "narrow")),
            P(("wide", "narrow")),
            P(("wide", "narrow")),
        ),
        check_vma=False,
    )
```

```python
import functools

import jax
import jax.numpy as jnp
from jax import lax
from jax.experimental import pallas as pl
from jax.experimental.pallas import tpu as pltpu
from jax.sharding import PartitionSpec as P

BF = jnp.bfloat16
F32 = jnp.float32
HW=64; LM=64; NEWTON=6; GH=6; GW=GH*HW
CHUNK=256
def nt(a,b): return lax.dot_general(a,b,(((1,),(1,)),((),())),preferred_element_type=F32)
def nn(a,b): return lax.dot_general(a,b,(((1,),(0,)),((),())),preferred_element_type=F32)
def split(a):
    hi=a.astype(BF); return hi,(a-hi.astype(F32)).astype(BF)
def wide(a):
    hi,lo=split(a); return jnp.concatenate([hi,hi,lo],axis=1)
def tall(b):
    hi,lo=split(b); return jnp.concatenate([hi,lo,hi],axis=0)
def mm3(a,b): return nn(wide(a),tall(b))
def eye(c):
    return jnp.where(lax.broadcasted_iota(jnp.int32,(LM,LM),0)==lax.broadcasted_iota(jnp.int32,(LM,LM),1),c,0.0)
def weave(first, second):
    done=0
    for i,step in enumerate(first):
        step()
        upto=(i+1)*len(second)//len(first)
        for other in second[done:upto]: other()
        done=upto
def att_fwd_kernel(x_ref,mean_ref,wq_ref,wk_ref,wv_ref,vec_ref,tok_ref,ldc_ref,ldr_ref,conv_ref,
               q_ref,k_ref,v_ref,k1_ref,k3_ref,inv_ref,stash_ref,small_ref,ctx_ref,
               qlo_ref,klo_ref,score_ref,bias_ref):
    T=x_ref.shape[1]
    heads=range(GH); chunks=[slice(c,c+CHUNK) for c in range(0,T,CHUNK)]
    rows=[slice(h*HW,(h+1)*HW) for h in heads]
    scale=HW**-0.25
    bq=vec_ref[0:1,:].T; bv=vec_ref[1:2,:].T
    ldc=ldc_ref[0]
    for cs in chunks:
        member=lax.broadcasted_iota(jnp.int32,(LM,CHUNK),0)==tok_ref[0,:,cs]
        doc=jnp.sum(jnp.where(member,ldc,0),axis=0,keepdims=True)
        bias_ref[:,cs]=jnp.where(doc==ldc,0.0,-1e30)
    mean=jnp.concatenate(split(mean_ref[0]),axis=0)
    def land(w_ref):
        both=nt(w_ref[...],mean)
        return both[:,:LM]+both[:,LM:]
    lqt=(land(wq_ref)+bq)*scale; lkt=land(wk_ref)*scale
    lq=[lqt[r].T for r in rows]; lk=[lkt[r].T for r in rows]
    lqw=[wide(a) for a in lq]; lkw=[wide(a) for a in lk]
    allow2=ldc==ldr_ref[0]
    k2=[];z=[]
    for h in heads:
        s=jnp.where(allow2,nn(lqw[h],tall(lkt[rows[h]])),-1e30)
        e=jnp.exp(s-jnp.max(s,axis=1,keepdims=True))
        k2.append(e/jnp.sum(e,axis=1,keepdims=True))
        z.append(k2[h].T*(1.0/jnp.sum(k2[h]*k2[h])))
    state={"z":z}
    k2w=[wide(a) for a in k2]
    def newton(n):
        def one():
            state["p"]=[nn(k2w[h],tall(state["z"][h])) for h in heads]
            state["pw"]=[wide(a) for a in state["p"]]
        def two(): state["b"]=[eye(15.0)-nn(state["pw"][h],tall(eye(7.0)-state["p"][h])) for h in heads]
        def three(): state["c"]=[eye(13.0)-nn(state["pw"][h],tall(state["b"][h])) for h in heads]
        def four():
            for h in heads:
                stash_ref[0,h,2*n]=jnp.concatenate([state["p"][h],state["b"][h]],axis=1)
                stash_ref[0,h,2*n+1]=jnp.concatenate([state["c"][h],state["z"][h].T],axis=1)
            state["z"]=[0.25*mm3(state["z"][h],state["c"][h]) for h in heads]
        return [one,two,three,four]
    chain=[step for n in range(NEWTON) for step in newton(n)]
    side=[]
    def project(cs):
        x=x_ref[0,cs,:]
        def q():
            a=(nt(wq_ref[...],x)+bq)*scale
            hi,lo=split(a); q_ref[0,:,cs]=hi; qlo_ref[:,cs]=lo
        def k():
            a=nt(wk_ref[...],x)*scale
            hi,lo=split(a); k_ref[0,:,cs]=hi; klo_ref[:,cs]=lo
        def v(): v_ref[0,:,cs]=(nt(wv_ref[...],x)+bv).astype(BF)
        return [q,k,v]
    tops=[None]*GH; sums=[None]*GH; r=[None]*GH
    def lanes(a): return [a[:,i:i+128] for i in range(0,CHUNK,128)]
    def first(h,cs):
        def go():
            hi=q_ref[0,rows[h],cs]
            s=nn(lkw[h],jnp.concatenate([hi,qlo_ref[rows[h],cs],hi],axis=0))+bias_ref[:,cs]
            e=jnp.exp(s-jnp.max(s,axis=0,keepdims=True))
            e=e.astype(BF); k1_ref[0,rows[h],cs]=e
            inv_ref[0,0,h:h+1,cs]=1.0/jnp.sum(e.astype(F32),axis=0,keepdims=True)
        return go
    def third(h,cs):
        def go():
            hi=k_ref[0,rows[h],cs]
            s=nn(lqw[h],jnp.concatenate([hi,klo_ref[rows[h],cs],hi],axis=0))+bias_ref[:,cs]
            score_ref[rows[h],cs]=s
            for a in lanes(s): tops[h]=a if tops[h] is None else jnp.maximum(tops[h],a)
        return go
    def raised(h,cs):
        def go():
            if cs.start==0: tops[h]=jnp.max(tops[h],axis=1,keepdims=True)
            e=jnp.exp(score_ref[rows[h],cs]-tops[h])
            e=e.astype(BF); k3_ref[0,rows[h],cs]=e
            for a in lanes(e.astype(F32)): sums[h]=a if sums[h] is None else sums[h]+a
        return go
    def gathered(h):
        def go():
            sums[h]=1.0/jnp.sum(sums[h],axis=1,keepdims=True)
            r[h]=nt(k3_ref[0,rows[h]],v_ref[0,rows[h]])*sums[h]
        return go
    for cs in chunks: side+=project(cs)
    for h in heads:
        side+=[third(h,cs) for cs in chunks]
        side+=[raised(h,cs) for cs in chunks]+[gathered(h)]
        side+=[first(h,cs) for cs in chunks]
    weave(chain,side)
    uts=[]
    for h in heads:
        u=mm3(state["z"][h],r[h])
        small_ref[0,h,0]=jnp.concatenate([lq[h],lk[h]],axis=1)
        small_ref[0,h,1]=jnp.concatenate([k2[h],state["z"][h].T],axis=1)
        small_ref[0,h,2]=jnp.concatenate([r[h],u],axis=1)
        small_ref[0,h,3]=jnp.broadcast_to(sums[h],(LM,128))
        uts.append(u.T.astype(BF))
    for cs in chunks:
        mixed=jnp.concatenate([nn(uts[h],k1_ref[0,rows[h],cs])*inv_ref[0,0,h:h+1,cs] for h in heads],axis=0)
        ctx_ref[0,cs,:]=(mixed.T+conv_ref[0,cs,:]).astype(BF)
def att_specs(D,T):
    seq=lambda s: pl.BlockSpec((1,)+s,lambda g,b:(b,)+(0,)*len(s))
    wsp=pl.BlockSpec((GW,D),lambda g,b:(g,0)); bsp=pl.BlockSpec((GW,1),lambda g,b:(g,0))
    rows=pl.BlockSpec((1,GW,T),lambda g,b:(b,g,0)); cols=pl.BlockSpec((1,T,GW),lambda g,b:(b,0,g))
    sq=lambda n: pl.BlockSpec((1,GH,n,LM,2*LM),lambda g,b:(b,g,0,0,0))
    turned=pl.BlockSpec((1,1,8,T),lambda g,b:(b,g,0,0))
    return seq,wsp,bsp,rows,cols,sq,turned
def att_fwd(x,mean,wq,wk,wv,vec,tok,ld,conv):
    B,T,D=x.shape; G=D//GW; H=D//HW
    seq,wsp,bsp,rows,cols,sq,turned=att_specs(D,T)
    sd=jax.ShapeDtypeStruct; big=sd((B,D,T),BF)
    return pl.pallas_call(att_fwd_kernel,grid=(G,B),
        in_specs=[seq((T,D)),seq((LM,D)),wsp,wsp,wsp,pl.BlockSpec((8,GW),lambda g,b:(0,g)),seq((1,T)),seq((LM,1)),seq((1,LM)),cols],
        out_specs=[rows]*5+[turned,sq(2*NEWTON),sq(4),cols],
        out_shape=[big]*5+[sd((B,G,8,T),F32),sd((B,H,2*NEWTON,LM,2*LM),F32),sd((B,H,4,LM,2*LM),F32),sd((B,T,D),BF)],
        scratch_shapes=[pltpu.VMEM((GW,T),BF)]*2+[pltpu.VMEM((GW,T),F32),pltpu.VMEM((LM,T),F32)],
        compiler_params=pltpu.CompilerParams(vmem_limit_bytes=60*2**20))(
            x,mean,wq,wk,wv,vec,tok[:,None,:],ld[:,:,None],ld[:,None,:],conv)
def att_bwd_kernel(x_ref,al_ref,wo_ref,q_ref,k_ref,v_ref,k1_ref,k3_ref,inv_ref,stash_ref,small_ref,tok_ref,conv_ref,
               dq_ref,dk_ref,dv_ref,gq_ref,gk_ref,gv_ref,sq_ref,sv_ref,
               g_ref,ds1_ref,ds3_ref,hot_ref):
    T=x_ref.shape[1]
    heads=range(GH); chunks=[slice(c,c+CHUNK) for c in range(0,T,CHUNK)]
    rows=[slice(h*HW,(h+1)*HW) for h in heads]
    scale=HW**-0.25
    for cs in chunks:
        member=lax.broadcasted_iota(jnp.int32,(LM,CHUNK),0)==tok_ref[0,:,cs]
        hot_ref[:,cs]=jnp.where(member,1.0,0.0).astype(BF)
    per=1.0/nt(jnp.ones((8,T),BF),hot_ref[...])[0:1]
    left=lambda i: [small_ref[0,h,i,:,:LM] for h in heads]
    right=lambda i: [small_ref[0,h,i,:,LM:] for h in heads]
    lq,lk,k2,zt,r,u=left(0),right(0),left(1),right(1),left(2),right(2)
    inv=[small_ref[0,h,3,:,:LM] for h in heads]
    ub=[a.astype(BF) for a in u]
    def upstream(cs):
        def go():
            a=nt(wo_ref[...],al_ref[0,cs,:])
            for h in heads: g_ref[rows[h],cs]=(a[rows[h]]*inv_ref[0,0,h:h+1,cs]).astype(BF)
        return go
    def first(h,cs):
        def go():
            k1=k1_ref[0,rows[h],cs].astype(F32)
            t=k1*nn(ub[h],g_ref[rows[h],cs])
            ds1_ref[rows[h],cs]=(t-k1*(jnp.sum(t,axis=0,keepdims=True)*inv_ref[0,0,h:h+1,cs])).astype(BF)
        return go
    for cs in chunks: upstream(cs)()
    du=[nt(k1_ref[0,rows[h]],g_ref[rows[h],:]) for h in heads]
    dr=[mm3(zt[h],du[h]) for h in heads]
    state={"dz":[mm3(du[h],r[h].T) for h in heads],"dk2":[None]*GH}
    drs=[(dr[h]*inv[h]) for h in heads]
    drb=[a.astype(BF) for a in drs]; drt=[a.T.astype(BF) for a in drs]
    delta=[jnp.sum(drb[h].astype(F32)*r[h],axis=1,keepdims=True) for h in heads]
    dlq=[None]*GH; dlk=[None]*GH
    def third(h,cs):
        def go():
            d=k3_ref[0,rows[h],cs].astype(F32)*(nn(drb[h],v_ref[0,rows[h],cs])-delta[h])
            ds3_ref[rows[h],cs]=d.astype(BF)
        return go
    def values(cs):
        def go():
            a=jnp.concatenate([nn(drt[h],k3_ref[0,rows[h],cs]) for h in heads],axis=0)
            dv_ref[0,:,cs]=(a+conv_ref[0,cs,:].T).astype(BF)
        return go
    def to_lk(h):
        def go(): dlk[h]=nt(ds1_ref[rows[h],:],q_ref[0,rows[h]])
        return go
    def to_lq(h):
        def go(): dlq[h]=nt(ds3_ref[rows[h],:],k_ref[0,rows[h]])
        return go
    @pl.when(pl.program_id(1)==0)
    def _():
        for ref in (gq_ref,gk_ref,gv_ref,sq_ref,sv_ref): ref[...]=jnp.zeros_like(ref)
    def value_weights():
        dv=dv_ref[0]
        gv_ref[...]+=nn(dv,x_ref[0]); sv_ref[...]+=jnp.sum(dv.astype(F32),axis=1,keepdims=True)
    side=[]
    for h in heads: side+=[third(h,cs) for cs in chunks]+[to_lq(h)]+[first(h,cs) for cs in chunks]+[to_lk(h)]
    side+=[values(cs) for cs in chunks]+[value_weights]
    k2t=[a.T for a in k2]; k2tw=[wide(a) for a in k2t]
    def newton(n):
        def one():
            a=[stash_ref[0,h,2*n] for h in heads]; c=[stash_ref[0,h,2*n+1] for h in heads]
            state["p"]=[m[:,:LM] for m in a]; state["b"]=[tall(m[:,LM:]) for m in a]
            state["c"]=[tall(m[:,:LM]) for m in c]; state["zt"]=[m[:,LM:] for m in c]
            state["gz"]=[0.25*d for d in state["dz"]]
            state["dc"]=[mm3(state["zt"][h],state["gz"][h]) for h in heads]
            state["pw"]=[wide(m) for m in state["p"]]
        def two(): state["db"]=[nn(state["pw"][h],tall(state["dc"][h])) for h in heads]
        def three():
            da=[nn(state["pw"][h],tall(state["db"][h])) for h in heads]
            state["dp"]=[mm3(state["db"][h],eye(7.0)-state["p"][h])-nn(wide(state["dc"][h]),state["b"][h])-da[h] for h in heads]
        def four():
            for h in heads:
                t=mm3(state["dp"][h],state["zt"][h])
                state["dk2"][h]=t if state["dk2"][h] is None else state["dk2"][h]+t
            state["dz"]=[nn(wide(state["gz"][h]),state["c"][h])+nn(k2tw[h],tall(state["dp"][h])) for h in heads]
        return [one,two,three,four]
    chain=[step for n in reversed(range(NEWTON)) for step in newton(n)]
    weave(chain,side)
    lhq=[];lhk=[]
    for h in heads:
        i2=1.0/jnp.sum(k2[h]*k2[h]); dz=state["dz"][h]
        d=state["dk2"][h]+i2*dz.T-k2[h]*(2.0*i2*i2*jnp.sum(dz*k2t[h]))
        d=k2[h]*(d-jnp.sum(k2[h]*d,axis=1,keepdims=True))
        dlqh=dlq[h]+mm3(d,lk[h]); dlkh=dlk[h]+mm3(d.T,lq[h])
        lhq.append(jnp.concatenate([lk[h].T,dlqh.T*per],axis=1).astype(BF))
        lhk.append(jnp.concatenate([lq[h].T,dlkh.T*per],axis=1).astype(BF))
    for cs in chunks:
        hot=hot_ref[:,cs]
        for lh,ds_ref,out_ref in ((lhq,ds1_ref,dq_ref),(lhk,ds3_ref,dk_ref)):
            for h in heads:
                a=nn(lh[h],jnp.concatenate([ds_ref[rows[h],cs],hot],axis=0))
                out_ref[0,rows[h],cs]=(a*scale).astype(BF)
    dq=dq_ref[0]
    gq_ref[...]+=nn(dq,x_ref[0]); gk_ref[...]+=nn(dk_ref[0],x_ref[0])
    sq_ref[...]+=jnp.sum(dq.astype(F32),axis=1,keepdims=True)
def att_bwd(x,al,wo,q,k,v,k1,k3,inv,stash,small,tok,conv,group):
    B,T,D=x.shape
    seq=lambda s: pl.BlockSpec((1,)+s,lambda g,b:(b,)+(0,)*len(s))
    rows=pl.BlockSpec((1,GW,T),lambda g,b:(b,group,0))
    sq=lambda n: pl.BlockSpec((1,GH,n,LM,2*LM),lambda g,b:(b,group,0,0,0))
    whole=lambda r,c: pl.BlockSpec((r,c),lambda g,b:(0,0))
    sd=jax.ShapeDtypeStruct
    return pl.pallas_call(att_bwd_kernel,grid=(1,B),
        in_specs=[seq((T,D)),seq((T,D)),pl.BlockSpec((GW,D),lambda g,b:(group,0))]+[rows]*5+[
            pl.BlockSpec((1,1,8,T),lambda g,b:(b,group,0,0)),sq(2*NEWTON),sq(4),seq((1,T)),seq((T,GW))],
        out_specs=[seq((GW,T))]*3+[whole(GW,D)]*3+[whole(GW,1)]*2,
        out_shape=[sd((B,GW,T),BF)]*3+[sd((GW,D),F32)]*3+[sd((GW,1),F32)]*2,
        scratch_shapes=[pltpu.VMEM((GW,T),BF)]*3+[pltpu.VMEM((LM,T),BF)],
        compiler_params=pltpu.CompilerParams(vmem_limit_bytes=60*2**20))(
            x,al,wo,q,k,v,k1,k3,inv,stash,small,tok[:,None,:],conv)

KW=33; HALF=16; DOCS=4; GAP=16
def spread(dst, get, bounds, length, step):
    total=length+GAP*(DOCS+1)
    ids=lax.broadcasted_iota(jnp.int32,(step,128),0)
    for p0 in range(0,total,step):
        size=min(step,total-p0)
        acc=None
        for d in range(DOCS):
            s0=p0-GAP*(d+1)
            lo=max(s0,0); hi=min(s0+size,length)
            if hi<=lo: continue
            row=ids[:hi-lo]+lo
            inside=(row>=bounds[d])&(row<bounds[d+1])
            part=jnp.where(inside,get(lo,hi-lo),0.0)
            pads=[]
            if lo>s0: pads.append(jnp.zeros((lo-s0,128),F32))
            pads.append(part)
            if s0+size>hi: pads.append(jnp.zeros((s0+size-hi,128),F32))
            part=jnp.concatenate(pads,0) if len(pads)>1 else part
            acc=part if acc is None else acc+part
        if acc is None: acc=jnp.zeros((size,128),F32)
        dst[HALF+p0:HALF+p0+size,:]=acc
def collect(src, bounds, lo, size):
    row=lax.broadcasted_iota(jnp.int32,(size,128),0)+lo
    acc=None
    for d in range(DOCS):
        part=src[lo+GAP*(d+1):lo+GAP*(d+1)+size,:]
        acc=part if acc is None else jnp.where(row>=bounds[d],part,acc)
    return acc
BLOCK=64
def taps(ref, base, weight, sign):
    acc=None
    for r in range(8):
        win=ref[pl.ds(base+r,BLOCK+32),:] if r==0 else ref[pl.ds(base+r,BLOCK+24),:]
        for a in range(5 if r==0 else 4):
            o=8*a+r
            t=weight(o if sign>0 else 2*HALF-o)*win[8*a:8*a+BLOCK]
            acc=t if acc is None else acc+t
    return acc

def conv_fwd_kernel(bounds_ref, x_ref, wv_ref, vec_ref, w_ref, v_ref, out_ref, pad_ref, res_ref):
    b=pl.program_id(0)
    bounds=[bounds_ref[b,d] for d in range(DOCS+1)]
    length=v_ref.shape[1]; total=length+GAP*(DOCS+1)
    pad_ref[0:HALF,:]=jnp.zeros((HALF,128),F32); pad_ref[HALF+total:,:]=jnp.zeros((pad_ref.shape[0]-HALF-total,128),F32)
    for lo in range(0,length,256):
        v_ref[0,lo:lo+256,:]=nt(x_ref[0,lo:lo+256,:],wv_ref[...])+vec_ref[1:2,:]
    spread(pad_ref, lambda lo,n: v_ref[0,lo:lo+n,:], bounds, length, BLOCK)
    def block(i,c):
        base=pl.multiple_of(i*BLOCK,BLOCK)
        res_ref[pl.ds(base,BLOCK),:]=taps(pad_ref, base, lambda s: w_ref[s:s+1,:], 1)
        return c
    lax.fori_loop(0,-(-total//BLOCK),block,0)
    for lo in range(0,length,BLOCK):
        out_ref[0,lo:lo+BLOCK,:]=collect(res_ref,bounds,lo,BLOCK)
def padded_rows(length):
    total=length+GAP*(DOCS+1)
    return -(-total//BLOCK)*BLOCK

def conv_fwd(bounds, x, w_v, vec, w):
    B,L,D=x.shape
    rows=padded_rows(L)
    slab=pl.BlockSpec((1,L,128),lambda b,c,_:(b,0,c)); big=jax.ShapeDtypeStruct((B,L,D),F32)
    return pl.pallas_call(conv_fwd_kernel,grid_spec=pltpu.PrefetchScalarGridSpec(num_scalar_prefetch=1,grid=(B,D//128),
        in_specs=[pl.BlockSpec((1,L,D),lambda b,c,_:(b,0,0)),pl.BlockSpec((128,D),lambda b,c,_:(c,0)),
            pl.BlockSpec((8,128),lambda b,c,_:(0,c)),pl.BlockSpec((KW,128),lambda b,c,_:(0,c))],
        out_specs=[slab,slab],
        scratch_shapes=[pltpu.VMEM((rows+2*HALF+8,128),F32),pltpu.VMEM((rows,128),F32)]),
        out_shape=[big,big],
        compiler_params=pltpu.CompilerParams(vmem_limit_bytes=60*2**20))(bounds,x,w_v,vec,w)
def conv_bwd_kernel(bounds_ref, v_ref, al_ref, wo_ref, w_ref, dv_ref, dw_ref, vpad_ref, gpad_ref, res_ref, acc_ref, g_ref):
    b=pl.program_id(1)
    bounds=[bounds_ref[b,d] for d in range(DOCS+1)]
    length=v_ref.shape[1]; total=length+GAP*(DOCS+1)
    for lo in range(0,length,256):
        g_ref[lo:lo+256,:]=nn(al_ref[0,lo:lo+256,:],wo_ref[...])
    for ref in (vpad_ref,gpad_ref):
        ref[0:HALF,:]=jnp.zeros((HALF,128),F32)
        ref[HALF+total:,:]=jnp.zeros((ref.shape[0]-HALF-total,128),F32)
    spread(vpad_ref, lambda lo,n: v_ref[0,lo:lo+n,:], bounds, length, BLOCK)
    spread(gpad_ref, lambda lo,n: g_ref[lo:lo+n,:], bounds, length, BLOCK)
    @pl.when(b==0)
    def _(): acc_ref[...]=jnp.zeros_like(acc_ref)
    def block(i,c):
        base=pl.multiple_of(i*BLOCK,BLOCK)
        here=vpad_ref[pl.ds(base+HALF,BLOCK),:]
        acc=None
        for r in range(8):
            n=5 if r==0 else 4
            win=gpad_ref[pl.ds(base+r,BLOCK+8*(n-1)),:]
            for a in range(n):
                s=2*HALF-(8*a+r)
                x=win[8*a:8*a+BLOCK]
                t=w_ref[s:s+1,:]*x
                acc=t if acc is None else acc+t
                p=(here*x).reshape(BLOCK//8,8,128)
                acc_ref[s]+=jnp.sum(p,axis=0)
        res_ref[pl.ds(base,BLOCK),:]=acc
        return c
    lax.fori_loop(0,-(-total//BLOCK),block,0)
    for lo in range(0,length,BLOCK):
        dv_ref[0,lo:lo+BLOCK,:]=collect(res_ref,bounds,lo,BLOCK)
    @pl.when(b==pl.num_programs(1)-1)
    def _():
        for s in range(KW):
            dw_ref[s:s+1,:]=jnp.sum(acc_ref[s],axis=0,keepdims=True)

def conv_bwd(bounds, v, al, w_o, w, group):
    B,L,D=v.shape
    rows=padded_rows(L); slabs=GW//128; at=group*slabs
    return pl.pallas_call(conv_bwd_kernel,grid_spec=pltpu.PrefetchScalarGridSpec(num_scalar_prefetch=1,grid=(slabs,B),
        in_specs=[pl.BlockSpec((1,L,128),lambda c,b,_:(b,0,at+c)),pl.BlockSpec((1,L,D),lambda c,b,_:(b,0,0)),
            pl.BlockSpec((D,128),lambda c,b,_:(0,at+c)),pl.BlockSpec((KW,128),lambda c,b,_:(0,at+c))],
        out_specs=[pl.BlockSpec((1,L,128),lambda c,b,_:(b,0,c)),pl.BlockSpec((KW,128),lambda c,b,_:(0,c))],
        scratch_shapes=[pltpu.VMEM((rows+2*HALF+8,128),F32)]*2+[pltpu.VMEM((rows,128),F32),pltpu.VMEM((KW,8,128),F32),pltpu.VMEM((L,128),F32)]),
        out_shape=[jax.ShapeDtypeStruct((B,L,GW),F32),jax.ShapeDtypeStruct((KW,GW),F32)],
        compiler_params=pltpu.CompilerParams(vmem_limit_bytes=60*2**20))(bounds,v,al,w_o,w)

def gelu_parts(x):
    size=jnp.abs(x)
    density=jnp.exp(-0.5*x*x)*0.3989422804014327
    t=1.0/(1.0+0.2316419*size)
    tail=density*(t*(0.319381530+t*(-0.356563782+t*(1.781477937+t*(-1.821255978+t*1.330274429)))))
    dist=jnp.where(x<0.0,tail,1.0-tail)
    return dist, x*density
def norm(v):
    mean=jnp.mean(v,axis=-1,keepdims=True); c=v-mean
    r=lax.rsqrt(jnp.mean(c*c,axis=-1,keepdims=True)+1e-5)
    return c*r, r
def norm_back(up,n,r,g):
    e=up*g
    return r*(e-jnp.mean(e,axis=-1,keepdims=True)-n*jnp.mean(e*n,axis=-1,keepdims=True))
def ffn_kernel(chunks, ctx_ref,x_ref,cot_ref,wo_ref,wu_ref,wd_ref,vec_ref,bu_ref,
               out_ref,normed_ref,hidden_ref,down_ref,up_ref,one_ref,att_ref,sums_ref,sumu_ref,slope_ref):
    width=wu_ref.shape[0]//chunks
    @pl.when(pl.program_id(0)==0)
    def _():
        sums_ref[...]=jnp.zeros_like(sums_ref); sumu_ref[...]=jnp.zeros_like(sumu_ref)
    v=lambda i: vec_ref[i:i+1,:]
    b_o,g1,s1,b_d,g2,s2=[v(i) for i in range(2,8)]
    n1,r1=norm(x_ref[...].astype(F32)+(nt(ctx_ref[...],wo_ref[...])+b_o))
    normed=n1*g1+s1
    low=normed.astype(BF); normed_ref[...]=low
    down=None
    for k in range(chunks):
        part=slice(k*width,(k+1)*width)
        pre=nt(low,wu_ref[part,:])+bu_ref[:,part]
        dist,slope=gelu_parts(pre)
        slope_ref[:,part]=dist+slope
        hid=(pre*dist).astype(BF); hidden_ref[:,part]=hid
        add=nt(hid,wd_ref[k]); down=add if down is None else down+add
    n2,r2=norm(normed+(down+b_d))
    out_ref[...]=(n2*g2+s2).astype(BF)
    cot=cot_ref[...].astype(F32)
    g_two=norm_back(cot,n2,r2,g2)
    low2=g_two.astype(BF); down_ref[...]=low2
    back=g_two
    for k in range(chunks):
        part=slice(k*width,(k+1)*width)
        hg=nn(low2,wd_ref[k])
        upl=(hg*slope_ref[:,part]).astype(BF); up_ref[:,part]=upl
        sumu_ref[:,part]+=jnp.sum(upl.astype(F32),axis=0,keepdims=True)
        back=back+nn(upl,wu_ref[part,:])
    g_one=norm_back(back,n1,r1,g1)
    one_ref[...]=g_one
    al=g_one.astype(BF); att_ref[...]=al
    s=lambda a: jnp.sum(a,axis=0,keepdims=True)
    sums_ref[...]+=jnp.concatenate([s(al.astype(F32)),s(back*n1),s(back),s(low2.astype(F32)),s(cot*n2),s(cot),jnp.zeros((2,n1.shape[1]),F32)],axis=0)
def ffn(ctx,x,cot,wo,wu,wd,vec,bu,block=512):
    chunks=wd.shape[0]
    T,D=x.shape; F=wu.shape[0]
    row=lambda w: pl.BlockSpec((block,w),lambda i:(i,0))
    full=lambda a: pl.BlockSpec(a.shape,lambda i:(0,)*a.ndim,pipeline_mode=pl.Buffered(1))
    keep=lambda r,w: pl.BlockSpec((r,w),lambda i:(0,0))
    sd=jax.ShapeDtypeStruct
    return pl.pallas_call(functools.partial(ffn_kernel,chunks),grid=(T//block,),
        in_specs=[row(D),row(D),row(D),full(wo),full(wu),full(wd),full(vec),full(bu)],
        out_specs=[row(D),row(D),row(F),row(D),row(F),row(D),row(D),keep(8,D),keep(1,F)],
        out_shape=[sd((T,D),BF),sd((T,D),BF),sd((T,F),BF),sd((T,D),BF),sd((T,F),BF),sd((T,D),F32),sd((T,D),BF),sd((8,D),F32),sd((1,F),F32)],
        scratch_shapes=[pltpu.VMEM((block,F),F32)],
        compiler_params=pltpu.CompilerParams(vmem_limit_bytes=60*2**20,dimension_semantics=("arbitrary",)),
    )(ctx,x,cot,wo,wu,wd,vec,bu)


def digits():
    found = []
    for axis in ("wide", "narrow"):
        stride = lax.axis_size(axis) // 2
        while stride >= 1:
            found.append((axis, stride))
            stride //= 2
    return found


def link_order(number):
    count = len(digits())
    if lax.axis_size("wide") == 8 and lax.axis_size("narrow") == 4:
        return [(4, 2, 3, 1, 0), (4, 3, 1, 2, 0), (4, 1, 2, 3, 0)][number]
    return tuple(range(count - 1, -1, -1))


def exchange(values, axis, stride):
    return lax.ppermute(values, axis, [(i, i ^ stride) for i in range(lax.axis_size(axis))])


def digit_of(axis, stride):
    return (lax.axis_index(axis) // stride) % 2


def gather_rows(shard, number):
    places = digits()
    held = shard.reshape((1,) * len(places) + shard.shape)
    for dim in link_order(number)[::-1]:
        mine = digit_of(*places[dim])
        got = exchange(held, *places[dim])
        first = jnp.where(mine == 0, held, got)
        second = jnp.where(mine == 0, got, held)
        held = jnp.concatenate([first, second], dim)
    return held.reshape((-1,) + shard.shape)


def scatter_start(whole):
    return whole.reshape((2,) * len(digits()) + whole.shape[1:])


def scatter_step(held, number, step):
    places = digits()
    dim = link_order(number)[step]
    mine = digit_of(*places[dim])
    keep = lax.dynamic_slice_in_dim(held, mine, 1, dim).astype(F32)
    send = lax.dynamic_slice_in_dim(held, 1 - mine, 1, dim).astype(BF)
    return keep + exchange(send, *places[dim]).astype(F32)


def scatter_rest(held, number, step):
    for later in range(step, len(digits())):
        held = scatter_step(held, number, later)
    return held.reshape(held.shape[-2:])


def pad_rows(flat, rows):
    count, length = flat.shape
    return jnp.pad(flat, ((0, 0), (0, rows * 768 - length))).reshape(count, rows, 768)


def across_rows(left_side, right_side):
    return lax.dot_general(left_side, right_side, (((0,), (0,)), ((), ())), preferred_element_type=F32)


def shards(
    inputs,
    tok_landmark,
    landmark_doc,
    w_query,
    b_query,
    w_key,
    w_value,
    b_value,
    conv_weight,
    w_out,
    b_out,
    gain_one,
    shift_one,
    w_up,
    b_up,
    w_down,
    b_down,
    gain_two,
    shift_two,
    cotangent,
):
    batch_rows, sequence_length, feature_width = inputs.shape
    group_count = lax.axis_size("wide") * lax.axis_size("narrow")
    own = feature_width // group_count
    tokens = batch_rows * sequence_length
    lines = b_up.shape[0] // own
    vectors = (b_query, b_value, b_out, gain_one, shift_one, b_down, gain_two, shift_two)
    flat = jnp.concatenate([conv_weight.reshape(-1)] + list(vectors) + [b_up])
    small = pad_rows(flat[None], -(-flat.shape[0] // 768))[0]
    gathered_v = gather_rows(jnp.concatenate([w_value.T, small], axis=0), 0)
    w_q = gather_rows(w_query.T, 1).reshape(feature_width, feature_width)
    w_k = gather_rows(w_key.T, 2).reshape(feature_width, feature_width)
    w_v = gathered_v[:, :own].reshape(feature_width, feature_width)
    small = gathered_v[:, own:].reshape(group_count, -1).astype(F32)[:, : flat.shape[0]]
    small = small.reshape(group_count, -1, own)
    b_u = small[:, KW + 8 :].reshape(1, -1)
    small = jnp.moveaxis(small[:, : KW + 8], 0, 1).reshape(KW + 8, feature_width)
    conv_taps, vec = small[:KW], small[KW:]
    ff_count = w_down.shape[0] // feature_width
    shard = jnp.concatenate(
        [w_out.T, w_up.T] + [w_down[i * feature_width : (i + 1) * feature_width].T for i in range(ff_count)]
    )
    gathered = lax.all_gather(shard, ("wide", "narrow"), axis=0)
    w_o = gathered[:, :own].reshape(feature_width, feature_width)
    w_u = gathered[:, own : own * (1 + lines)].reshape(-1, feature_width)
    w_d = jnp.moveaxis(
        gathered[:, own * (1 + lines) :].reshape(group_count, ff_count, own, feature_width), 0, 1
    ).reshape(ff_count, feature_width, feature_width)
    member = tok_landmark[:, None, :] == jnp.arange(LM)[None, :, None]
    means = jnp.einsum("bjt,bti->bji", member.astype(BF), inputs, preferred_element_type=F32)
    means = means / jnp.sum(member, axis=2)[..., None].astype(F32)
    doc = jnp.sum(jnp.where(member, landmark_doc[:, :, None], 0), axis=1)
    bounds = jnp.sum(doc[:, None, :] < jnp.arange(DOCS + 1)[None, :, None], axis=2).astype(jnp.int32)
    rows_low = inputs.reshape(tokens, feature_width)
    value_rows, conv_part = conv_fwd(bounds, inputs, w_v, vec, conv_taps)
    q, k, v, k1, k3, inv, stash, landmarks, context = att_fwd(
        inputs, means, w_q, w_k, w_v, vec, tok_landmark, landmark_doc, conv_part
    )
    context = context.reshape(tokens, feature_width)
    layer_out, normed, hidden, down_low, up_low, grad_one, att_low, sums, sums_up = ffn(
        context, rows_low, cotangent.reshape(tokens, feature_width), w_o, w_u, w_d, vec, b_u
    )

    def by_device(values):
        return values.reshape((group_count, -1) + values.shape[1:])

    early = jnp.concatenate([by_device(sums[i]) for i in range(6)] + [by_device(sums_up[0])], axis=1)
    grad_out = jnp.concatenate(
        [by_device(across_rows(att_low, context)), pad_rows(early, -(-early.shape[1] // 768))], axis=1
    )
    shares = [
        scatter_start(by_device(across_rows(up_low, normed))),
        scatter_start(by_device(across_rows(down_low, hidden))),
        scatter_start(grad_out),
    ]

    def advance(shares, step):
        return [scatter_step(share, i, step) for i, share in enumerate(shares)]

    shares = advance(shares, 0)
    w_plain = w_o.T
    att_low = att_low.reshape(inputs.shape)
    groups = feature_width // GW
    conv_grads, att_grads = [], []
    att_low, shares = lax.optimization_barrier((att_low, shares))
    for group in range(groups):
        moved = advance(shares, 1 + group)
        found = conv_bwd(bounds, value_rows, att_low, w_o, conv_taps, group)
        att_low, found, shares = lax.optimization_barrier((att_low, found, moved))
        conv_grads.append(found)
    for group in range(groups):
        moved = advance(shares, 1 + groups + group)
        found = att_bwd(
            inputs, att_low, w_plain, q, k, v, k1, k3, inv, stash, landmarks, tok_landmark,
            conv_grads[group][0], group,
        )
        att_low, found, shares = lax.optimization_barrier((att_low, found, moved))
        att_grads.append(found)
    share_up, share_down, share_out = [
        scatter_rest(share, i, 1 + 2 * groups) for i, share in enumerate(shares)
    ]
    grad_q, grad_k, grad_v, sum_q, sum_v = [
        jnp.concatenate([found[i] for found in att_grads]) for i in range(3, 8)
    ]
    taps_grad = jnp.concatenate([found[1] for found in conv_grads], axis=1)
    late = jnp.concatenate(
        [by_device(taps_grad.T).reshape(group_count, -1), by_device(sum_q[:, 0]), by_device(sum_v[:, 0])], axis=1
    )
    grad_v = jnp.concatenate([by_device(grad_v), pad_rows(late, -(-late.shape[1] // 768))], axis=1)
    share_v = scatter_rest(scatter_start(grad_v), 0, 0)
    share_q = scatter_rest(scatter_start(by_device(grad_q)), 1, 0)
    share_k = scatter_rest(scatter_start(by_device(grad_k)), 2, 0)
    input_grad = grad_one.reshape(inputs.shape)
    for group, found in enumerate(att_grads):
        for grad, weight in zip(found[:3], (w_q, w_k, w_v)):
            part = weight[group * GW : (group + 1) * GW]
            input_grad = input_grad + jnp.einsum("bot,oi->bti", grad, part, preferred_element_type=F32)
    early = share_out[own:].reshape(-1)
    late = share_v[own:].reshape(-1)
    return (
        layer_out.reshape(inputs.shape),
        input_grad,
        share_q.T,
        late[own * KW : own * KW + own],
        share_k.T,
        share_v[:own].T,
        late[own * KW + own : own * KW + 2 * own],
        late[: own * KW].reshape(own, KW).T,
        share_out[:own].T,
        early[:own],
        early[own : 2 * own],
        early[2 * own : 3 * own],
        share_up.T,
        early[6 * own : 6 * own + b_up.shape[0]],
        share_down.T,
        early[3 * own : 4 * own],
        early[4 * own : 5 * own],
        early[5 * own : 6 * own],
    )


def solution(mesh):
    return jax.shard_map(
        shards,
        mesh=mesh,
        in_specs=(
            P(("wide", "narrow"), None, None),
            P(("wide", "narrow"), None),
            P(("wide", "narrow"), None),
            P(None, ("wide", "narrow")),
            P(("wide", "narrow")),
            P(None, ("wide", "narrow")),
            P(None, ("wide", "narrow")),
            P(("wide", "narrow")),
            P(None, ("wide", "narrow")),
            P(None, ("wide", "narrow")),
            P(("wide", "narrow")),
            P(("wide", "narrow")),
            P(("wide", "narrow")),
            P(None, ("wide", "narrow")),
            P(("wide", "narrow")),
            P(None, ("wide", "narrow")),
            P(("wide", "narrow")),
            P(("wide", "narrow")),
            P(("wide", "narrow")),
            P(("wide", "narrow"), None, None),
        ),
        out_specs=(
            P(("wide", "narrow"), None, None),
            P(("wide", "narrow"), None, None),
            P(None, ("wide", "narrow")),
            P(("wide", "narrow")),
            P(None, ("wide", "narrow")),
            P(None, ("wide", "narrow")),
            P(("wide", "narrow")),
            P(None, ("wide", "narrow")),
            P(None, ("wide", "narrow")),
            P(("wide", "narrow")),
            P(("wide", "narrow")),
            P(("wide", "narrow")),
            P(None, ("wide", "narrow")),
            P(("wide", "narrow")),
            P(None, ("wide", "narrow")),
            P(("wide", "narrow")),
            P(("wide", "narrow")),
            P(("wide", "narrow")),
        ),
        check_vma=False,
    )
```

```python
import functools

import jax
import jax.numpy as jnp
from jax import lax
from jax.experimental import pallas as pl
from jax.experimental.pallas import tpu as pltpu
from jax.sharding import PartitionSpec as P

BF = jnp.bfloat16
F32 = jnp.float32
HW=64; LM=64; NEWTON=6; GH=6; GW=GH*HW
CHUNK=256
KW=33
SMALL=48
def nt(a,b): return lax.dot_general(a,b,(((1,),(1,)),((),())),preferred_element_type=F32)
def nn(a,b): return lax.dot_general(a,b,(((1,),(0,)),((),())),preferred_element_type=F32)
def split(a):
    hi=a.astype(BF); return hi,(a-hi.astype(F32)).astype(BF)
def wide(a):
    hi,lo=split(a); return jnp.concatenate([hi,hi,lo],axis=1)
def tall(b):
    hi,lo=split(b); return jnp.concatenate([hi,lo,hi],axis=0)
def mm3(a,b): return nn(wide(a),tall(b))
def eye(c):
    return jnp.where(lax.broadcasted_iota(jnp.int32,(LM,LM),0)==lax.broadcasted_iota(jnp.int32,(LM,LM),1),c,0.0)
def weave(first, second):
    done=0
    for i,step in enumerate(first):
        step()
        upto=(i+1)*len(second)//len(first)
        for other in second[done:upto]: other()
        done=upto
def att_fwd_kernel(x_ref,mean_ref,wq_ref,wk_ref,wv_ref,vec_ref,tok_ref,ldc_ref,ldr_ref,conv_ref,
               q_ref,k_ref,v_ref,k1_ref,k3_ref,inv_ref,stash_ref,small_ref,ctx_ref,
               qlo_ref,klo_ref,score_ref,bias_ref):
    T=x_ref.shape[1]
    heads=range(GH); chunks=[slice(c,c+CHUNK) for c in range(0,T,CHUNK)]
    rows=[slice(h*HW,(h+1)*HW) for h in heads]
    scale=HW**-0.25
    bq=vec_ref[KW:KW+1,:].T; bv=vec_ref[KW+1:KW+2,:].T
    ldc=ldc_ref[0]
    for cs in chunks:
        member=lax.broadcasted_iota(jnp.int32,(LM,CHUNK),0)==tok_ref[0,:,cs]
        doc=jnp.sum(jnp.where(member,ldc,0),axis=0,keepdims=True)
        bias_ref[:,cs]=jnp.where(doc==ldc,0.0,-1e30)
    mean=jnp.concatenate(split(mean_ref[0]),axis=0)
    def land(w_ref):
        both=nt(w_ref[...],mean)
        return both[:,:LM]+both[:,LM:]
    lqt=(land(wq_ref)+bq)*scale; lkt=land(wk_ref)*scale
    lq=[lqt[r].T for r in rows]; lk=[lkt[r].T for r in rows]
    lqw=[wide(a) for a in lq]; lkw=[wide(a) for a in lk]
    allow2=ldc==ldr_ref[0]
    k2=[];z=[]
    for h in heads:
        s=jnp.where(allow2,nn(lqw[h],tall(lkt[rows[h]])),-1e30)
        e=jnp.exp(s-jnp.max(s,axis=1,keepdims=True))
        k2.append(e/jnp.sum(e,axis=1,keepdims=True))
        z.append(k2[h].T*(1.0/jnp.sum(k2[h]*k2[h])))
    state={"z":z}
    k2w=[wide(a) for a in k2]
    def newton(n):
        def one():
            state["p"]=[nn(k2w[h],tall(state["z"][h])) for h in heads]
            state["pw"]=[wide(a) for a in state["p"]]
        def two(): state["b"]=[eye(15.0)-nn(state["pw"][h],tall(eye(7.0)-state["p"][h])) for h in heads]
        def three(): state["c"]=[eye(13.0)-nn(state["pw"][h],tall(state["b"][h])) for h in heads]
        def four():
            for h in heads:
                stash_ref[0,h,2*n]=jnp.concatenate([state["p"][h],state["b"][h]],axis=1)
                stash_ref[0,h,2*n+1]=jnp.concatenate([state["c"][h],state["z"][h].T],axis=1)
            state["z"]=[0.25*mm3(state["z"][h],state["c"][h]) for h in heads]
        return [one,two,three,four]
    chain=[step for n in range(NEWTON) for step in newton(n)]
    side=[]
    def project(cs):
        x=x_ref[0,cs,:]
        def q():
            a=(nt(wq_ref[...],x)+bq)*scale
            hi,lo=split(a); q_ref[0,:,cs]=hi; qlo_ref[:,cs]=lo
        def k():
            a=nt(wk_ref[...],x)*scale
            hi,lo=split(a); k_ref[0,:,cs]=hi; klo_ref[:,cs]=lo
        def v(): v_ref[0,:,cs]=(nt(wv_ref[...],x)+bv).astype(BF)
        return [q,k,v]
    tops=[None]*GH; sums=[None]*GH; r=[None]*GH
    def lanes(a): return [a[:,i:i+128] for i in range(0,CHUNK,128)]
    def first(h,cs):
        def go():
            hi=q_ref[0,rows[h],cs]
            s=nn(lkw[h],jnp.concatenate([hi,qlo_ref[rows[h],cs],hi],axis=0))+bias_ref[:,cs]
            e=jnp.exp(s-jnp.max(s,axis=0,keepdims=True))
            e=e.astype(BF); k1_ref[0,rows[h],cs]=e
            inv_ref[0,0,h:h+1,cs]=1.0/jnp.sum(e.astype(F32),axis=0,keepdims=True)
        return go
    def third(h,cs):
        def go():
            hi=k_ref[0,rows[h],cs]
            s=nn(lqw[h],jnp.concatenate([hi,klo_ref[rows[h],cs],hi],axis=0))+bias_ref[:,cs]
            score_ref[rows[h],cs]=s
            for a in lanes(s): tops[h]=a if tops[h] is None else jnp.maximum(tops[h],a)
        return go
    def raised(h,cs):
        def go():
            if cs.start==0: tops[h]=jnp.max(tops[h],axis=1,keepdims=True)
            e=jnp.exp(score_ref[rows[h],cs]-tops[h])
            e=e.astype(BF); k3_ref[0,rows[h],cs]=e
            for a in lanes(e.astype(F32)): sums[h]=a if sums[h] is None else sums[h]+a
        return go
    def gathered(h):
        def go():
            sums[h]=1.0/jnp.sum(sums[h],axis=1,keepdims=True)
            r[h]=nt(k3_ref[0,rows[h]],v_ref[0,rows[h]])*sums[h]
        return go
    for cs in chunks: side+=project(cs)
    for h in heads:
        side+=[third(h,cs) for cs in chunks]
        side+=[raised(h,cs) for cs in chunks]+[gathered(h)]
        side+=[first(h,cs) for cs in chunks]
    weave(chain,side)
    uts=[]
    for h in heads:
        u=mm3(state["z"][h],r[h])
        small_ref[0,h,0]=jnp.concatenate([lq[h],lk[h]],axis=1)
        small_ref[0,h,1]=jnp.concatenate([k2[h],state["z"][h].T],axis=1)
        small_ref[0,h,2]=jnp.concatenate([r[h],u],axis=1)
        small_ref[0,h,3]=jnp.broadcast_to(sums[h],(LM,128))
        uts.append(u.T.astype(BF))
    for cs in chunks:
        mixed=jnp.concatenate([nn(uts[h],k1_ref[0,rows[h],cs])*inv_ref[0,0,h:h+1,cs] for h in heads],axis=0)
        ctx_ref[0,cs,:]=(mixed.T+conv_ref[0,cs,:]).astype(BF)
def att_specs(D,T):
    seq=lambda s: pl.BlockSpec((1,)+s,lambda g,b:(b,)+(0,)*len(s))
    wsp=pl.BlockSpec((GW,D),lambda g,b:(g,0)); bsp=pl.BlockSpec((GW,1),lambda g,b:(g,0))
    rows=pl.BlockSpec((1,GW,T),lambda g,b:(b,g,0)); cols=pl.BlockSpec((1,T,GW),lambda g,b:(b,0,g))
    sq=lambda n: pl.BlockSpec((1,GH,n,LM,2*LM),lambda g,b:(b,g,0,0,0))
    turned=pl.BlockSpec((1,1,8,T),lambda g,b:(b,g,0,0))
    return seq,wsp,bsp,rows,cols,sq,turned
def att_fwd(x,mean,wq,wk,wv,vec,tok,ld,conv):
    B,T,D=x.shape; G=D//GW; H=D//HW
    seq,wsp,bsp,rows,cols,sq,turned=att_specs(D,T)
    sd=jax.ShapeDtypeStruct; big=sd((B,D,T),BF)
    return pl.pallas_call(att_fwd_kernel,grid=(G,B),
        in_specs=[seq((T,D)),seq((LM,D)),wsp,wsp,wsp,pl.BlockSpec((SMALL,GW),lambda g,b:(0,g)),seq((1,T)),seq((LM,1)),seq((1,LM)),cols],
        out_specs=[rows]*5+[turned,sq(2*NEWTON),sq(4),cols],
        out_shape=[big]*5+[sd((B,G,8,T),F32),sd((B,H,2*NEWTON,LM,2*LM),F32),sd((B,H,4,LM,2*LM),F32),sd((B,T,D),BF)],
        scratch_shapes=[pltpu.VMEM((GW,T),BF)]*2+[pltpu.VMEM((GW,T),F32),pltpu.VMEM((LM,T),F32)],
        compiler_params=pltpu.CompilerParams(vmem_limit_bytes=60*2**20))(
            x,mean,wq,wk,wv,vec,tok[:,None,:],ld[:,:,None],ld[:,None,:],conv)
def att_bwd_kernel(x_ref,al_ref,wo_ref,q_ref,k_ref,v_ref,k1_ref,k3_ref,inv_ref,stash_ref,small_ref,tok_ref,
               dq_ref,dk_ref,dv_ref,gqk_ref,sq_ref,
               g_ref,ds1_ref,ds3_ref,hot_ref):
    T=x_ref.shape[1]
    heads=range(GH); chunks=[slice(c,c+CHUNK) for c in range(0,T,CHUNK)]
    rows=[slice(h*HW,(h+1)*HW) for h in heads]
    scale=HW**-0.25
    for cs in chunks:
        member=lax.broadcasted_iota(jnp.int32,(LM,CHUNK),0)==tok_ref[0,:,cs]
        hot_ref[:,cs]=jnp.where(member,1.0,0.0).astype(BF)
    per=1.0/nt(jnp.ones((8,T),BF),hot_ref[...])[0:1]
    left=lambda i: [small_ref[0,h,i,:,:LM] for h in heads]
    right=lambda i: [small_ref[0,h,i,:,LM:] for h in heads]
    lq,lk,k2,zt,r,u=left(0),right(0),left(1),right(1),left(2),right(2)
    inv=[small_ref[0,h,3,:,:LM] for h in heads]
    ub=[a.astype(BF) for a in u]
    def upstream(cs):
        def go():
            a=nt(wo_ref[...],al_ref[0,cs,:])
            for h in heads: g_ref[rows[h],cs]=(a[rows[h]]*inv_ref[0,0,h:h+1,cs]).astype(BF)
        return go
    def first(h,cs):
        def go():
            k1=k1_ref[0,rows[h],cs].astype(F32)
            t=k1*nn(ub[h],g_ref[rows[h],cs])
            ds1_ref[rows[h],cs]=(t-k1*(jnp.sum(t,axis=0,keepdims=True)*inv_ref[0,0,h:h+1,cs])).astype(BF)
        return go
    for cs in chunks: upstream(cs)()
    du=[nt(k1_ref[0,rows[h]],g_ref[rows[h],:]) for h in heads]
    dr=[mm3(zt[h],du[h]) for h in heads]
    state={"dz":[mm3(du[h],r[h].T) for h in heads],"dk2":[None]*GH}
    drs=[(dr[h]*inv[h]) for h in heads]
    drb=[a.astype(BF) for a in drs]; drt=[a.T.astype(BF) for a in drs]
    delta=[jnp.sum(drb[h].astype(F32)*r[h],axis=1,keepdims=True) for h in heads]
    dlq=[None]*GH; dlk=[None]*GH
    def third(h,cs):
        def go():
            d=k3_ref[0,rows[h],cs].astype(F32)*(nn(drb[h],v_ref[0,rows[h],cs])-delta[h])
            ds3_ref[rows[h],cs]=d.astype(BF)
        return go
    def values(cs):
        def go():
            a=jnp.concatenate([nn(drt[h],k3_ref[0,rows[h],cs]) for h in heads],axis=0)
            dv_ref[0,:,cs]=a
        return go
    def to_lk(h):
        def go(): dlk[h]=nt(ds1_ref[rows[h],:],q_ref[0,rows[h]])
        return go
    def to_lq(h):
        def go(): dlq[h]=nt(ds3_ref[rows[h],:],k_ref[0,rows[h]])
        return go
    @pl.when(pl.program_id(1)==0)
    def _():
        for ref in (gqk_ref,sq_ref): ref[...]=jnp.zeros_like(ref)
    side=[]
    for h in heads: side+=[third(h,cs) for cs in chunks]+[to_lq(h)]+[first(h,cs) for cs in chunks]+[to_lk(h)]
    side+=[values(cs) for cs in chunks]
    k2t=[a.T for a in k2]; k2tw=[wide(a) for a in k2t]
    def newton(n):
        def one():
            a=[stash_ref[0,h,2*n] for h in heads]; c=[stash_ref[0,h,2*n+1] for h in heads]
            state["p"]=[m[:,:LM] for m in a]; state["b"]=[tall(m[:,LM:]) for m in a]
            state["c"]=[tall(m[:,:LM]) for m in c]; state["zt"]=[m[:,LM:] for m in c]
            state["gz"]=[0.25*d for d in state["dz"]]
            state["dc"]=[mm3(state["zt"][h],state["gz"][h]) for h in heads]
            state["pw"]=[wide(m) for m in state["p"]]
        def two(): state["db"]=[nn(state["pw"][h],tall(state["dc"][h])) for h in heads]
        def three():
            da=[nn(state["pw"][h],tall(state["db"][h])) for h in heads]
            state["dp"]=[mm3(state["db"][h],eye(7.0)-state["p"][h])-nn(wide(state["dc"][h]),state["b"][h])-da[h] for h in heads]
        def four():
            for h in heads:
                t=mm3(state["dp"][h],state["zt"][h])
                state["dk2"][h]=t if state["dk2"][h] is None else state["dk2"][h]+t
            state["dz"]=[nn(wide(state["gz"][h]),state["c"][h])+nn(k2tw[h],tall(state["dp"][h])) for h in heads]
        return [one,two,three,four]
    chain=[step for n in reversed(range(NEWTON)) for step in newton(n)]
    weave(chain,side)
    lhq=[];lhk=[]
    for h in heads:
        i2=1.0/jnp.sum(k2[h]*k2[h]); dz=state["dz"][h]
        d=state["dk2"][h]+i2*dz.T-k2[h]*(2.0*i2*i2*jnp.sum(dz*k2t[h]))
        d=k2[h]*(d-jnp.sum(k2[h]*d,axis=1,keepdims=True))
        dlqh=dlq[h]+mm3(d,lk[h]); dlkh=dlk[h]+mm3(d.T,lq[h])
        lhq.append(jnp.concatenate([lk[h].T,dlqh.T*per],axis=1).astype(BF))
        lhk.append(jnp.concatenate([lq[h].T,dlkh.T*per],axis=1).astype(BF))
    for cs in chunks:
        hot=hot_ref[:,cs]
        for lh,ds_ref,out_ref in ((lhq,ds1_ref,dq_ref),(lhk,ds3_ref,dk_ref)):
            for h in heads:
                a=nn(lh[h],jnp.concatenate([ds_ref[rows[h],cs],hot],axis=0))
                out_ref[0,rows[h],cs]=(a*scale).astype(BF)
    dq=dq_ref[0]
    gqk_ref[0]+=nn(dq,x_ref[0]); gqk_ref[1]+=nn(dk_ref[0],x_ref[0])
    sq_ref[...]+=jnp.sum(dq.astype(F32),axis=1,keepdims=True)
def att_bwd(x,al,wo,q,k,v,k1,k3,inv,stash,small,tok):
    B,T,D=x.shape; G=D//GW
    seq,wsp,bsp,rows,cols,sq,turned=att_specs(D,T)
    sd=jax.ShapeDtypeStruct; big=sd((B,D,T),BF)
    return pl.pallas_call(att_bwd_kernel,grid=(G,B),
        in_specs=[seq((T,D)),seq((T,D)),wsp]+[rows]*5+[turned,sq(2*NEWTON),sq(4),seq((1,T))],
        out_specs=[rows]*3+[pl.BlockSpec((2,GW,D),lambda g,b:(0,g,0)),bsp],
        out_shape=[big,big,sd((B,D,T),F32),sd((2,D,D),F32),sd((D,1),F32)],
        scratch_shapes=[pltpu.VMEM((GW,T),BF)]*3+[pltpu.VMEM((LM,T),BF)],
        compiler_params=pltpu.CompilerParams(vmem_limit_bytes=60*2**20))(
            x,al,wo,q,k,v,k1,k3,inv,stash,small,tok[:,None,:])

HALF=16; DOCS=4; GAP=16
def spread(dst, get, bounds, length, step):
    total=length+GAP*(DOCS+1)
    ids=lax.broadcasted_iota(jnp.int32,(step,128),0)
    for p0 in range(0,total,step):
        size=min(step,total-p0)
        acc=None
        for d in range(DOCS):
            s0=p0-GAP*(d+1)
            lo=max(s0,0); hi=min(s0+size,length)
            if hi<=lo: continue
            row=ids[:hi-lo]+lo
            inside=(row>=bounds[d])&(row<bounds[d+1])
            part=jnp.where(inside,get(lo,hi-lo),0.0)
            pads=[]
            if lo>s0: pads.append(jnp.zeros((lo-s0,128),F32))
            pads.append(part)
            if s0+size>hi: pads.append(jnp.zeros((s0+size-hi,128),F32))
            part=jnp.concatenate(pads,0) if len(pads)>1 else part
            acc=part if acc is None else acc+part
        if acc is None: acc=jnp.zeros((size,128),F32)
        dst[HALF+p0:HALF+p0+size,:]=acc
def collect(src, bounds, lo, size):
    row=lax.broadcasted_iota(jnp.int32,(size,128),0)+lo
    acc=None
    for d in range(DOCS):
        part=src[lo+GAP*(d+1):lo+GAP*(d+1)+size,:]
        acc=part if acc is None else jnp.where(row>=bounds[d],part,acc)
    return acc
BLOCK=64
def taps(ref, base, weight, sign):
    acc=None
    for r in range(8):
        win=ref[pl.ds(base+r,BLOCK+32),:] if r==0 else ref[pl.ds(base+r,BLOCK+24),:]
        for a in range(5 if r==0 else 4):
            o=8*a+r
            t=weight(o if sign>0 else 2*HALF-o)*win[8*a:8*a+BLOCK]
            acc=t if acc is None else acc+t
    return acc

def conv_fwd_kernel(bounds_ref, x_ref, wv_ref, w_ref, v_ref, out_ref, pad_ref, res_ref):
    b=pl.program_id(0)
    bounds=[bounds_ref[b,d] for d in range(DOCS+1)]
    length=v_ref.shape[1]; total=length+GAP*(DOCS+1)
    pad_ref[0:HALF,:]=jnp.zeros((HALF,128),F32); pad_ref[HALF+total:,:]=jnp.zeros((pad_ref.shape[0]-HALF-total,128),F32)
    for lo in range(0,length,256):
        v_ref[0,lo:lo+256,:]=nt(x_ref[0,lo:lo+256,:],wv_ref[...])+w_ref[KW+1:KW+2,:]
    spread(pad_ref, lambda lo,n: v_ref[0,lo:lo+n,:], bounds, length, BLOCK)
    def block(i,c):
        base=pl.multiple_of(i*BLOCK,BLOCK)
        res_ref[pl.ds(base,BLOCK),:]=taps(pad_ref, base, lambda s: w_ref[s:s+1,:], 1)
        return c
    lax.fori_loop(0,-(-total//BLOCK),block,0)
    for lo in range(0,length,BLOCK):
        out_ref[0,lo:lo+BLOCK,:]=collect(res_ref,bounds,lo,BLOCK)
def padded_rows(length):
    total=length+GAP*(DOCS+1)
    return -(-total//BLOCK)*BLOCK

def conv_fwd(bounds, x, w_v, w):
    B,L,D=x.shape
    rows=padded_rows(L)
    slab=pl.BlockSpec((1,L,128),lambda b,c,_:(b,0,c)); big=jax.ShapeDtypeStruct((B,L,D),F32)
    return pl.pallas_call(conv_fwd_kernel,grid_spec=pltpu.PrefetchScalarGridSpec(num_scalar_prefetch=1,grid=(B,D//128),
        in_specs=[pl.BlockSpec((1,L,D),lambda b,c,_:(b,0,0)),pl.BlockSpec((128,D),lambda b,c,_:(c,0)),
            pl.BlockSpec((SMALL,128),lambda b,c,_:(0,c))],
        out_specs=[slab,slab],
        scratch_shapes=[pltpu.VMEM((rows+2*HALF+8,128),F32),pltpu.VMEM((rows,128),F32)]),
        out_shape=[big,big],
        compiler_params=pltpu.CompilerParams(vmem_limit_bytes=60*2**20))(bounds,x,w_v,w)
def conv_bwd_kernel(bounds_ref, v_ref, al_ref, wo_ref, w_ref, x_ref, att_ref, more_ref, *refs):
    dv_ref, gv_ref, vpad_ref, gpad_ref, res_ref, acc_ref, g_ref, sum_ref = refs[-8:]
    b=pl.program_id(1)
    bounds=[bounds_ref[b,d] for d in range(DOCS+1)]
    length=v_ref.shape[1]; total=length+GAP*(DOCS+1)
    for lo in range(0,length,256):
        g_ref[lo:lo+256,:]=nn(al_ref[0,lo:lo+256,:],wo_ref[...])
    for ref in (vpad_ref,gpad_ref):
        ref[0:HALF,:]=jnp.zeros((HALF,128),F32)
        ref[HALF+total:,:]=jnp.zeros((ref.shape[0]-HALF-total,128),F32)
    spread(vpad_ref, lambda lo,n: v_ref[0,lo:lo+n,:], bounds, length, BLOCK)
    spread(gpad_ref, lambda lo,n: g_ref[lo:lo+n,:], bounds, length, BLOCK)
    @pl.when(b==0)
    def _():
        acc_ref[...]=jnp.zeros_like(acc_ref); gv_ref[...]=jnp.zeros_like(gv_ref); sum_ref[...]=jnp.zeros_like(sum_ref)
    def block(i,c):
        base=pl.multiple_of(i*BLOCK,BLOCK)
        here=vpad_ref[pl.ds(base+HALF,BLOCK),:]
        acc=None
        for r in range(8):
            n=5 if r==0 else 4
            win=gpad_ref[pl.ds(base+r,BLOCK+8*(n-1)),:]
            for a in range(n):
                s=2*HALF-(8*a+r)
                x=win[8*a:8*a+BLOCK]
                t=w_ref[s:s+1,:]*x
                acc=t if acc is None else acc+t
                p=(here*x).reshape(BLOCK//8,8,128)
                acc_ref[s]+=jnp.sum(p,axis=0)
        res_ref[pl.ds(base,BLOCK),:]=acc
        return c
    lax.fori_loop(0,-(-total//BLOCK),block,0)
    for lo in range(0,length,BLOCK*2):
        part=collect(res_ref,bounds,lo,BLOCK*2).T+att_ref[0,:,lo:lo+BLOCK*2]
        dv_ref[0,:,lo:lo+BLOCK*2]=part.astype(BF)
    dv=dv_ref[0]; depth=x_ref.shape[2]
    gv_ref[:,:depth]+=nn(dv,x_ref[0])
    sum_ref[...]+=jnp.sum(dv.astype(F32),axis=1,keepdims=True)
    @pl.when(b==pl.num_programs(1)-1)
    def _():
        rows=[jnp.sum(acc_ref[s],axis=0,keepdims=True) for s in range(KW)]
        side=jnp.concatenate(rows+[jnp.zeros((128-KW,128),F32)],axis=0).T
        lane=lax.broadcasted_iota(jnp.int32,(128,128),1)
        gv_ref[:,depth:]=more_ref[...]+side+jnp.where(lane==KW,sum_ref[:,:1],0.0)
def conv_bwd(bounds, v, al, w_o, w, x, att, more, before, slabs, at):
    B,L,D=v.shape
    rows=padded_rows(L)
    sd=jax.ShapeDtypeStruct
    seq=pl.BlockSpec((1,L,D),lambda c,b,_:(b,0,0))
    feats=pl.BlockSpec((1,128,L),lambda c,b,_:(b,at+c,0))
    alias={9:0,10:1} if before else {}
    return pl.pallas_call(conv_bwd_kernel,grid_spec=pltpu.PrefetchScalarGridSpec(num_scalar_prefetch=1,grid=(slabs,B),
        in_specs=[pl.BlockSpec((1,L,128),lambda c,b,_:(b,0,at+c)),seq,
            pl.BlockSpec((D,128),lambda c,b,_:(0,at+c)),pl.BlockSpec((SMALL,128),lambda c,b,_:(0,at+c)),
            seq,feats,pl.BlockSpec((128,128),lambda c,b,_:(at+c,0))]+[pl.BlockSpec(memory_space=pl.ANY)]*len(before),
        out_specs=[feats,pl.BlockSpec((128,D+128),lambda c,b,_:(at+c,0))],
        scratch_shapes=[pltpu.VMEM((rows+2*HALF+8,128),F32)]*2+[pltpu.VMEM((rows,128),F32),pltpu.VMEM((KW,8,128),F32),
            pltpu.VMEM((L,128),F32),pltpu.VMEM((128,128),F32)]),
        out_shape=[sd((B,D,L),BF),sd((D,D+128),F32)],input_output_aliases={i-1:o for i,o in alias.items()},
        compiler_params=pltpu.CompilerParams(vmem_limit_bytes=60*2**20))(bounds,v,al,w_o,w,x,att,more,*before)

def gelu_parts(x):
    size=jnp.abs(x)
    density=jnp.exp(-0.5*x*x)*0.3989422804014327
    t=1.0/(1.0+0.2316419*size)
    tail=density*(t*(0.319381530+t*(-0.356563782+t*(1.781477937+t*(-1.821255978+t*1.330274429)))))
    dist=jnp.where(x<0.0,tail,1.0-tail)
    return dist, x*density
def norm(v):
    mean=jnp.mean(v,axis=-1,keepdims=True); c=v-mean
    r=lax.rsqrt(jnp.mean(c*c,axis=-1,keepdims=True)+1e-5)
    return c*r, r
def norm_back(up,n,r,g):
    e=up*g
    return r*(e-jnp.mean(e,axis=-1,keepdims=True)-n*jnp.mean(e*n,axis=-1,keepdims=True))
def ffn_kernel(chunks, ctx_ref,x_ref,cot_ref,wo_ref,wu_ref,wd_ref,vec_ref,bu_ref,
               out_ref,normed_ref,hidden_ref,down_ref,up_ref,one_ref,att_ref,sums_ref,sumu_ref,slope_ref):
    width=wu_ref.shape[0]//chunks
    @pl.when(pl.program_id(0)==0)
    def _():
        sums_ref[...]=jnp.zeros_like(sums_ref); sumu_ref[...]=jnp.zeros_like(sumu_ref)
    v=lambda i: vec_ref[i:i+1,:]
    b_o,g1,s1,b_d,g2,s2=[v(KW+i) for i in range(2,8)]
    n1,r1=norm(x_ref[...].astype(F32)+(nt(ctx_ref[...],wo_ref[...])+b_o))
    normed=n1*g1+s1
    low=normed.astype(BF); normed_ref[...]=low
    down=None
    for k in range(chunks):
        part=slice(k*width,(k+1)*width)
        pre=nt(low,wu_ref[part,:])+bu_ref[:,part]
        dist,slope=gelu_parts(pre)
        slope_ref[:,part]=dist+slope
        hid=(pre*dist).astype(BF); hidden_ref[:,part]=hid
        add=nt(hid,wd_ref[k]); down=add if down is None else down+add
    n2,r2=norm(normed+(down+b_d))
    out_ref[...]=(n2*g2+s2).astype(BF)
    cot=cot_ref[...].astype(F32)
    g_two=norm_back(cot,n2,r2,g2)
    low2=g_two.astype(BF); down_ref[...]=low2
    back=g_two
    for k in range(chunks):
        part=slice(k*width,(k+1)*width)
        hg=nn(low2,wd_ref[k])
        upl=(hg*slope_ref[:,part]).astype(BF); up_ref[:,part]=upl
        sumu_ref[:,part]+=jnp.sum(upl.astype(F32),axis=0,keepdims=True)
        back=back+nn(upl,wu_ref[part,:])
    g_one=norm_back(back,n1,r1,g1)
    one_ref[...]=g_one
    al=g_one.astype(BF); att_ref[...]=al
    s=lambda a: jnp.sum(a,axis=0,keepdims=True)
    sums_ref[...]+=jnp.concatenate([s(al.astype(F32)),s(back*n1),s(back),s(low2.astype(F32)),s(cot*n2),s(cot),jnp.zeros((2,n1.shape[1]),F32)],axis=0)
def ffn(ctx,x,cot,wo,wu,wd,vec,bu,block=512):
    chunks=wd.shape[0]
    T,D=x.shape; F=wu.shape[0]
    row=lambda w: pl.BlockSpec((block,w),lambda i:(i,0))
    full=lambda a: pl.BlockSpec(a.shape,lambda i:(0,)*a.ndim,pipeline_mode=pl.Buffered(1))
    keep=lambda r,w: pl.BlockSpec((r,w),lambda i:(0,0))
    sd=jax.ShapeDtypeStruct
    return pl.pallas_call(functools.partial(ffn_kernel,chunks),grid=(T//block,),
        in_specs=[row(D),row(D),row(D),full(wo),full(wu),full(wd),pl.BlockSpec((SMALL,D),lambda i:(0,0)),full(bu)],
        out_specs=[row(D),row(D),row(F),row(D),row(F),row(D),row(D),keep(8,D),keep(1,F)],
        out_shape=[sd((T,D),BF),sd((T,D),BF),sd((T,F),BF),sd((T,D),BF),sd((T,F),BF),sd((T,D),F32),sd((T,D),BF),sd((8,D),F32),sd((1,F),F32)],
        scratch_shapes=[pltpu.VMEM((block,F),F32)],
        compiler_params=pltpu.CompilerParams(vmem_limit_bytes=60*2**20,dimension_semantics=("arbitrary",)),
    )(ctx,x,cot,wo,wu,wd,vec,bu)


def across_rows(left_side, right_side):
    return lax.dot_general(left_side, right_side, (((0,), (0,)), ((), ())), preferred_element_type=F32)


def weight_kernel(own, up_ref, normed_ref, hidden_ref, down_ref, att_ref, ctx_ref, out_ref, acc_ref):
    depth=normed_ref.shape[1]; k=pl.program_id(1)
    wide_rows=up_ref.shape[1]; rows=down_ref.shape[1]; parts=hidden_ref.shape[1]//depth
    @pl.when(k==0)
    def _(): acc_ref[...]=jnp.zeros_like(acc_ref)
    for lo in range(0,wide_rows,rows):
        acc_ref[lo:lo+rows]+=across_rows(up_ref[:,lo:lo+rows],normed_ref[...])
    for i in range(parts):
        at=wide_rows+i*rows
        acc_ref[at:at+rows]+=across_rows(down_ref[...],hidden_ref[:,i*depth:(i+1)*depth])
    at=wide_rows+parts*rows
    acc_ref[at:at+rows]+=across_rows(att_ref[...],ctx_ref[...])
    @pl.when(k==pl.num_programs(1)-1)
    def _():
        many=rows//own; lines=wide_rows//many
        out_ref[:,:lines]=acc_ref[:wide_rows].reshape(many,lines,depth).astype(BF)
        narrow=[acc_ref[wide_rows+i*rows:wide_rows+(i+1)*rows].reshape(many,own,depth) for i in range(parts+1)]
        narrow.append(jnp.zeros((many,out_ref.shape[1]-lines-(parts+1)*own,depth),F32))
        out_ref[:,lines:]=jnp.concatenate(narrow,axis=1).astype(BF)
def weight_grads(own, up, normed, hidden, down, att, ctx):
    T,D=normed.shape; F=up.shape[1]; halves=2; many=D//own//halves; block=512
    R=-(-(F//D*2+1)*own//16)*16
    if own%8:
        by=lambda a: a.reshape(D//own,-1,D)
        pieces=[by(across_rows(up,normed))]+[by(across_rows(down,hidden[:,i*D:(i+1)*D])) for i in range(F//D)]
        pieces.append(by(across_rows(att,ctx)))
        pieces.append(jnp.zeros((D//own,R-(F//D*2+1)*own,D),F32))
        return jnp.concatenate(pieces,axis=1).astype(BF)
    col=lambda w: pl.BlockSpec((block,w),lambda h,k:(k,h)); row=lambda w: pl.BlockSpec((block,w),lambda h,k:(k,0))
    return pl.pallas_call(functools.partial(weight_kernel,own),grid=(halves,T//block),
        in_specs=[col(F//halves),row(D),row(F),col(D//halves),col(D//halves),row(D)],
        out_specs=pl.BlockSpec((many,R,D),lambda h,k:(h,0,0)),
        out_shape=jax.ShapeDtypeStruct((D//own,R,D),BF),
        scratch_shapes=[pltpu.VMEM((many*own*(F//D*2+1),D),F32)],
        compiler_params=pltpu.CompilerParams(vmem_limit_bytes=60*2**20))(up,normed,hidden,down,att,ctx)


def digits():
    found = []
    for axis in ("wide", "narrow"):
        stride = lax.axis_size(axis) // 2
        while stride >= 1:
            found.append((axis, stride))
            stride //= 2
    return found


def link_order(number):
    count = len(digits())
    if lax.axis_size("wide") == 8 and lax.axis_size("narrow") == 4:
        return [(4, 2, 3, 1, 0), (4, 3, 1, 2, 0), (4, 1, 2, 3, 0)][number]
    return tuple(range(count - 1, -1, -1))


def exchange(values, axis, stride):
    return lax.ppermute(values, axis, [(i, i ^ stride) for i in range(lax.axis_size(axis))])


def digit_of(axis, stride):
    return (lax.axis_index(axis) // stride) % 2


def gather_rows(shard, number, passed=None):
    places = digits()
    held = shard.reshape((1,) * len(places) + shard.shape)
    for dim in link_order(number)[::-1]:
        if passed is not None:
            passed.append(held)
        mine = digit_of(*places[dim])
        got = exchange(held, *places[dim])
        first = jnp.where(mine == 0, held, got)
        second = jnp.where(mine == 0, got, held)
        held = jnp.concatenate([first, second], dim)
    return held.reshape((-1,) + shard.shape)


def scatter_start(whole, own):
    return whole.reshape(whole.shape[:-2] + (2,) * len(digits()) + (own, whole.shape[-1]))


def scatter_step(held, number, step):
    places = digits()
    dim = link_order(number)[step] + held.ndim - 2 - len(places)
    place = places[link_order(number)[step]]
    mine = digit_of(*place)
    keep = lax.dynamic_slice_in_dim(held, mine, 1, dim).astype(F32)
    send = lax.dynamic_slice_in_dim(held, 1 - mine, 1, dim).astype(BF)
    return keep + exchange(send, *place).astype(F32)


def scatter_rest(held, number, step):
    for later in range(step, len(digits())):
        held = scatter_step(held, number, later)
    return held.reshape(held.shape[: held.ndim - 2 - len(digits())] + held.shape[-2:])


def shards(
    inputs,
    tok_landmark,
    landmark_doc,
    w_query,
    b_query,
    w_key,
    w_value,
    b_value,
    conv_weight,
    w_out,
    b_out,
    gain_one,
    shift_one,
    w_up,
    b_up,
    w_down,
    b_down,
    gain_two,
    shift_two,
    cotangent,
):
    batch_rows, sequence_length, feature_width = inputs.shape
    group_count = lax.axis_size("wide") * lax.axis_size("narrow")
    own = feature_width // group_count
    tokens = batch_rows * sequence_length
    lines = b_up.shape[0] // own
    vectors = (b_query, b_value, b_out, gain_one, shift_one, b_down, gain_two, shift_two)
    small = jnp.concatenate(
        [conv_weight] + [vector[None] for vector in vectors] + [b_up.reshape(own, lines).T]
    )
    small = jnp.pad(small.T, ((0, 0), (0, 128 - small.shape[0])))
    passed = []
    w_q = gather_rows(w_query.T, 1).reshape(feature_width, feature_width)
    w_k = gather_rows(w_key.T, 2).reshape(feature_width, feature_width)
    gathered_v = gather_rows(jnp.concatenate([w_value.T, small], axis=1), 0, passed)
    gathered_v = gathered_v.reshape(feature_width, feature_width + 128)
    w_v = gathered_v[:, :feature_width]
    small = gathered_v[:, feature_width:]
    b_u = small[:, KW + 8 : KW + 8 + lines].reshape(1, -1).astype(F32)
    small = small.astype(F32).T
    ff_count = w_down.shape[0] // feature_width
    shard = jnp.concatenate(
        [w_out.T, w_up.T] + [w_down[i * feature_width : (i + 1) * feature_width].T for i in range(ff_count)]
    )
    shard, _ = lax.optimization_barrier((shard, passed[2]))
    gathered = lax.all_gather(shard, ("wide", "narrow"), axis=0)
    w_o = gathered[:, :own].reshape(feature_width, feature_width)
    w_u = gathered[:, own : own * (1 + lines)].reshape(-1, feature_width)
    w_d = jnp.moveaxis(
        gathered[:, own * (1 + lines) :].reshape(group_count, ff_count, own, feature_width), 0, 1
    ).reshape(ff_count, feature_width, feature_width)
    member = tok_landmark[:, None, :] == jnp.arange(LM)[None, :, None]
    means = jnp.einsum("bjt,bti->bji", member.astype(BF), inputs, preferred_element_type=F32)
    means = means / jnp.sum(member, axis=2)[..., None].astype(F32)
    doc = jnp.sum(jnp.where(member, landmark_doc[:, :, None], 0), axis=1)
    bounds = jnp.sum(doc[:, None, :] < jnp.arange(DOCS + 1)[None, :, None], axis=2).astype(jnp.int32)
    rows_low = inputs.reshape(tokens, feature_width)
    value_rows, conv_part = conv_fwd(bounds, inputs, w_v, small)
    q, k, v, k1, k3, inv, stash, landmarks, context = att_fwd(
        inputs, means, w_q, w_k, w_v, small, tok_landmark, landmark_doc, conv_part
    )
    context = context.reshape(tokens, feature_width)
    layer_out, normed, hidden, down_low, up_low, grad_one, att_low, sums, sums_up = ffn(
        context, rows_low, cotangent.reshape(tokens, feature_width), w_o, w_u, w_d, small, b_u
    )
    grads = weight_grads(own, up_low, normed, hidden, down_low, att_low, context)
    share = lax.psum_scatter(grads, ("wide", "narrow"), scatter_dimension=0, tiled=True)[0].astype(F32)
    w_plain = w_o.T
    att_low = att_low.reshape(inputs.shape)
    dq, dk, dv, grad_qk, sum_q = att_bwd(
        inputs, att_low, w_plain, q, k, v, k1, k3, inv, stash, landmarks, tok_landmark
    )
    more = jnp.concatenate(
        [
            jnp.zeros((feature_width, KW + 1), F32),
            sum_q,
            sums[:6].T,
            sums_up.reshape(feature_width, lines),
            jnp.zeros((feature_width, 128 - KW - 8 - lines), F32),
        ],
        axis=1,
    )
    moving = scatter_step(scatter_start(grad_qk, own), 1, 0)
    calls, before = 3, ()
    slabs = feature_width // 128 // calls
    for call in range(calls):
        moved = scatter_step(moving, 1, 1 + call)
        before = conv_bwd(
            bounds, value_rows, att_low, w_o, small, inputs, dv, more, before, slabs, call * slabs
        )
        before, att_low, moving = lax.optimization_barrier((tuple(before), att_low, moved))
    dv, grad_v = before
    share_qk = scatter_rest(moving, 1, 1 + calls)
    share_v = scatter_rest(scatter_start(grad_v, own), 0, 0)
    input_grad = grad_one.reshape(inputs.shape)
    for grad, weight in zip((dq, dk, dv), (w_q, w_k, w_v)):
        input_grad = input_grad + jnp.einsum("bot,oi->bti", grad, weight, preferred_element_type=F32)
    late = share_v[:, feature_width:]
    share_down = share[own * lines : 2 * own * lines].reshape(ff_count, own, feature_width)
    share_out = share[2 * own * lines : 2 * own * lines + own]
    return (
        layer_out.reshape(inputs.shape),
        input_grad,
        share_qk[0].T,
        late[:, KW + 1],
        share_qk[1].T,
        share_v[:, :feature_width].T,
        late[:, KW],
        late[:, :KW].T,
        share_out.T,
        late[:, KW + 2],
        late[:, KW + 3],
        late[:, KW + 4],
        share[: own * lines].T,
        late[:, KW + 8 : KW + 8 + lines].reshape(-1),
        jnp.moveaxis(share_down, 1, 2).reshape(-1, own),
        late[:, KW + 5],
        late[:, KW + 6],
        late[:, KW + 7],
    )


def solution(mesh):
    return jax.shard_map(
        shards,
        mesh=mesh,
        in_specs=(
            P(("wide", "narrow"), None, None),
            P(("wide", "narrow"), None),
            P(("wide", "narrow"), None),
            P(None, ("wide", "narrow")),
            P(("wide", "narrow")),
            P(None, ("wide", "narrow")),
            P(None, ("wide", "narrow")),
            P(("wide", "narrow")),
            P(None, ("wide", "narrow")),
            P(None, ("wide", "narrow")),
            P(("wide", "narrow")),
            P(("wide", "narrow")),
            P(("wide", "narrow")),
            P(None, ("wide", "narrow")),
            P(("wide", "narrow")),
            P(None, ("wide", "narrow")),
            P(("wide", "narrow")),
            P(("wide", "narrow")),
            P(("wide", "narrow")),
            P(("wide", "narrow"), None, None),
        ),
        out_specs=(
            P(("wide", "narrow"), None, None),
            P(("wide", "narrow"), None, None),
            P(None, ("wide", "narrow")),
            P(("wide", "narrow")),
            P(None, ("wide", "narrow")),
            P(None, ("wide", "narrow")),
            P(("wide", "narrow")),
            P(None, ("wide", "narrow")),
            P(None, ("wide", "narrow")),
            P(("wide", "narrow")),
            P(("wide", "narrow")),
            P(("wide", "narrow")),
            P(None, ("wide", "narrow")),
            P(("wide", "narrow")),
            P(None, ("wide", "narrow")),
            P(("wide", "narrow")),
            P(("wide", "narrow")),
            P(("wide", "narrow")),
        ),
        check_vma=False,
    )
```

```python
import functools

import jax
import jax.numpy as jnp
from jax import lax
from jax.experimental import pallas as pl
from jax.experimental.pallas import tpu as pltpu
from jax.sharding import PartitionSpec as P

BF = jnp.bfloat16
F32 = jnp.float32
HW=64; LM=64; NEWTON=6; GH=12; GW=GH*HW
CHUNK=256
KW=33
SMALL=48
def nt(a,b): return lax.dot_general(a,b,(((1,),(1,)),((),())),preferred_element_type=F32)
def nn(a,b): return lax.dot_general(a,b,(((1,),(0,)),((),())),preferred_element_type=F32)
def split(a):
    hi=a.astype(BF); return hi,(a-hi.astype(F32)).astype(BF)
def wide(a):
    hi,lo=split(a); return jnp.concatenate([hi,hi,lo],axis=1)
def tall(b):
    hi,lo=split(b); return jnp.concatenate([hi,lo,hi],axis=0)
def mm3(a,b): return nn(wide(a),tall(b))
def eye(c):
    row=lax.broadcasted_iota(jnp.int32,(LM,2*LM),0); col=lax.broadcasted_iota(jnp.int32,(LM,2*LM),1)
    return jnp.where((row==col)|(row+LM==col),c,0.0)
def beside(a):
    return [jnp.concatenate([a[i],a[i+1]],axis=1) for i in range(0,len(a),2)]
def blocks(b):
    lane=lax.broadcasted_iota(jnp.int32,(1,2*LM),1)
    first=jnp.where(lane<LM,1.0,0.0).astype(BF); second=jnp.where(lane<LM,0.0,1.0).astype(BF)
    hi,lo=split(b)
    return jnp.concatenate([hi*first,hi*second,lo*first,lo*second,hi*first,hi*second],axis=0)
def mmb(a,b): return nn(wide(a),blocks(b))
def weave(first, second):
    done=0
    for i,step in enumerate(first):
        step()
        upto=(i+1)*len(second)//len(first)
        for other in second[done:upto]: other()
        done=upto
def att_fwd_kernel(x_ref,mean_ref,wq_ref,wk_ref,wv_ref,vec_ref,tok_ref,ldc_ref,ldr_ref,conv_ref,
               q_ref,k_ref,v_ref,k1_ref,k3_ref,inv_ref,stash_ref,small_ref,ctx_ref,
               qlo_ref,klo_ref,score_ref,bias_ref):
    T=x_ref.shape[1]
    heads=range(GH); chunks=[slice(c,c+CHUNK) for c in range(0,T,CHUNK)]
    rows=[slice(h*HW,(h+1)*HW) for h in heads]
    scale=HW**-0.25
    bq=vec_ref[KW:KW+1,:].T; bv=vec_ref[KW+1:KW+2,:].T
    ldc=ldc_ref[0]
    for cs in chunks:
        member=lax.broadcasted_iota(jnp.int32,(LM,CHUNK),0)==tok_ref[0,:,cs]
        doc=jnp.sum(jnp.where(member,ldc,0),axis=0,keepdims=True)
        bias_ref[:,cs]=jnp.where(doc==ldc,0.0,-1e30)
    mean=jnp.concatenate(split(mean_ref[0]),axis=0)
    def land(w_ref):
        both=nt(w_ref[...],mean)
        return both[:,:LM]+both[:,LM:]
    lqt=(land(wq_ref)+bq)*scale; lkt=land(wk_ref)*scale
    lq=[lqt[r].T for r in rows]; lk=[lkt[r].T for r in rows]
    lqw=[wide(a) for a in lq]; lkw=[wide(a) for a in lk]
    allow2=ldc==ldr_ref[0]
    k2=[];zt=[]
    for h in heads:
        sc=jnp.where(allow2,nn(lqw[h],tall(lkt[rows[h]])),-1e30)
        e=jnp.exp(sc-jnp.max(sc,axis=1,keepdims=True))
        k2.append(e/jnp.sum(e,axis=1,keepdims=True))
        zt.append(k2[h]*(1.0/jnp.sum(k2[h]*k2[h])))
    pairs=range(GH//2)
    state={"zt":beside(zt)}
    k2tb=[blocks(a) for a in beside([a.T for a in k2])]
    def newton(n):
        def one():
            state["p"]=[nn(wide(state["zt"][i]),k2tb[i]) for i in pairs]
            state["pw"]=[wide(a) for a in state["p"]]
        def two(): state["b"]=[eye(15.0)-nn(state["pw"][i],blocks(eye(7.0)-state["p"][i])) for i in pairs]
        def three(): state["c"]=[eye(13.0)-nn(state["pw"][i],blocks(state["b"][i])) for i in pairs]
        def four():
            for i in pairs:
                for place,key in enumerate(("p","b","c","zt")): stash_ref[0,i,4*n+place]=state[key][i]
            state["zt"]=[0.25*mmb(state["c"][i],state["zt"][i]) for i in pairs]
        return [one,two,three,four]
    chain=[step for n in range(NEWTON) for step in newton(n)]
    side=[]
    def project(cs):
        x=x_ref[0,cs,:]
        def q():
            a=(nt(wq_ref[...],x)+bq)*scale
            hi,lo=split(a); q_ref[0,:,cs]=hi; qlo_ref[:,cs]=lo
        def k():
            a=nt(wk_ref[...],x)*scale
            hi,lo=split(a); k_ref[0,:,cs]=hi; klo_ref[:,cs]=lo
        def v(): v_ref[0,:,cs]=(nt(wv_ref[...],x)+bv).astype(BF)
        return [q,k,v]
    tops=[None]*GH; sums=[None]*GH; r=[None]*GH
    def lanes(a): return [a[:,i:i+128] for i in range(0,CHUNK,128)]
    def first(h,cs):
        def go():
            hi=q_ref[0,rows[h],cs]
            s=nn(lkw[h],jnp.concatenate([hi,qlo_ref[rows[h],cs],hi],axis=0))+bias_ref[:,cs]
            e=jnp.exp(s-jnp.max(s,axis=0,keepdims=True))
            e=e.astype(BF); k1_ref[0,rows[h],cs]=e
            inv_ref[0,0,h:h+1,cs]=1.0/jnp.sum(e.astype(F32),axis=0,keepdims=True)
        return go
    def third(h,cs):
        def go():
            hi=k_ref[0,rows[h],cs]
            s=nn(lqw[h],jnp.concatenate([hi,klo_ref[rows[h],cs],hi],axis=0))+bias_ref[:,cs]
            score_ref[rows[h],cs]=s
            for a in lanes(s): tops[h]=a if tops[h] is None else jnp.maximum(tops[h],a)
        return go
    def raised(h,cs):
        def go():
            if cs.start==0: tops[h]=jnp.max(tops[h],axis=1,keepdims=True)
            e=jnp.exp(score_ref[rows[h],cs]-tops[h])
            e=e.astype(BF); k3_ref[0,rows[h],cs]=e
            for a in lanes(e.astype(F32)): sums[h]=a if sums[h] is None else sums[h]+a
        return go
    def gathered(h):
        def go():
            sums[h]=1.0/jnp.sum(sums[h],axis=1,keepdims=True)
            r[h]=nt(k3_ref[0,rows[h]],v_ref[0,rows[h]])*sums[h]
        return go
    for cs in chunks: side+=project(cs)
    for h in heads:
        side+=[third(h,cs) for cs in chunks]
        side+=[raised(h,cs) for cs in chunks]+[gathered(h)]
        side+=[first(h,cs) for cs in chunks]
    weave(chain,side)
    uts=[]
    for h in heads:
        zt=state["zt"][h//2][:,h%2*LM:(h%2+1)*LM]
        u=mm3(zt.T,r[h])
        small_ref[0,h,0]=jnp.concatenate([lq[h],lk[h]],axis=1)
        small_ref[0,h,1]=jnp.concatenate([k2[h],zt],axis=1)
        small_ref[0,h,2]=jnp.concatenate([r[h],u],axis=1)
        small_ref[0,h,3]=jnp.broadcast_to(sums[h],(LM,128))
        uts.append(u.T.astype(BF))
    for cs in chunks:
        mixed=jnp.concatenate([nn(uts[h],k1_ref[0,rows[h],cs])*inv_ref[0,0,h:h+1,cs] for h in heads],axis=0)
        ctx_ref[0,cs,:]=(mixed.T+conv_ref[0,cs,:]).astype(BF)
def att_specs(D,T):
    seq=lambda s: pl.BlockSpec((1,)+s,lambda g,b:(b,)+(0,)*len(s))
    wsp=pl.BlockSpec((GW,D),lambda g,b:(g,0)); bsp=pl.BlockSpec((GW,1),lambda g,b:(g,0))
    rows=pl.BlockSpec((1,GW,T),lambda g,b:(b,g,0)); cols=pl.BlockSpec((1,T,GW),lambda g,b:(b,0,g))
    sq=lambda m,n: pl.BlockSpec((1,m,n,LM,2*LM),lambda g,b:(b,g,0,0,0))
    turned=pl.BlockSpec((1,1,-(-GH//8)*8,T),lambda g,b:(b,g,0,0))
    return seq,wsp,bsp,rows,cols,sq,turned
def att_fwd(x,mean,wq,wk,wv,vec,tok,ld,conv):
    B,T,D=x.shape; G=D//GW; H=D//HW
    seq,wsp,bsp,rows,cols,sq,turned=att_specs(D,T)
    sd=jax.ShapeDtypeStruct; big=sd((B,D,T),BF)
    return pl.pallas_call(att_fwd_kernel,grid=(G,B),
        in_specs=[seq((T,D)),seq((LM,D)),wsp,wsp,wsp,pl.BlockSpec((SMALL,GW),lambda g,b:(0,g)),seq((1,T)),seq((LM,1)),seq((1,LM)),cols],
        out_specs=[rows]*5+[turned,sq(GH//2,4*NEWTON),sq(GH,4),cols],
        out_shape=[big]*5+[sd((B,G,-(-GH//8)*8,T),F32),sd((B,H//2,4*NEWTON,LM,2*LM),F32),sd((B,H,4,LM,2*LM),F32),sd((B,T,D),BF)],
        scratch_shapes=[pltpu.VMEM((GW,T),BF)]*2+[pltpu.VMEM((GW,T),F32),pltpu.VMEM((LM,T),F32)],
        compiler_params=pltpu.CompilerParams(vmem_limit_bytes=60*2**20))(
            x,mean,wq,wk,wv,vec,tok[:,None,:],ld[:,:,None],ld[:,None,:],conv)
def att_bwd_kernel(x_ref,al_ref,wo_ref,q_ref,k_ref,v_ref,k1_ref,k3_ref,inv_ref,stash_ref,small_ref,tok_ref,
               dq_ref,dk_ref,dv_ref,gqk_ref,sq_ref,
               g_ref,ds1_ref,ds3_ref,hot_ref):
    T=x_ref.shape[1]
    heads=range(GH); chunks=[slice(c,c+CHUNK) for c in range(0,T,CHUNK)]
    rows=[slice(h*HW,(h+1)*HW) for h in heads]
    scale=HW**-0.25
    for cs in chunks:
        member=lax.broadcasted_iota(jnp.int32,(LM,CHUNK),0)==tok_ref[0,:,cs]
        hot_ref[:,cs]=jnp.where(member,1.0,0.0).astype(BF)
    per=1.0/nt(jnp.ones((8,T),BF),hot_ref[...])[0:1]
    left=lambda i: [small_ref[0,h,i,:,:LM] for h in heads]
    right=lambda i: [small_ref[0,h,i,:,LM:] for h in heads]
    lq,lk,k2,zt,r,u=left(0),right(0),left(1),right(1),left(2),right(2)
    inv=[small_ref[0,h,3,:,:LM] for h in heads]
    ub=[a.astype(BF) for a in u]
    def upstream(cs):
        def go():
            a=nt(wo_ref[...],al_ref[0,cs,:])
            for h in heads: g_ref[rows[h],cs]=(a[rows[h]]*inv_ref[0,0,h:h+1,cs]).astype(BF)
        return go
    def first(h,cs):
        def go():
            k1=k1_ref[0,rows[h],cs].astype(F32)
            t=k1*nn(ub[h],g_ref[rows[h],cs])
            ds1_ref[rows[h],cs]=(t-k1*(jnp.sum(t,axis=0,keepdims=True)*inv_ref[0,0,h:h+1,cs])).astype(BF)
        return go
    for cs in chunks: upstream(cs)()
    du=[nt(k1_ref[0,rows[h]],g_ref[rows[h],:]) for h in heads]
    dr=[mm3(zt[h],du[h]) for h in heads]
    state={"dz":beside([mm3(du[h],r[h].T) for h in heads]),"dk2":[None]*(GH//2)}
    drs=[(dr[h]*inv[h]) for h in heads]
    drb=[a.astype(BF) for a in drs]; drt=[a.T.astype(BF) for a in drs]
    delta=[jnp.sum(drb[h].astype(F32)*r[h],axis=1,keepdims=True) for h in heads]
    dlq=[None]*GH; dlk=[None]*GH
    def third(h,cs):
        def go():
            d=k3_ref[0,rows[h],cs].astype(F32)*(nn(drb[h],v_ref[0,rows[h],cs])-delta[h])
            ds3_ref[rows[h],cs]=d.astype(BF)
        return go
    def values(cs):
        def go():
            a=jnp.concatenate([nn(drt[h],k3_ref[0,rows[h],cs]) for h in heads],axis=0)
            dv_ref[0,:,cs]=a
        return go
    def to_lk(h):
        def go(): dlk[h]=nt(ds1_ref[rows[h],:],q_ref[0,rows[h]])
        return go
    def to_lq(h):
        def go(): dlq[h]=nt(ds3_ref[rows[h],:],k_ref[0,rows[h]])
        return go
    @pl.when(pl.program_id(1)==0)
    def _():
        for ref in (gqk_ref,sq_ref): ref[...]=jnp.zeros_like(ref)
    side=[]
    for h in heads: side+=[third(h,cs) for cs in chunks]+[to_lq(h)]+[first(h,cs) for cs in chunks]+[to_lk(h)]
    side+=[values(cs) for cs in chunks]
    pairs=range(GH//2)
    k2t=[a.T for a in k2]; k2tw=[wide(a) for a in beside(k2t)]
    def newton(n):
        def one():
            state["p"],state["b"],state["c"],state["zt"]=[[stash_ref[0,i,4*n+place] for i in pairs] for place in range(4)]
            state["gz"]=[0.25*d for d in state["dz"]]
            state["dc"]=[mmb(state["zt"][i],state["gz"][i]) for i in pairs]
            state["pw"]=[wide(m) for m in state["p"]]
        def two(): state["db"]=[nn(state["pw"][i],blocks(state["dc"][i])) for i in pairs]
        def three():
            da=[nn(state["pw"][i],blocks(state["db"][i])) for i in pairs]
            state["dp"]=[mmb(state["db"][i],eye(7.0)-state["p"][i])-mmb(state["dc"][i],state["b"][i])-da[i] for i in pairs]
        def four():
            for i in pairs:
                t=mmb(state["dp"][i],state["zt"][i])
                state["dk2"][i]=t if state["dk2"][i] is None else state["dk2"][i]+t
            state["dz"]=[mmb(state["gz"][i],state["c"][i])+nn(k2tw[i],blocks(state["dp"][i])) for i in pairs]
        return [one,two,three,four]
    chain=[step for n in reversed(range(NEWTON)) for step in newton(n)]
    weave(chain,side)
    lhq=[];lhk=[]
    for h in heads:
        half=slice(h%2*LM,(h%2+1)*LM)
        i2=1.0/jnp.sum(k2[h]*k2[h]); dz=state["dz"][h//2][:,half]
        d=state["dk2"][h//2][:,half]+i2*dz.T-k2[h]*(2.0*i2*i2*jnp.sum(dz*k2t[h]))
        d=k2[h]*(d-jnp.sum(k2[h]*d,axis=1,keepdims=True))
        dlqh=dlq[h]+mm3(d,lk[h]); dlkh=dlk[h]+mm3(d.T,lq[h])
        lhq.append(jnp.concatenate([lk[h].T,dlqh.T*per],axis=1).astype(BF))
        lhk.append(jnp.concatenate([lq[h].T,dlkh.T*per],axis=1).astype(BF))
    for cs in chunks:
        hot=hot_ref[:,cs]
        for lh,ds_ref,out_ref in ((lhq,ds1_ref,dq_ref),(lhk,ds3_ref,dk_ref)):
            for h in heads:
                a=nn(lh[h],jnp.concatenate([ds_ref[rows[h],cs],hot],axis=0))
                out_ref[0,rows[h],cs]=(a*scale).astype(BF)
    dq=dq_ref[0]
    gqk_ref[0]+=nn(dq,x_ref[0]); gqk_ref[1]+=nn(dk_ref[0],x_ref[0])
    sq_ref[...]+=jnp.sum(dq.astype(F32),axis=1,keepdims=True)
def att_bwd(x,al,wo,q,k,v,k1,k3,inv,stash,small,tok):
    B,T,D=x.shape; G=D//GW
    seq,wsp,bsp,rows,cols,sq,turned=att_specs(D,T)
    sd=jax.ShapeDtypeStruct; big=sd((B,D,T),BF)
    return pl.pallas_call(att_bwd_kernel,grid=(G,B),
        in_specs=[seq((T,D)),seq((T,D)),wsp]+[rows]*5+[turned,sq(GH//2,4*NEWTON),sq(GH,4),seq((1,T))],
        out_specs=[rows]*3+[pl.BlockSpec((2,GW,D),lambda g,b:(0,g,0)),bsp],
        out_shape=[big,big,sd((B,D,T),F32),sd((2,D,D),F32),sd((D,1),F32)],
        scratch_shapes=[pltpu.VMEM((GW,T),BF)]*3+[pltpu.VMEM((LM,T),BF)],
        compiler_params=pltpu.CompilerParams(vmem_limit_bytes=60*2**20))(
            x,al,wo,q,k,v,k1,k3,inv,stash,small,tok[:,None,:])

HALF=16; DOCS=4; GAP=16
def spread(dst, get, bounds, length, step):
    total=length+GAP*(DOCS+1)
    ids=lax.broadcasted_iota(jnp.int32,(step,128),0)
    for p0 in range(0,total,step):
        size=min(step,total-p0)
        acc=None
        for d in range(DOCS):
            s0=p0-GAP*(d+1)
            lo=max(s0,0); hi=min(s0+size,length)
            if hi<=lo: continue
            row=ids[:hi-lo]+lo
            inside=(row>=bounds[d])&(row<bounds[d+1])
            part=jnp.where(inside,get(lo,hi-lo),0.0)
            pads=[]
            if lo>s0: pads.append(jnp.zeros((lo-s0,128),F32))
            pads.append(part)
            if s0+size>hi: pads.append(jnp.zeros((s0+size-hi,128),F32))
            part=jnp.concatenate(pads,0) if len(pads)>1 else part
            acc=part if acc is None else acc+part
        if acc is None: acc=jnp.zeros((size,128),F32)
        dst[HALF+p0:HALF+p0+size,:]=acc
def collect(src, bounds, lo, size):
    row=lax.broadcasted_iota(jnp.int32,(size,128),0)+lo
    acc=None
    for d in range(DOCS):
        part=src[lo+GAP*(d+1):lo+GAP*(d+1)+size,:]
        acc=part if acc is None else jnp.where(row>=bounds[d],part,acc)
    return acc
BLOCK=64
TALL=128
WIDTH=256
SLABS=range(WIDTH//128)
def taps(ref, base, weight, sign):
    acc=None
    for r in range(8):
        win=ref[pl.ds(base+r,TALL+32),:] if r==0 else ref[pl.ds(base+r,TALL+24),:]
        for a in range(5 if r==0 else 4):
            o=8*a+r
            t=weight(o if sign>0 else 2*HALF-o)*win[8*a:8*a+TALL]
            acc=t if acc is None else acc+t
    return acc

def cut(h): return slice(h*128,(h+1)*128)
def conv_fwd_kernel(bounds_ref, x_ref, wv_ref, w_ref, v_ref, out_ref, pad_ref, res_ref):
    b=pl.program_id(0)
    bounds=[bounds_ref[b,d] for d in range(DOCS+1)]
    length=v_ref.shape[1]; total=length+GAP*(DOCS+1)
    for lo in range(0,length,256):
        v_ref[0,lo:lo+256,:]=nt(x_ref[0,lo:lo+256,:],wv_ref[...])+w_ref[KW+1:KW+2,:]
    for h in SLABS:
        pad_ref[h,0:HALF,:]=jnp.zeros((HALF,128),F32)
        pad_ref[h,HALF+total:,:]=jnp.zeros((pad_ref.shape[1]-HALF-total,128),F32)
        spread(pad_ref.at[h], lambda lo,n: v_ref[0,lo:lo+n,cut(h)], bounds, length, BLOCK)
    def block(i,c):
        base=pl.multiple_of(i*TALL,TALL)
        for h in SLABS:
            res_ref[h,pl.ds(base,TALL),:]=taps(pad_ref.at[h], base, lambda s: w_ref[s:s+1,cut(h)], 1)
        return c
    lax.fori_loop(0,-(-total//TALL),block,0)
    for h in SLABS:
        for lo in range(0,length,BLOCK):
            out_ref[0,lo:lo+BLOCK,cut(h)]=collect(res_ref.at[h],bounds,lo,BLOCK)
def padded_rows(length):
    total=length+GAP*(DOCS+1)
    return -(-total//TALL)*TALL

def conv_fwd(bounds, x, w_v, w):
    B,L,D=x.shape
    rows=padded_rows(L)
    slab=pl.BlockSpec((1,L,WIDTH),lambda b,c,_:(b,0,c)); big=jax.ShapeDtypeStruct((B,L,D),F32)
    return pl.pallas_call(conv_fwd_kernel,grid_spec=pltpu.PrefetchScalarGridSpec(num_scalar_prefetch=1,grid=(B,D//WIDTH),
        in_specs=[pl.BlockSpec((1,L,D),lambda b,c,_:(b,0,0)),pl.BlockSpec((WIDTH,D),lambda b,c,_:(c,0)),
            pl.BlockSpec((SMALL,WIDTH),lambda b,c,_:(0,c))],
        out_specs=[slab,slab],
        scratch_shapes=[pltpu.VMEM((WIDTH//128,rows+2*HALF+8,128),F32),pltpu.VMEM((WIDTH//128,rows,128),F32)]),
        out_shape=[big,big],
        compiler_params=pltpu.CompilerParams(vmem_limit_bytes=60*2**20))(bounds,x,w_v,w)
def conv_bwd_kernel(bounds_ref, v_ref, al_ref, wo_ref, w_ref, x_ref, att_ref, q_ref, sums_ref, su_ref, *refs):
    dv_ref, gv_ref, vpad_ref, gpad_ref, res_ref, acc_ref, g_ref, sum_ref = refs[-8:]
    b=pl.program_id(1)
    bounds=[bounds_ref[b,d] for d in range(DOCS+1)]
    length=v_ref.shape[1]; total=length+GAP*(DOCS+1)
    for lo in range(0,length,256):
        g_ref[lo:lo+256,:]=nn(al_ref[0,lo:lo+256,:],wo_ref[...])
    for ref in (vpad_ref,gpad_ref):
        ref[0:HALF,:]=jnp.zeros((HALF,128),F32)
        ref[HALF+total:,:]=jnp.zeros((ref.shape[0]-HALF-total,128),F32)
    spread(vpad_ref, lambda lo,n: v_ref[0,lo:lo+n,:], bounds, length, BLOCK)
    spread(gpad_ref, lambda lo,n: g_ref[lo:lo+n,:], bounds, length, BLOCK)
    @pl.when(b==0)
    def _():
        acc_ref[...]=jnp.zeros_like(acc_ref); gv_ref[...]=jnp.zeros_like(gv_ref); sum_ref[...]=jnp.zeros_like(sum_ref)
    def block(i,c):
        base=pl.multiple_of(i*BLOCK,BLOCK)
        here=vpad_ref[pl.ds(base+HALF,BLOCK),:]
        acc=None
        for r in range(8):
            n=5 if r==0 else 4
            win=gpad_ref[pl.ds(base+r,BLOCK+8*(n-1)),:]
            for a in range(n):
                s=2*HALF-(8*a+r)
                x=win[8*a:8*a+BLOCK]
                t=w_ref[s:s+1,:]*x
                acc=t if acc is None else acc+t
                p=(here*x).reshape(BLOCK//8,8,128)
                acc_ref[s]+=jnp.sum(p,axis=0)
        res_ref[pl.ds(base,BLOCK),:]=acc
        return c
    lax.fori_loop(0,-(-total//BLOCK),block,0)
    for lo in range(0,length,BLOCK*2):
        part=collect(res_ref,bounds,lo,BLOCK*2).T+att_ref[0,:,lo:lo+BLOCK*2]
        dv_ref[0,:,lo:lo+BLOCK*2]=part.astype(BF)
    dv=dv_ref[0]; depth=x_ref.shape[2]
    gv_ref[:,:depth]+=nn(dv,x_ref[0])
    sum_ref[...]+=jnp.sum(dv.astype(F32),axis=1,keepdims=True)
    @pl.when(b==pl.num_programs(1)-1)
    def _():
        rows=[jnp.sum(acc_ref[s],axis=0,keepdims=True) for s in range(KW)]
        side=jnp.concatenate(rows+[jnp.zeros((128-KW,128),F32)],axis=0).T
        lane=lax.broadcasted_iota(jnp.int32,(128,128),1)
        lines=su_ref.shape[1]
        side=side+jnp.where(lane==KW,sum_ref[:,:1],0.0)+jnp.where(lane==KW+1,q_ref[...],0.0)
        early=sums_ref[...].T
        for i in range(6): side=side+jnp.where(lane==KW+2+i,early[:,i:i+1],0.0)
        for i in range(lines): side=side+jnp.where(lane==KW+8+i,su_ref[:,i:i+1],0.0)
        gv_ref[:,depth:]=side
def conv_bwd(bounds, v, al, w_o, w, x, att, more, before, slabs, at):
    B,L,D=v.shape
    rows=padded_rows(L)
    sd=jax.ShapeDtypeStruct
    seq=pl.BlockSpec((1,L,D),lambda c,b,_:(b,0,0))
    feats=pl.BlockSpec((1,128,L),lambda c,b,_:(b,at+c,0))
    alias={11:0,12:1} if before else {}
    return pl.pallas_call(conv_bwd_kernel,grid_spec=pltpu.PrefetchScalarGridSpec(num_scalar_prefetch=1,grid=(slabs,B),
        in_specs=[pl.BlockSpec((1,L,128),lambda c,b,_:(b,0,at+c)),seq,
            pl.BlockSpec((D,128),lambda c,b,_:(0,at+c)),pl.BlockSpec((SMALL,128),lambda c,b,_:(0,at+c)),
            seq,feats,pl.BlockSpec((128,1),lambda c,b,_:(at+c,0)),pl.BlockSpec((8,128),lambda c,b,_:(0,at+c)),
            pl.BlockSpec((128,more[2].shape[1]),lambda c,b,_:(at+c,0))]+[pl.BlockSpec(memory_space=pl.ANY)]*len(before),
        out_specs=[feats,pl.BlockSpec((128,D+128),lambda c,b,_:(at+c,0))],
        scratch_shapes=[pltpu.VMEM((rows+2*HALF+8,128),F32)]*2+[pltpu.VMEM((rows,128),F32),pltpu.VMEM((KW,8,128),F32),
            pltpu.VMEM((L,128),F32),pltpu.VMEM((128,128),F32)]),
        out_shape=[sd((B,D,L),BF),sd((D,D+128),F32)],input_output_aliases={i-1:o for i,o in alias.items()},
        compiler_params=pltpu.CompilerParams(vmem_limit_bytes=60*2**20))(bounds,v,al,w_o,w,x,att,*more,*before)

def gelu_parts(x):
    size=jnp.abs(x)
    density=jnp.exp(-0.5*x*x)*0.3989422804014327
    t=1.0/(1.0+0.2316419*size)
    tail=density*(t*(0.319381530+t*(-0.356563782+t*(1.781477937+t*(-1.821255978+t*1.330274429)))))
    dist=jnp.where(x<0.0,tail,1.0-tail)
    return dist, x*density
def norm(v):
    mean=jnp.mean(v,axis=-1,keepdims=True); c=v-mean
    r=lax.rsqrt(jnp.mean(c*c,axis=-1,keepdims=True)+1e-5)
    return c*r, r
def norm_back(up,n,r,g):
    e=up*g
    return r*(e-jnp.mean(e,axis=-1,keepdims=True)-n*jnp.mean(e*n,axis=-1,keepdims=True))
def ffn_kernel(chunks, parts, ctx_ref,x_ref,cot_ref,wo_ref,wu_ref,wd_ref,vec_ref,bu_ref,
               out_ref,normed_ref,hidden_ref,down_ref,up_ref,one_ref,att_ref,sums_ref,sumu_ref,slope_ref):
    wu=wu_ref[...].reshape(-1,wu_ref.shape[-1]); width=wu.shape[0]//chunks
    size=x_ref.shape[0]//parts
    @pl.when(pl.program_id(0)==0)
    def _():
        sums_ref[...]=jnp.zeros_like(sums_ref); sumu_ref[...]=jnp.zeros_like(sumu_ref)
    v=lambda i: vec_ref[i:i+1,:]
    b_o,g1,s1,b_d,g2,s2=[v(KW+i) for i in range(2,8)]
    total=lambda a: jnp.sum(a,axis=0,keepdims=True)
    def steps(at):
        rows=slice(at*size,(at+1)*size); st={}
        def attend(): st["one"]=nt(ctx_ref[rows,:],wo_ref[...])
        def norm_one():
            st["n1"],st["r1"]=norm(x_ref[rows,:].astype(F32)+(st["one"]+b_o))
            st["normed"]=st["n1"]*g1+s1
            st["low"]=st["normed"].astype(BF); normed_ref[rows,:]=st["low"]
        def up(k):
            def go():
                if k>0:
                    add=nt(st["hid"],wd_ref[k-1]); st["down"]=add if k==1 else st["down"]+add
                if k<chunks: st["pre"]=nt(st["low"],wu[k*width:(k+1)*width,:])
            return go
        def gelu(k):
            part=slice(k*width,(k+1)*width)
            def go():
                pre=st["pre"]+bu_ref[:,part]
                dist,slope=gelu_parts(pre)
                slope_ref[rows,part]=dist+slope
                st["hid"]=(pre*dist).astype(BF); hidden_ref[rows,part]=st["hid"]
            return go
        def norm_two():
            n2,r2=norm(st["normed"]+(st["down"]+b_d))
            out_ref[rows,:]=(n2*g2+s2).astype(BF)
            cot=cot_ref[rows,:].astype(F32)
            st["back"]=norm_back(cot,n2,r2,g2)
            st["low2"]=st["back"].astype(BF); down_ref[rows,:]=st["low2"]
            sums_ref[3:6,:]+=jnp.concatenate([total(st["low2"].astype(F32)),total(cot*n2),total(cot)],axis=0)
        def back(k):
            def go():
                if k>0: st["back"]=st["back"]+nn(st["upl"],wu[(k-1)*width:k*width,:])
                if k<chunks: st["hg"]=nn(st["low2"],wd_ref[k])
            return go
        def scale(k):
            part=slice(k*width,(k+1)*width)
            def go():
                upl=(st["hg"]*slope_ref[rows,part]).astype(BF); up_ref[rows,part]=upl; st["upl"]=upl
                sumu_ref[:,part]+=total(upl.astype(F32))
            return go
        def norm_last():
            g_one=norm_back(st["back"],st["n1"],st["r1"],g1)
            one_ref[rows,:]=g_one
            al=g_one.astype(BF); att_ref[rows,:]=al
            sums_ref[0:3,:]+=jnp.concatenate([total(al.astype(F32)),total(st["back"]*st["n1"]),total(st["back"])],axis=0)
        out=[attend,norm_one]
        for k in range(chunks): out+=[up(k),gelu(k)]
        out+=[up(chunks),norm_two]
        for k in range(chunks): out+=[back(k),scale(k)]
        return out+[back(chunks),norm_last]
    lists=[steps(at) for at in range(parts)]
    for i in range(len(lists[0])+parts-1):
        for at in range(parts):
            if 0<=i-at<len(lists[at]): lists[at][i-at]()
def ffn(ctx,x,cot,wo,wu,wd,vec,bu,block=512,parts=2):
    chunks=wd.shape[0]
    T,D=x.shape; F=bu.shape[1]
    row=lambda w: pl.BlockSpec((block,w),lambda i:(i,0))
    full=lambda a: pl.BlockSpec(a.shape,lambda i:(0,)*a.ndim,pipeline_mode=pl.Buffered(1))
    keep=lambda r,w: pl.BlockSpec((r,w),lambda i:(0,0))
    sd=jax.ShapeDtypeStruct
    return pl.pallas_call(functools.partial(ffn_kernel,chunks,parts),grid=(T//block,),
        in_specs=[row(D),row(D),row(D),full(wo),pl.BlockSpec((wu.shape[0],F//wu.shape[0],D),lambda i:(0,0,0),pipeline_mode=pl.Buffered(1)),full(wd),pl.BlockSpec((SMALL,D),lambda i:(0,0)),full(bu)],
        out_specs=[row(D),row(D),row(F),row(D),row(F),row(D),row(D),keep(8,D),keep(1,F)],
        out_shape=[sd((T,D),BF),sd((T,D),BF),sd((T,F),BF),sd((T,D),BF),sd((T,F),BF),sd((T,D),F32),sd((T,D),BF),sd((8,D),F32),sd((1,F),F32)],
        scratch_shapes=[pltpu.VMEM((block,F),F32)],
        compiler_params=pltpu.CompilerParams(vmem_limit_bytes=60*2**20,dimension_semantics=("arbitrary",)),
    )(ctx,x,cot,wo,wu,wd,vec,bu)


def across_rows(left_side, right_side):
    return lax.dot_general(left_side, right_side, (((0,), (0,)), ((), ())), preferred_element_type=F32)


def weight_kernel(own, up_ref, normed_ref, hidden_ref, down_ref, att_ref, ctx_ref, out_ref, acc_ref):
    depth=normed_ref.shape[1]; k=pl.program_id(1)
    wide_rows=up_ref.shape[1]; rows=down_ref.shape[1]; parts=hidden_ref.shape[1]//depth
    @pl.when(k==0)
    def _(): acc_ref[...]=jnp.zeros_like(acc_ref)
    for lo in range(0,wide_rows,rows):
        acc_ref[lo:lo+rows]+=across_rows(up_ref[:,lo:lo+rows],normed_ref[...])
    for i in range(parts):
        at=wide_rows+i*rows
        acc_ref[at:at+rows]+=across_rows(down_ref[...],hidden_ref[:,i*depth:(i+1)*depth])
    at=wide_rows+parts*rows
    acc_ref[at:at+rows]+=across_rows(att_ref[...],ctx_ref[...])
    @pl.when(k==pl.num_programs(1)-1)
    def _():
        many=rows//own; lines=wide_rows//many
        out_ref[:,:lines]=acc_ref[:wide_rows].reshape(many,lines,depth).astype(BF)
        narrow=[acc_ref[wide_rows+i*rows:wide_rows+(i+1)*rows].reshape(many,own,depth) for i in range(parts+1)]
        narrow.append(jnp.zeros((many,out_ref.shape[1]-lines-(parts+1)*own,depth),F32))
        out_ref[:,lines:]=jnp.concatenate(narrow,axis=1).astype(BF)
def weight_grads(own, up, normed, hidden, down, att, ctx):
    T,D=normed.shape; F=up.shape[1]; halves=2; many=D//own//halves; block=512
    R=-(-(F//D*2+1)*own//16)*16
    if own%8:
        by=lambda a: a.reshape(D//own,-1,D)
        pieces=[by(across_rows(up,normed))]+[by(across_rows(down,hidden[:,i*D:(i+1)*D])) for i in range(F//D)]
        pieces.append(by(across_rows(att,ctx)))
        pieces.append(jnp.zeros((D//own,R-(F//D*2+1)*own,D),F32))
        return jnp.concatenate(pieces,axis=1).astype(BF)
    col=lambda w: pl.BlockSpec((block,w),lambda h,k:(k,h)); row=lambda w: pl.BlockSpec((block,w),lambda h,k:(k,0))
    return pl.pallas_call(functools.partial(weight_kernel,own),grid=(halves,T//block),
        in_specs=[col(F//halves),row(D),row(F),col(D//halves),col(D//halves),row(D)],
        out_specs=pl.BlockSpec((many,R,D),lambda h,k:(h,0,0)),
        out_shape=jax.ShapeDtypeStruct((D//own,R,D),BF),
        scratch_shapes=[pltpu.VMEM((many*own*(F//D*2+1),D),F32)],
        compiler_params=pltpu.CompilerParams(vmem_limit_bytes=60*2**20))(up,normed,hidden,down,att,ctx)


def digits():
    found = []
    for axis in ("wide", "narrow"):
        stride = lax.axis_size(axis) // 2
        while stride >= 1:
            found.append((axis, stride))
            stride //= 2
    return found


def link_order(number):
    count = len(digits())
    if lax.axis_size("wide") == 8 and lax.axis_size("narrow") == 4:
        return [(4, 2, 3, 1, 0), (4, 3, 1, 2, 0), (4, 1, 2, 3, 0)][number]
    return tuple(range(count - 1, -1, -1))


def exchange(values, axis, stride):
    return lax.ppermute(values, axis, [(i, i ^ stride) for i in range(lax.axis_size(axis))])


def digit_of(axis, stride):
    return (lax.axis_index(axis) // stride) % 2


def gather_rows(shard, number, passed=None):
    places = digits()
    held = shard.reshape((1,) * len(places) + shard.shape)
    for dim in link_order(number)[::-1]:
        if passed is not None:
            passed.append(held)
        mine = digit_of(*places[dim])
        got = exchange(held, *places[dim])
        first = jnp.where(mine == 0, held, got)
        second = jnp.where(mine == 0, got, held)
        held = jnp.concatenate([first, second], dim)
    return held.reshape((-1,) + shard.shape)


def scatter_start(whole, own):
    return whole.reshape(whole.shape[:-2] + (2,) * len(digits()) + (own, whole.shape[-1]))


def scatter_step(held, number, step):
    places = digits()
    dim = link_order(number)[step] + held.ndim - 2 - len(places)
    place = places[link_order(number)[step]]
    mine = digit_of(*place)
    keep = lax.dynamic_slice_in_dim(held, mine, 1, dim).astype(F32)
    send = lax.dynamic_slice_in_dim(held, 1 - mine, 1, dim).astype(BF)
    return keep + exchange(send, *place).astype(F32)


def scatter_rest(held, number, step):
    for later in range(step, len(digits())):
        held = scatter_step(held, number, later)
    return held.reshape(held.shape[: held.ndim - 2 - len(digits())] + held.shape[-2:])


def shards(
    inputs,
    tok_landmark,
    landmark_doc,
    w_query,
    b_query,
    w_key,
    w_value,
    b_value,
    conv_weight,
    w_out,
    b_out,
    gain_one,
    shift_one,
    w_up,
    b_up,
    w_down,
    b_down,
    gain_two,
    shift_two,
    cotangent,
):
    batch_rows, sequence_length, feature_width = inputs.shape
    group_count = lax.axis_size("wide") * lax.axis_size("narrow")
    own = feature_width // group_count
    tokens = batch_rows * sequence_length
    lines = b_up.shape[0] // own
    vectors = (b_query, b_value, b_out, gain_one, shift_one, b_down, gain_two, shift_two)
    flat = 0
    for place, vector in enumerate(vectors + (b_up,)):
        before = place * own
        flat = flat + jnp.pad(vector, (before, (8 + lines) * own - before - vector.shape[0]))
    small = jnp.concatenate([conv_weight, flat.reshape(8 + lines, own)])
    small = jnp.pad(small.T, ((0, 0), (0, 128 - small.shape[0])))
    passed = []
    w_q = gather_rows(w_query.T, 1).reshape(feature_width, feature_width)
    w_k = gather_rows(w_key.T, 2).reshape(feature_width, feature_width)
    gathered_v = gather_rows(jnp.concatenate([w_value.T, small], axis=1), 0, passed)
    gathered_v = gathered_v.reshape(feature_width, feature_width + 128)
    w_v = gathered_v[:, :feature_width]
    small = gathered_v[:, feature_width:]
    b_u = jnp.moveaxis(small[:, KW + 8 : KW + 8 + lines].reshape(group_count, own, lines), 1, 2)
    b_u = b_u.reshape(1, -1).astype(F32)
    small = small.astype(F32).T
    ff_count = w_down.shape[0] // feature_width
    w_out, w_up, w_down, _ = lax.optimization_barrier((w_out, w_up, w_down, passed[2]))
    shard = jnp.concatenate(
        [w_up.T, w_out.T] + [w_down[i * feature_width : (i + 1) * feature_width].T for i in range(ff_count)]
    )
    gathered = lax.all_gather(shard, ("wide", "narrow"), axis=0)
    w_o = gathered[:, own * lines : own * (1 + lines)].reshape(feature_width, feature_width)
    w_u = gathered if own * lines % 16 == 0 else gathered[:, : own * lines].reshape(1, -1, feature_width)
    w_d = jnp.moveaxis(
        gathered[:, own * (1 + lines) :].reshape(group_count, ff_count, own, feature_width), 0, 1
    ).reshape(ff_count, feature_width, feature_width)
    member = tok_landmark[:, None, :] == jnp.arange(LM)[None, :, None]
    means = jnp.einsum("bjt,bti->bji", member.astype(BF), inputs, preferred_element_type=F32)
    means = means / jnp.sum(member, axis=2)[..., None].astype(F32)
    doc = jnp.sum(jnp.where(member, landmark_doc[:, :, None], 0), axis=1)
    bounds = jnp.sum(doc[:, None, :] < jnp.arange(DOCS + 1)[None, :, None], axis=2).astype(jnp.int32)
    rows_low = inputs.reshape(tokens, feature_width)
    value_rows, conv_part = conv_fwd(bounds, inputs, w_v, small)
    q, k, v, k1, k3, inv, stash, landmarks, context = att_fwd(
        inputs, means, w_q, w_k, w_v, small, tok_landmark, landmark_doc, conv_part
    )
    context = context.reshape(tokens, feature_width)
    layer_out, normed, hidden, down_low, up_low, grad_one, att_low, sums, sums_up = ffn(
        context, rows_low, cotangent.reshape(tokens, feature_width), w_o, w_u, w_d, small, b_u
    )
    grads = weight_grads(own, up_low, normed, hidden, down_low, att_low, context)
    share = lax.psum_scatter(grads, ("wide", "narrow"), scatter_dimension=0, tiled=True)[0].astype(F32)
    w_plain = w_o.T
    att_low = att_low.reshape(inputs.shape)
    dq, dk, dv, grad_qk, sum_q = att_bwd(
        inputs, att_low, w_plain, q, k, v, k1, k3, inv, stash, landmarks, tok_landmark
    )
    more = (sum_q, sums, sums_up.reshape(feature_width, lines))
    moving = scatter_start(grad_qk, own)
    calls, before = 3, ()
    slabs = feature_width // 128 // calls
    for call in range(calls):
        moved = scatter_step(moving, 1, call)
        before = conv_bwd(
            bounds, value_rows, att_low, w_o, small, inputs, dv, more, before, slabs, call * slabs
        )
        before, att_low, moving = lax.optimization_barrier((tuple(before), att_low, moved))
    dv, grad_v = before
    share_qk = scatter_rest(moving, 1, calls)
    share_v = scatter_rest(scatter_start(grad_v, own), 0, 0)
    input_grad = grad_one.reshape(inputs.shape)
    for grad, weight in zip((dq, dk, dv), (w_q, w_k, w_v)):
        input_grad = input_grad + jnp.einsum("bot,oi->bti", grad, weight, preferred_element_type=F32)
    late = share_v[:, feature_width:]
    share_down = share[own * lines : 2 * own * lines].reshape(ff_count, own, feature_width)
    share_out = share[2 * own * lines : 2 * own * lines + own]
    return (
        layer_out.reshape(inputs.shape),
        input_grad,
        share_qk[0].T,
        late[:, KW + 1],
        share_qk[1].T,
        share_v[:, :feature_width].T,
        late[:, KW],
        late[:, :KW].T,
        share_out.T,
        late[:, KW + 2],
        late[:, KW + 3],
        late[:, KW + 4],
        share[: own * lines].T,
        late[:, KW + 8 : KW + 8 + lines].reshape(-1),
        jnp.moveaxis(share_down, 1, 2).reshape(-1, own),
        late[:, KW + 5],
        late[:, KW + 6],
        late[:, KW + 7],
    )


def solution(mesh):
    return jax.shard_map(
        shards,
        mesh=mesh,
        in_specs=(
            P(("wide", "narrow"), None, None),
            P(("wide", "narrow"), None),
            P(("wide", "narrow"), None),
            P(None, ("wide", "narrow")),
            P(("wide", "narrow")),
            P(None, ("wide", "narrow")),
            P(None, ("wide", "narrow")),
            P(("wide", "narrow")),
            P(None, ("wide", "narrow")),
            P(None, ("wide", "narrow")),
            P(("wide", "narrow")),
            P(("wide", "narrow")),
            P(("wide", "narrow")),
            P(None, ("wide", "narrow")),
            P(("wide", "narrow")),
            P(None, ("wide", "narrow")),
            P(("wide", "narrow")),
            P(("wide", "narrow")),
            P(("wide", "narrow")),
            P(("wide", "narrow"), None, None),
        ),
        out_specs=(
            P(("wide", "narrow"), None, None),
            P(("wide", "narrow"), None, None),
            P(None, ("wide", "narrow")),
            P(("wide", "narrow")),
            P(None, ("wide", "narrow")),
            P(None, ("wide", "narrow")),
            P(("wide", "narrow")),
            P(None, ("wide", "narrow")),
            P(None, ("wide", "narrow")),
            P(("wide", "narrow")),
            P(("wide", "narrow")),
            P(("wide", "narrow")),
            P(None, ("wide", "narrow")),
            P(("wide", "narrow")),
            P(None, ("wide", "narrow")),
            P(("wide", "narrow")),
            P(("wide", "narrow")),
            P(("wide", "narrow")),
        ),
        check_vma=False,
    )
```

```python
import functools

import jax
import jax.numpy as jnp
from jax import lax
from jax.experimental import pallas as pl
from jax.experimental.pallas import tpu as pltpu
from jax.sharding import PartitionSpec as P

BF = jnp.bfloat16
F32 = jnp.float32
HW=64; LM=64; NEWTON=6; GH=12; GW=GH*HW
CHUNK=256
KW=33
SMALL=48
def nt(a,b): return lax.dot_general(a,b,(((1,),(1,)),((),())),preferred_element_type=F32)
def nn(a,b): return lax.dot_general(a,b,(((1,),(0,)),((),())),preferred_element_type=F32)
def split(a):
    hi=a.astype(BF); return hi,(a-hi.astype(F32)).astype(BF)
def wide(a):
    hi,lo=split(a); return jnp.concatenate([hi,hi,lo],axis=1)
def tall(b):
    hi,lo=split(b); return jnp.concatenate([hi,lo,hi],axis=0)
def mm3(a,b): return nn(wide(a),tall(b))
def eye(c):
    row=lax.broadcasted_iota(jnp.int32,(LM,2*LM),0); col=lax.broadcasted_iota(jnp.int32,(LM,2*LM),1)
    return jnp.where((row==col)|(row+LM==col),c,0.0)
def beside(a):
    return [jnp.concatenate([a[i],a[i+1]],axis=1) for i in range(0,len(a),2)]
def blocks(b):
    lane=lax.broadcasted_iota(jnp.int32,(1,2*LM),1)
    first=jnp.where(lane<LM,1.0,0.0).astype(BF); second=jnp.where(lane<LM,0.0,1.0).astype(BF)
    hi,lo=split(b)
    return jnp.concatenate([hi*first,hi*second,lo*first,lo*second,hi*first,hi*second],axis=0)
def mmb(a,b): return nn(wide(a),blocks(b))
def weave(first, second):
    done=0
    for i,step in enumerate(first):
        step()
        upto=(i+1)*len(second)//len(first)
        for other in second[done:upto]: other()
        done=upto
def att_fwd_kernel(x_ref,mean_ref,wq_ref,wk_ref,wv_ref,vec_ref,tok_ref,ldc_ref,ldr_ref,conv_ref,
               q_ref,k_ref,v_ref,k1_ref,k3_ref,inv_ref,stash_ref,small_ref,ctx_ref,
               qlo_ref,klo_ref,score_ref,bias_ref):
    T=x_ref.shape[1]
    heads=range(GH); chunks=[slice(c,c+CHUNK) for c in range(0,T,CHUNK)]
    rows=[slice(h*HW,(h+1)*HW) for h in heads]
    scale=HW**-0.25
    bq=vec_ref[KW:KW+1,:].T; bv=vec_ref[KW+1:KW+2,:].T
    ldc=ldc_ref[0]
    for cs in chunks:
        member=lax.broadcasted_iota(jnp.int32,(LM,CHUNK),0)==tok_ref[0,:,cs]
        doc=jnp.sum(jnp.where(member,ldc,0),axis=0,keepdims=True)
        bias_ref[:,cs]=jnp.where(doc==ldc,0.0,-1e30)
    mean=jnp.concatenate(split(mean_ref[0]),axis=0)
    def land(w_ref):
        both=nt(w_ref[...],mean)
        return both[:,:LM]+both[:,LM:]
    lqt=(land(wq_ref)+bq)*scale; lkt=land(wk_ref)*scale
    lq=[lqt[r].T for r in rows]; lk=[lkt[r].T for r in rows]
    lqw=[wide(a) for a in lq]; lkw=[wide(a) for a in lk]
    allow2=ldc==ldr_ref[0]
    k2=[];zt=[]
    for h in heads:
        sc=jnp.where(allow2,nn(lqw[h],tall(lkt[rows[h]])),-1e30)
        e=jnp.exp(sc-jnp.max(sc,axis=1,keepdims=True))
        k2.append(e/jnp.sum(e,axis=1,keepdims=True))
        zt.append(k2[h]*(1.0/jnp.sum(k2[h]*k2[h])))
    pairs=range(GH//2)
    state={"zt":beside(zt)}
    k2tb=[blocks(a) for a in beside([a.T for a in k2])]
    def newton(n):
        def one():
            state["p"]=[nn(wide(state["zt"][i]),k2tb[i]) for i in pairs]
            state["pw"]=[wide(a) for a in state["p"]]
        def two(): state["b"]=[eye(15.0)-nn(state["pw"][i],blocks(eye(7.0)-state["p"][i])) for i in pairs]
        def three(): state["c"]=[eye(13.0)-nn(state["pw"][i],blocks(state["b"][i])) for i in pairs]
        def four():
            for i in pairs:
                for place,key in enumerate(("p","b","c","zt")): stash_ref[0,i,4*n+place]=state[key][i]
            state["zt"]=[0.25*mmb(state["c"][i],state["zt"][i]) for i in pairs]
        return [one,two,three,four]
    chain=[step for n in range(NEWTON) for step in newton(n)]
    side=[]
    def project(cs):
        x=x_ref[0,cs,:]
        def q():
            a=(nt(wq_ref[...],x)+bq)*scale
            hi,lo=split(a); q_ref[0,:,cs]=hi; qlo_ref[:,cs]=lo
        def k():
            a=nt(wk_ref[...],x)*scale
            hi,lo=split(a); k_ref[0,:,cs]=hi; klo_ref[:,cs]=lo
        def v(): v_ref[0,:,cs]=(nt(wv_ref[...],x)+bv).astype(BF)
        return [q,k,v]
    tops=[None]*GH; sums=[None]*GH; r=[None]*GH
    def lanes(a): return [a[:,i:i+128] for i in range(0,CHUNK,128)]
    def first(h,cs):
        def go():
            hi=q_ref[0,rows[h],cs]
            s=nn(lkw[h],jnp.concatenate([hi,qlo_ref[rows[h],cs],hi],axis=0))+bias_ref[:,cs]
            e=jnp.exp(s-jnp.max(s,axis=0,keepdims=True))
            e=e.astype(BF); k1_ref[0,rows[h],cs]=e
            inv_ref[0,0,h:h+1,cs]=1.0/jnp.sum(e.astype(F32),axis=0,keepdims=True)
        return go
    def third(h,cs):
        def go():
            hi=k_ref[0,rows[h],cs]
            s=nn(lqw[h],jnp.concatenate([hi,klo_ref[rows[h],cs],hi],axis=0))+bias_ref[:,cs]
            score_ref[rows[h],cs]=s
            for a in lanes(s): tops[h]=a if tops[h] is None else jnp.maximum(tops[h],a)
        return go
    def raised(h,cs):
        def go():
            if cs.start==0: tops[h]=jnp.max(tops[h],axis=1,keepdims=True)
            e=jnp.exp(score_ref[rows[h],cs]-tops[h])
            e=e.astype(BF); k3_ref[0,rows[h],cs]=e
            for a in lanes(e.astype(F32)): sums[h]=a if sums[h] is None else sums[h]+a
        return go
    def gathered(h):
        def go():
            sums[h]=1.0/jnp.sum(sums[h],axis=1,keepdims=True)
            r[h]=nt(k3_ref[0,rows[h]],v_ref[0,rows[h]])*sums[h]
        return go
    for cs in chunks: side+=project(cs)
    for h in heads:
        side+=[third(h,cs) for cs in chunks]
        side+=[raised(h,cs) for cs in chunks]+[gathered(h)]
        side+=[first(h,cs) for cs in chunks]
    weave(chain,side)
    uts=[]
    for h in heads:
        zt=state["zt"][h//2][:,h%2*LM:(h%2+1)*LM]
        u=mm3(zt.T,r[h])
        small_ref[0,h,0]=jnp.concatenate([lq[h],lk[h]],axis=1)
        small_ref[0,h,1]=jnp.concatenate([k2[h],zt],axis=1)
        small_ref[0,h,2]=jnp.concatenate([r[h],u],axis=1)
        small_ref[0,h,3]=jnp.broadcast_to(sums[h],(LM,128))
        uts.append(u.T.astype(BF))
    for cs in chunks:
        mixed=jnp.concatenate([nn(uts[h],k1_ref[0,rows[h],cs])*inv_ref[0,0,h:h+1,cs] for h in heads],axis=0)
        ctx_ref[0,cs,:]=(mixed.T+conv_ref[0,cs,:]).astype(BF)
def att_specs(D,T):
    seq=lambda s: pl.BlockSpec((1,)+s,lambda g,b:(b,)+(0,)*len(s))
    wsp=pl.BlockSpec((GW,D),lambda g,b:(g,0)); bsp=pl.BlockSpec((GW,1),lambda g,b:(g,0))
    rows=pl.BlockSpec((1,GW,T),lambda g,b:(b,g,0)); cols=pl.BlockSpec((1,T,GW),lambda g,b:(b,0,g))
    sq=lambda m,n: pl.BlockSpec((1,m,n,LM,2*LM),lambda g,b:(b,g,0,0,0))
    turned=pl.BlockSpec((1,1,-(-GH//8)*8,T),lambda g,b:(b,g,0,0))
    return seq,wsp,bsp,rows,cols,sq,turned
def att_fwd(x,mean,wq,wk,wv,vec,tok,ld,conv):
    B,T,D=x.shape; G=D//GW; H=D//HW
    seq,wsp,bsp,rows,cols,sq,turned=att_specs(D,T)
    sd=jax.ShapeDtypeStruct; big=sd((B,D,T),BF)
    return pl.pallas_call(att_fwd_kernel,grid=(G,B),
        in_specs=[seq((T,D)),seq((LM,D)),wsp,wsp,wsp,pl.BlockSpec((SMALL,GW),lambda g,b:(0,g)),seq((1,T)),seq((LM,1)),seq((1,LM)),cols],
        out_specs=[rows]*5+[turned,sq(GH//2,4*NEWTON),sq(GH,4),cols],
        out_shape=[big]*5+[sd((B,G,-(-GH//8)*8,T),F32),sd((B,H//2,4*NEWTON,LM,2*LM),F32),sd((B,H,4,LM,2*LM),F32),sd((B,T,D),BF)],
        scratch_shapes=[pltpu.VMEM((GW,T),BF)]*2+[pltpu.VMEM((GW,T),F32),pltpu.VMEM((LM,T),F32)],
        compiler_params=pltpu.CompilerParams(vmem_limit_bytes=60*2**20))(
            x,mean,wq,wk,wv,vec,tok[:,None,:],ld[:,:,None],ld[:,None,:],conv)
def att_bwd_kernel(x_ref,al_ref,wo_ref,q_ref,k_ref,v_ref,k1_ref,k3_ref,inv_ref,stash_ref,small_ref,tok_ref,
               dq_ref,dk_ref,dv_ref,gqk_ref,sq_ref,
               g_ref,ds1_ref,ds3_ref,hot_ref):
    T=x_ref.shape[1]
    heads=range(GH); chunks=[slice(c,c+CHUNK) for c in range(0,T,CHUNK)]
    rows=[slice(h*HW,(h+1)*HW) for h in heads]
    scale=HW**-0.25
    for cs in chunks:
        member=lax.broadcasted_iota(jnp.int32,(LM,CHUNK),0)==tok_ref[0,:,cs]
        hot_ref[:,cs]=jnp.where(member,1.0,0.0).astype(BF)
    per=1.0/nt(jnp.ones((8,T),BF),hot_ref[...])[0:1]
    left=lambda i: [small_ref[0,h,i,:,:LM] for h in heads]
    right=lambda i: [small_ref[0,h,i,:,LM:] for h in heads]
    lq,lk,k2,zt,r,u=left(0),right(0),left(1),right(1),left(2),right(2)
    inv=[small_ref[0,h,3,:,:LM] for h in heads]
    ub=[a.astype(BF) for a in u]
    def upstream(cs):
        def go():
            a=nt(wo_ref[...],al_ref[0,cs,:])
            for h in heads: g_ref[rows[h],cs]=(a[rows[h]]*inv_ref[0,0,h:h+1,cs]).astype(BF)
        return go
    def first(h,cs):
        def go():
            k1=k1_ref[0,rows[h],cs].astype(F32)
            t=k1*nn(ub[h],g_ref[rows[h],cs])
            ds1_ref[rows[h],cs]=(t-k1*(jnp.sum(t,axis=0,keepdims=True)*inv_ref[0,0,h:h+1,cs])).astype(BF)
        return go
    for cs in chunks: upstream(cs)()
    du=[nt(k1_ref[0,rows[h]],g_ref[rows[h],:]) for h in heads]
    dr=[mm3(zt[h],du[h]) for h in heads]
    state={"dz":beside([mm3(du[h],r[h].T) for h in heads]),"dk2":[None]*(GH//2)}
    drs=[(dr[h]*inv[h]) for h in heads]
    drb=[a.astype(BF) for a in drs]; drt=[a.T.astype(BF) for a in drs]
    delta=[jnp.sum(drb[h].astype(F32)*r[h],axis=1,keepdims=True) for h in heads]
    dlq=[None]*GH; dlk=[None]*GH
    def third(h,cs):
        def go():
            d=k3_ref[0,rows[h],cs].astype(F32)*(nn(drb[h],v_ref[0,rows[h],cs])-delta[h])
            ds3_ref[rows[h],cs]=d.astype(BF)
        return go
    def values(cs):
        def go():
            a=jnp.concatenate([nn(drt[h],k3_ref[0,rows[h],cs]) for h in heads],axis=0)
            dv_ref[0,:,cs]=a
        return go
    def to_lk(h):
        def go(): dlk[h]=nt(ds1_ref[rows[h],:],q_ref[0,rows[h]])
        return go
    def to_lq(h):
        def go(): dlq[h]=nt(ds3_ref[rows[h],:],k_ref[0,rows[h]])
        return go
    @pl.when(pl.program_id(1)==0)
    def _():
        for ref in (gqk_ref,sq_ref): ref[...]=jnp.zeros_like(ref)
    side=[]
    for h in heads: side+=[third(h,cs) for cs in chunks]+[to_lq(h)]+[first(h,cs) for cs in chunks]+[to_lk(h)]
    side+=[values(cs) for cs in chunks]
    pairs=range(GH//2)
    k2t=[a.T for a in k2]; k2tw=[wide(a) for a in beside(k2t)]
    def newton(n):
        def one():
            state["p"],state["b"],state["c"],state["zt"]=[[stash_ref[0,i,4*n+place] for i in pairs] for place in range(4)]
            state["gz"]=[0.25*d for d in state["dz"]]
            state["dc"]=[mmb(state["zt"][i],state["gz"][i]) for i in pairs]
            state["pw"]=[wide(m) for m in state["p"]]
        def two(): state["db"]=[nn(state["pw"][i],blocks(state["dc"][i])) for i in pairs]
        def three():
            da=[nn(state["pw"][i],blocks(state["db"][i])) for i in pairs]
            state["dp"]=[mmb(state["db"][i],eye(7.0)-state["p"][i])-mmb(state["dc"][i],state["b"][i])-da[i] for i in pairs]
        def four():
            for i in pairs:
                t=mmb(state["dp"][i],state["zt"][i])
                state["dk2"][i]=t if state["dk2"][i] is None else state["dk2"][i]+t
            state["dz"]=[mmb(state["gz"][i],state["c"][i])+nn(k2tw[i],blocks(state["dp"][i])) for i in pairs]
        return [one,two,three,four]
    chain=[step for n in reversed(range(NEWTON)) for step in newton(n)]
    weave(chain,side)
    lhq=[];lhk=[]
    for h in heads:
        half=slice(h%2*LM,(h%2+1)*LM)
        i2=1.0/jnp.sum(k2[h]*k2[h]); dz=state["dz"][h//2][:,half]
        d=state["dk2"][h//2][:,half]+i2*dz.T-k2[h]*(2.0*i2*i2*jnp.sum(dz*k2t[h]))
        d=k2[h]*(d-jnp.sum(k2[h]*d,axis=1,keepdims=True))
        dlqh=dlq[h]+mm3(d,lk[h]); dlkh=dlk[h]+mm3(d.T,lq[h])
        lhq.append(jnp.concatenate([lk[h].T,dlqh.T*per],axis=1).astype(BF))
        lhk.append(jnp.concatenate([lq[h].T,dlkh.T*per],axis=1).astype(BF))
    for cs in chunks:
        hot=hot_ref[:,cs]
        for lh,ds_ref,out_ref in ((lhq,ds1_ref,dq_ref),(lhk,ds3_ref,dk_ref)):
            for h in heads:
                a=nn(lh[h],jnp.concatenate([ds_ref[rows[h],cs],hot],axis=0))
                out_ref[0,rows[h],cs]=(a*scale).astype(BF)
    dq=dq_ref[0]
    gqk_ref[0]+=nn(dq,x_ref[0]); gqk_ref[1]+=nn(dk_ref[0],x_ref[0])
    sq_ref[...]+=jnp.sum(dq.astype(F32),axis=1,keepdims=True)
def att_bwd(x,al,wo,q,k,v,k1,k3,inv,stash,small,tok):
    B,T,D=x.shape; G=D//GW
    seq,wsp,bsp,rows,cols,sq,turned=att_specs(D,T)
    sd=jax.ShapeDtypeStruct; big=sd((B,D,T),BF)
    return pl.pallas_call(att_bwd_kernel,grid=(G,B),
        in_specs=[seq((T,D)),seq((T,D)),wsp]+[rows]*5+[turned,sq(GH//2,4*NEWTON),sq(GH,4),seq((1,T))],
        out_specs=[rows]*3+[pl.BlockSpec((2,GW,D),lambda g,b:(0,g,0)),bsp],
        out_shape=[big,big,sd((B,D,T),F32),sd((2,D,D),F32),sd((D,1),F32)],
        scratch_shapes=[pltpu.VMEM((GW,T),BF)]*3+[pltpu.VMEM((LM,T),BF)],
        compiler_params=pltpu.CompilerParams(vmem_limit_bytes=60*2**20))(
            x,al,wo,q,k,v,k1,k3,inv,stash,small,tok[:,None,:])

HALF=16; DOCS=4; GAP=16
def spread(places, bounds, length, step):
    total=length+GAP*(DOCS+1)
    ids=lax.broadcasted_iota(jnp.int32,(step,128),0)
    for p0 in range(0,total,step):
        size=min(step,total-p0)
        sums=[None]*len(places)
        for d in range(DOCS):
            s0=p0-GAP*(d+1)
            lo=max(s0,0); hi=min(s0+size,length)
            if hi<=lo: continue
            row=ids[:hi-lo]+lo
            inside=(row>=bounds[d])&(row<bounds[d+1])
            for i,(_,get) in enumerate(places):
                part=jnp.where(inside,get(lo,hi-lo),0.0)
                pads=[]
                if lo>s0: pads.append(jnp.zeros((lo-s0,128),F32))
                pads.append(part)
                if s0+size>hi: pads.append(jnp.zeros((s0+size-hi,128),F32))
                part=jnp.concatenate(pads,0) if len(pads)>1 else part
                sums[i]=part if sums[i] is None else sums[i]+part
        for i,(dst,_) in enumerate(places):
            dst[HALF+p0:HALF+p0+size,:]=jnp.zeros((size,128),F32) if sums[i] is None else sums[i]
def collect(src, bounds, lo, size):
    row=lax.broadcasted_iota(jnp.int32,(size,128),0)+lo
    acc=None
    for d in range(DOCS):
        part=src[lo+GAP*(d+1):lo+GAP*(d+1)+size,:]
        acc=part if acc is None else jnp.where(row>=bounds[d],part,acc)
    return acc
BLOCK=64
TALL=128
WIDTH=256
SLABS=range(WIDTH//128)
def taps(ref, base, weight, sign):
    acc=None
    for r in range(8):
        win=ref[pl.ds(base+r,TALL+32),:] if r==0 else ref[pl.ds(base+r,TALL+24),:]
        for a in range(5 if r==0 else 4):
            o=8*a+r
            t=weight(o if sign>0 else 2*HALF-o)*win[8*a:8*a+TALL]
            acc=t if acc is None else acc+t
    return acc

def cut(h): return slice(h*128,(h+1)*128)
def conv_fwd_kernel(bounds_ref, x_ref, wv_ref, w_ref, v_ref, out_ref, pad_ref, res_ref):
    b=pl.program_id(0)
    bounds=[bounds_ref[b,d] for d in range(DOCS+1)]
    length=v_ref.shape[1]; total=length+GAP*(DOCS+1)
    for lo in range(0,length,256):
        v_ref[0,lo:lo+256,:]=nt(x_ref[0,lo:lo+256,:],wv_ref[...])+w_ref[KW+1:KW+2,:]
    for h in SLABS:
        pad_ref[h,0:HALF,:]=jnp.zeros((HALF,128),F32)
        pad_ref[h,HALF+total:,:]=jnp.zeros((pad_ref.shape[1]-HALF-total,128),F32)
    spread([(pad_ref.at[h], lambda lo,n,h=h: v_ref[0,lo:lo+n,cut(h)]) for h in SLABS], bounds, length, BLOCK)
    def block(i,c):
        base=pl.multiple_of(i*TALL,TALL)
        for h in SLABS:
            res_ref[h,pl.ds(base,TALL),:]=taps(pad_ref.at[h], base, lambda s: w_ref[s:s+1,cut(h)], 1)
        return c
    lax.fori_loop(0,-(-total//TALL),block,0)
    for h in SLABS:
        for lo in range(0,length,BLOCK):
            out_ref[0,lo:lo+BLOCK,cut(h)]=collect(res_ref.at[h],bounds,lo,BLOCK)
def padded_rows(length):
    total=length+GAP*(DOCS+1)
    return -(-total//TALL)*TALL

def conv_fwd(bounds, x, w_v, w):
    B,L,D=x.shape
    rows=padded_rows(L)
    slab=pl.BlockSpec((1,L,WIDTH),lambda b,c,_:(b,0,c)); big=jax.ShapeDtypeStruct((B,L,D),F32)
    return pl.pallas_call(conv_fwd_kernel,grid_spec=pltpu.PrefetchScalarGridSpec(num_scalar_prefetch=1,grid=(B,D//WIDTH),
        in_specs=[pl.BlockSpec((1,L,D),lambda b,c,_:(b,0,0)),pl.BlockSpec((WIDTH,D),lambda b,c,_:(c,0)),
            pl.BlockSpec((SMALL,WIDTH),lambda b,c,_:(0,c))],
        out_specs=[slab,slab],
        scratch_shapes=[pltpu.VMEM((WIDTH//128,rows+2*HALF+8,128),F32),pltpu.VMEM((WIDTH//128,rows,128),F32)]),
        out_shape=[big,big],
        compiler_params=pltpu.CompilerParams(vmem_limit_bytes=60*2**20))(bounds,x,w_v,w)
def conv_bwd_kernel(bounds_ref, v_ref, al_ref, wo_ref, w_ref, x_ref, att_ref, q_ref, sums_ref, su_ref, *refs):
    dv_ref, gv_ref, vpad_ref, gpad_ref, res_ref, acc_ref, g_ref, sum_ref = refs[-8:]
    b=pl.program_id(1)
    bounds=[bounds_ref[b,d] for d in range(DOCS+1)]
    length=v_ref.shape[1]; total=length+GAP*(DOCS+1)
    for lo in range(0,length,256):
        g_ref[lo:lo+256,:]=nn(al_ref[0,lo:lo+256,:],wo_ref[...])
    for ref in (vpad_ref,gpad_ref):
        ref[0:HALF,:]=jnp.zeros((HALF,128),F32)
        ref[HALF+total:,:]=jnp.zeros((ref.shape[0]-HALF-total,128),F32)
    spread([(vpad_ref, lambda lo,n: v_ref[0,lo:lo+n,:]), (gpad_ref, lambda lo,n: g_ref[lo:lo+n,:])], bounds, length, BLOCK)
    @pl.when(b==0)
    def _():
        acc_ref[...]=jnp.zeros_like(acc_ref); gv_ref[...]=jnp.zeros_like(gv_ref); sum_ref[...]=jnp.zeros_like(sum_ref)
    def block(i,c):
        base=pl.multiple_of(i*BLOCK,BLOCK)
        here=vpad_ref[pl.ds(base+HALF,BLOCK),:]
        acc=None
        for r in range(8):
            n=5 if r==0 else 4
            win=gpad_ref[pl.ds(base+r,BLOCK+8*(n-1)),:]
            for a in range(n):
                s=2*HALF-(8*a+r)
                x=win[8*a:8*a+BLOCK]
                t=w_ref[s:s+1,:]*x
                acc=t if acc is None else acc+t
                p=(here*x).reshape(BLOCK//8,8,128)
                acc_ref[s]+=jnp.sum(p,axis=0)
        res_ref[pl.ds(base,BLOCK),:]=acc
        return c
    lax.fori_loop(0,-(-total//BLOCK),block,0)
    for lo in range(0,length,BLOCK*2):
        part=collect(res_ref,bounds,lo,BLOCK*2).T+att_ref[0,:,lo:lo+BLOCK*2]
        dv_ref[0,:,lo:lo+BLOCK*2]=part.astype(BF)
    dv=dv_ref[0]; depth=x_ref.shape[2]
    gv_ref[:,:depth]+=nn(dv,x_ref[0])
    sum_ref[...]+=jnp.sum(dv.astype(F32),axis=1,keepdims=True)
    @pl.when(b==pl.num_programs(1)-1)
    def _():
        rows=[jnp.sum(acc_ref[s],axis=0,keepdims=True) for s in range(KW)]
        side=jnp.concatenate(rows+[jnp.zeros((128-KW,128),F32)],axis=0).T
        lane=lax.broadcasted_iota(jnp.int32,(128,128),1)
        lines=su_ref.shape[1]
        side=side+jnp.where(lane==KW,sum_ref[:,:1],0.0)+jnp.where(lane==KW+1,q_ref[...],0.0)
        early=sums_ref[...].T
        for i in range(6): side=side+jnp.where(lane==KW+2+i,early[:,i:i+1],0.0)
        for i in range(lines): side=side+jnp.where(lane==KW+8+i,su_ref[:,i:i+1],0.0)
        gv_ref[:,depth:]=side
def conv_bwd(bounds, v, al, w_o, w, x, att, more, before, slabs, at):
    B,L,D=v.shape
    rows=padded_rows(L)
    sd=jax.ShapeDtypeStruct
    seq=pl.BlockSpec((1,L,D),lambda c,b,_:(b,0,0))
    feats=pl.BlockSpec((1,128,L),lambda c,b,_:(b,at+c,0))
    alias={11:0,12:1} if before else {}
    return pl.pallas_call(conv_bwd_kernel,grid_spec=pltpu.PrefetchScalarGridSpec(num_scalar_prefetch=1,grid=(slabs,B),
        in_specs=[pl.BlockSpec((1,L,128),lambda c,b,_:(b,0,at+c)),seq,
            pl.BlockSpec((D,128),lambda c,b,_:(0,at+c)),pl.BlockSpec((SMALL,128),lambda c,b,_:(0,at+c)),
            seq,feats,pl.BlockSpec((128,1),lambda c,b,_:(at+c,0)),pl.BlockSpec((8,128),lambda c,b,_:(0,at+c)),
            pl.BlockSpec((128,more[2].shape[1]),lambda c,b,_:(at+c,0))]+[pl.BlockSpec(memory_space=pl.ANY)]*len(before),
        out_specs=[feats,pl.BlockSpec((128,D+128),lambda c,b,_:(at+c,0))],
        scratch_shapes=[pltpu.VMEM((rows+2*HALF+8,128),F32)]*2+[pltpu.VMEM((rows,128),F32),pltpu.VMEM((KW,8,128),F32),
            pltpu.VMEM((L,128),F32),pltpu.VMEM((128,128),F32)]),
        out_shape=[sd((B,D,L),BF),sd((D,D+128),F32)],input_output_aliases={i-1:o for i,o in alias.items()},
        compiler_params=pltpu.CompilerParams(vmem_limit_bytes=60*2**20))(bounds,v,al,w_o,w,x,att,*more,*before)

def gelu_parts(x):
    size=jnp.abs(x)
    density=jnp.exp(-0.5*x*x)*0.3989422804014327
    t=1.0/(1.0+0.2316419*size)
    tail=density*(t*(0.319381530+t*(-0.356563782+t*(1.781477937+t*(-1.821255978+t*1.330274429)))))
    dist=jnp.where(x<0.0,tail,1.0-tail)
    return dist, x*density
def norm(v):
    mean=jnp.mean(v,axis=-1,keepdims=True); c=v-mean
    r=lax.rsqrt(jnp.mean(c*c,axis=-1,keepdims=True)+1e-5)
    return c*r, r
def norm_back(up,n,r,g):
    e=up*g
    return r*(e-jnp.mean(e,axis=-1,keepdims=True)-n*jnp.mean(e*n,axis=-1,keepdims=True))
def ffn_kernel(chunks, parts, ctx_ref,x_ref,cot_ref,wo_ref,wu_ref,*refs):
    wd_ref=refs[:chunks]
    (vec_ref,bu_ref,
               out_ref,normed_ref,hidden_ref,down_ref,up_ref,one_ref,att_ref,sums_ref,sumu_ref,slope_ref)=refs[chunks:]
    wu=wu_ref[...].reshape(-1,wu_ref.shape[-1]); width=wu.shape[0]//chunks
    size=x_ref.shape[0]//parts
    @pl.when(pl.program_id(0)==0)
    def _():
        sums_ref[...]=jnp.zeros_like(sums_ref); sumu_ref[...]=jnp.zeros_like(sumu_ref)
    v=lambda i: vec_ref[i:i+1,:]
    b_o,g1,s1,b_d,g2,s2=[v(KW+i) for i in range(2,8)]
    total=lambda a: jnp.sum(a,axis=0,keepdims=True)
    def steps(at):
        rows=slice(at*size,(at+1)*size); st={}
        def attend(): st["one"]=nt(ctx_ref[rows,:],wo_ref[...])
        def norm_one():
            st["n1"],st["r1"]=norm(x_ref[rows,:].astype(F32)+(st["one"]+b_o))
            st["normed"]=st["n1"]*g1+s1
            st["low"]=st["normed"].astype(BF); normed_ref[rows,:]=st["low"]
        def up(k):
            def go():
                if k>0:
                    add=nt(st["hid"],wd_ref[k-1][...]); st["down"]=add if k==1 else st["down"]+add
                if k<chunks: st["pre"]=nt(st["low"],wu[k*width:(k+1)*width,:])
            return go
        def gelu(k):
            part=slice(k*width,(k+1)*width)
            def go():
                pre=st["pre"]+bu_ref[:,part]
                dist,slope=gelu_parts(pre)
                slope_ref[rows,part]=dist+slope
                st["hid"]=(pre*dist).astype(BF); hidden_ref[rows,part]=st["hid"]
            return go
        def norm_two():
            n2,r2=norm(st["normed"]+(st["down"]+b_d))
            out_ref[rows,:]=(n2*g2+s2).astype(BF)
            cot=cot_ref[rows,:].astype(F32)
            st["back"]=norm_back(cot,n2,r2,g2)
            st["low2"]=st["back"].astype(BF); down_ref[rows,:]=st["low2"]
            sums_ref[3:6,:]+=jnp.concatenate([total(st["low2"].astype(F32)),total(cot*n2),total(cot)],axis=0)
        def back(k):
            def go():
                if k>0: st["back"]=st["back"]+nn(st["upl"],wu[(k-1)*width:k*width,:])
                if k<chunks: st["hg"]=nn(st["low2"],wd_ref[k][...])
            return go
        def scale(k):
            part=slice(k*width,(k+1)*width)
            def go():
                upl=(st["hg"]*slope_ref[rows,part]).astype(BF); up_ref[rows,part]=upl; st["upl"]=upl
                sumu_ref[:,part]+=total(upl.astype(F32))
            return go
        def norm_last():
            g_one=norm_back(st["back"],st["n1"],st["r1"],g1)
            one_ref[rows,:]=g_one
            al=g_one.astype(BF); att_ref[rows,:]=al
            sums_ref[0:3,:]+=jnp.concatenate([total(al.astype(F32)),total(st["back"]*st["n1"]),total(st["back"])],axis=0)
        out=[attend,norm_one]
        for k in range(chunks): out+=[up(k),gelu(k)]
        out+=[up(chunks),norm_two]
        for k in range(chunks): out+=[back(k),scale(k)]
        return out+[back(chunks),norm_last]
    lists=[steps(at) for at in range(parts)]
    for i in range(len(lists[0])+parts-1):
        for at in range(parts):
            if 0<=i-at<len(lists[at]): lists[at][i-at]()
def ffn(ctx,x,cot,wo,wu,wd,vec,bu,block=512,parts=2):
    chunks=len(wd)
    T,D=x.shape; F=bu.shape[1]
    row=lambda w: pl.BlockSpec((block,w),lambda i:(i,0))
    full=lambda a: pl.BlockSpec(a.shape,lambda i:(0,)*a.ndim,pipeline_mode=pl.Buffered(1))
    keep=lambda r,w: pl.BlockSpec((r,w),lambda i:(0,0))
    sd=jax.ShapeDtypeStruct
    return pl.pallas_call(functools.partial(ffn_kernel,chunks,parts),grid=(T//block,),
        in_specs=[row(D),row(D),row(D),full(wo),pl.BlockSpec((wu.shape[0],F//wu.shape[0],D),lambda i:(0,0,0),pipeline_mode=pl.Buffered(1)),*[full(a) for a in wd],pl.BlockSpec((SMALL,D),lambda i:(0,0)),full(bu)],
        out_specs=[row(D),row(D),row(F),row(D),row(F),row(D),row(D),keep(8,D),keep(1,F)],
        out_shape=[sd((T,D),BF),sd((T,D),BF),sd((T,F),BF),sd((T,D),BF),sd((T,F),BF),sd((T,D),F32),sd((T,D),BF),sd((8,D),F32),sd((1,F),F32)],
        scratch_shapes=[pltpu.VMEM((block,F),F32)],
        compiler_params=pltpu.CompilerParams(vmem_limit_bytes=60*2**20,dimension_semantics=("arbitrary",)),
    )(ctx,x,cot,wo,wu,*wd,vec,bu)


def across_rows(left_side, right_side):
    return lax.dot_general(left_side, right_side, (((0,), (0,)), ((), ())), preferred_element_type=F32)


def weight_kernel(own, up_ref, normed_ref, hidden_ref, down_ref, att_ref, ctx_ref, out_ref, acc_ref):
    depth=normed_ref.shape[1]; k=pl.program_id(1)
    wide_rows=up_ref.shape[1]; rows=down_ref.shape[1]; parts=hidden_ref.shape[1]//depth
    @pl.when(k==0)
    def _(): acc_ref[...]=jnp.zeros_like(acc_ref)
    for lo in range(0,wide_rows,rows):
        acc_ref[lo:lo+rows]+=across_rows(up_ref[:,lo:lo+rows],normed_ref[...])
    for i in range(parts):
        at=wide_rows+i*rows
        acc_ref[at:at+rows]+=across_rows(down_ref[...],hidden_ref[:,i*depth:(i+1)*depth])
    at=wide_rows+parts*rows
    acc_ref[at:at+rows]+=across_rows(att_ref[...],ctx_ref[...])
    @pl.when(k==pl.num_programs(1)-1)
    def _():
        many=rows//own; lines=wide_rows//many
        out_ref[:,:lines]=acc_ref[:wide_rows].reshape(many,lines,depth).astype(BF)
        narrow=[acc_ref[wide_rows+i*rows:wide_rows+(i+1)*rows].reshape(many,own,depth) for i in range(parts+1)]
        narrow.append(jnp.zeros((many,out_ref.shape[1]-lines-(parts+1)*own,depth),F32))
        out_ref[:,lines:]=jnp.concatenate(narrow,axis=1).astype(BF)
def weight_grads(own, up, normed, hidden, down, att, ctx):
    T,D=normed.shape; F=up.shape[1]; halves=2; many=D//own//halves; block=512
    R=-(-(F//D*2+1)*own//16)*16
    if own%8:
        by=lambda a: a.reshape(D//own,-1,D)
        pieces=[by(across_rows(up,normed))]+[by(across_rows(down,hidden[:,i*D:(i+1)*D])) for i in range(F//D)]
        pieces.append(by(across_rows(att,ctx)))
        pieces.append(jnp.zeros((D//own,R-(F//D*2+1)*own,D),F32))
        return jnp.concatenate(pieces,axis=1).astype(BF)
    col=lambda w: pl.BlockSpec((block,w),lambda h,k:(k,h)); row=lambda w: pl.BlockSpec((block,w),lambda h,k:(k,0))
    return pl.pallas_call(functools.partial(weight_kernel,own),grid=(halves,T//block),
        in_specs=[col(F//halves),row(D),row(F),col(D//halves),col(D//halves),row(D)],
        out_specs=pl.BlockSpec((many,R,D),lambda h,k:(h,0,0)),
        out_shape=jax.ShapeDtypeStruct((D//own,R,D),BF),
        scratch_shapes=[pltpu.VMEM((many*own*(F//D*2+1),D),F32)],
        compiler_params=pltpu.CompilerParams(vmem_limit_bytes=60*2**20))(up,normed,hidden,down,att,ctx)


def digits():
    found = []
    for axis in ("wide", "narrow"):
        stride = lax.axis_size(axis) // 2
        while stride >= 1:
            found.append((axis, stride))
            stride //= 2
    return found


def link_order(number):
    count = len(digits())
    if lax.axis_size("wide") == 8 and lax.axis_size("narrow") == 4:
        return [(4, 2, 3, 1, 0), (4, 3, 1, 2, 0), (4, 1, 2, 3, 0)][number]
    return tuple(range(count - 1, -1, -1))


def exchange(values, axis, stride):
    return lax.ppermute(values, axis, [(i, i ^ stride) for i in range(lax.axis_size(axis))])


def digit_of(axis, stride):
    return (lax.axis_index(axis) // stride) % 2


def gather_rows(shards):
    places = digits()
    held = [shard.reshape((1,) * len(places) + shard.shape) for shard in shards]
    passed = []
    for step in range(len(places)):
        for number, values in enumerate(held):
            dim = link_order(number)[::-1][step]
            mine = digit_of(*places[dim])
            got = exchange(values, *places[dim])
            first = jnp.where(mine == 0, values, got)
            second = jnp.where(mine == 0, got, values)
            held[number] = jnp.concatenate([first, second], dim)
        held = list(lax.optimization_barrier(tuple(held)))
        passed.append(held[0])
    return [values.reshape((-1,) + values.shape[-2:]) for values in held], passed


def scatter_start(whole, own):
    return whole.reshape(whole.shape[:-2] + (2,) * len(digits()) + (own, whole.shape[-1]))


def scatter_step(held, number, step):
    places = digits()
    dim = link_order(number)[step] + held.ndim - 2 - len(places)
    place = places[link_order(number)[step]]
    mine = digit_of(*place)
    keep = lax.dynamic_slice_in_dim(held, mine, 1, dim).astype(F32)
    send = lax.dynamic_slice_in_dim(held, 1 - mine, 1, dim).astype(BF)
    return keep + exchange(send, *place).astype(F32)


def scatter_rest(held, number, step):
    for later in range(step, len(digits())):
        held = scatter_step(held, number, later)
    return held.reshape(held.shape[: held.ndim - 2 - len(digits())] + held.shape[-2:])


def shards(
    inputs,
    tok_landmark,
    landmark_doc,
    w_query,
    b_query,
    w_key,
    w_value,
    b_value,
    conv_weight,
    w_out,
    b_out,
    gain_one,
    shift_one,
    w_up,
    b_up,
    w_down,
    b_down,
    gain_two,
    shift_two,
    cotangent,
):
    batch_rows, sequence_length, feature_width = inputs.shape
    group_count = lax.axis_size("wide") * lax.axis_size("narrow")
    own = feature_width // group_count
    tokens = batch_rows * sequence_length
    lines = b_up.shape[0] // own
    vectors = (b_query, b_value, b_out, gain_one, shift_one, b_down, gain_two, shift_two)
    flat = 0
    for place, vector in enumerate(vectors + (b_up,)):
        before = place * own
        flat = flat + jnp.pad(vector, (before, (8 + lines) * own - before - vector.shape[0]))
    small = jnp.concatenate([conv_weight, flat.reshape(8 + lines, own)])
    small = jnp.pad(small.T, ((0, 0), (0, 128 - small.shape[0])))
    (gathered_v, w_q, w_k), passed = gather_rows(
        [jnp.concatenate([w_value.T, small], axis=1), w_query.T, w_key.T]
    )
    w_q = w_q.reshape(feature_width, feature_width)
    w_k = w_k.reshape(feature_width, feature_width)
    gathered_v = gathered_v.reshape(feature_width, feature_width + 128)
    w_v = gathered_v[:, :feature_width]
    small = gathered_v[:, feature_width:]
    b_u = jnp.moveaxis(small[:, KW + 8 : KW + 8 + lines].reshape(group_count, own, lines), 1, 2)
    b_u = b_u.reshape(1, -1).astype(F32)
    small = small.astype(F32).T
    ff_count = w_down.shape[0] // feature_width
    w_out, w_up, w_down, _ = lax.optimization_barrier((w_out, w_up, w_down, passed[0]))
    shard = jnp.concatenate(
        [w_up.T, w_out.T] + [w_down[i * feature_width : (i + 1) * feature_width].T for i in range(ff_count)]
    )
    gathered = lax.all_gather(shard, ("wide", "narrow"), axis=0)
    w_o = gathered[:, own * lines : own * (1 + lines)].reshape(feature_width, feature_width)
    w_u = gathered if own * lines % 16 == 0 else gathered[:, : own * lines].reshape(1, -1, feature_width)
    w_d = [
        gathered[:, own * (1 + lines + i) : own * (2 + lines + i)].reshape(feature_width, feature_width)
        for i in range(ff_count)
    ]
    member = tok_landmark[:, None, :] == jnp.arange(LM)[None, :, None]
    means = jnp.einsum("bjt,bti->bji", member.astype(BF), inputs, preferred_element_type=F32)
    means = means / jnp.sum(member, axis=2)[..., None].astype(F32)
    doc = jnp.sum(jnp.where(member, landmark_doc[:, :, None], 0), axis=1)
    bounds = jnp.sum(doc[:, None, :] < jnp.arange(DOCS + 1)[None, :, None], axis=2).astype(jnp.int32)
    rows_low = inputs.reshape(tokens, feature_width)
    value_rows, conv_part = conv_fwd(bounds, inputs, w_v, small)
    q, k, v, k1, k3, inv, stash, landmarks, context = att_fwd(
        inputs, means, w_q, w_k, w_v, small, tok_landmark, landmark_doc, conv_part
    )
    context = context.reshape(tokens, feature_width)
    layer_out, normed, hidden, down_low, up_low, grad_one, att_low, sums, sums_up = ffn(
        context, rows_low, cotangent.reshape(tokens, feature_width), w_o, w_u, w_d, small, b_u
    )
    grads = weight_grads(own, up_low, normed, hidden, down_low, att_low, context)
    share = lax.psum_scatter(grads, ("wide", "narrow"), scatter_dimension=0, tiled=True)[0].astype(F32)
    w_plain = w_o.T
    att_low = att_low.reshape(inputs.shape)
    dq, dk, dv, grad_qk, sum_q = att_bwd(
        inputs, att_low, w_plain, q, k, v, k1, k3, inv, stash, landmarks, tok_landmark
    )
    more = (sum_q, sums, sums_up.reshape(feature_width, lines))
    moving = scatter_start(grad_qk, own)
    calls, before = 3, ()
    slabs = feature_width // 128 // calls
    for call in range(calls):
        moved = scatter_step(moving, 1, call)
        before = conv_bwd(
            bounds, value_rows, att_low, w_o, small, inputs, dv, more, before, slabs, call * slabs
        )
        before, att_low, moving = lax.optimization_barrier((tuple(before), att_low, moved))
    (dv, grad_v), dq, dk = lax.optimization_barrier((before, dq, dk))
    share_qk = scatter_rest(moving, 1, calls)
    share_v = scatter_rest(scatter_start(grad_v, own), 0, 0)
    input_grad = grad_one.reshape(inputs.shape)
    for grad, weight in zip((dq, dk, dv), (w_q, w_k, w_v)):
        input_grad = input_grad + jnp.einsum("bot,oi->bti", grad, weight, preferred_element_type=F32)
    late = share_v[:, feature_width:]
    share_down = share[own * lines : 2 * own * lines].reshape(ff_count, own, feature_width)
    share_out = share[2 * own * lines : 2 * own * lines + own]
    return (
        layer_out.reshape(inputs.shape),
        input_grad,
        share_qk[0].T,
        late[:, KW + 1],
        share_qk[1].T,
        share_v[:, :feature_width].T,
        late[:, KW],
        late[:, :KW].T,
        share_out.T,
        late[:, KW + 2],
        late[:, KW + 3],
        late[:, KW + 4],
        share[: own * lines].T,
        late[:, KW + 8 : KW + 8 + lines].reshape(-1),
        jnp.moveaxis(share_down, 1, 2).reshape(-1, own),
        late[:, KW + 5],
        late[:, KW + 6],
        late[:, KW + 7],
    )


def solution(mesh):
    return jax.shard_map(
        shards,
        mesh=mesh,
        in_specs=(
            P(("wide", "narrow"), None, None),
            P(("wide", "narrow"), None),
            P(("wide", "narrow"), None),
            P(None, ("wide", "narrow")),
            P(("wide", "narrow")),
            P(None, ("wide", "narrow")),
            P(None, ("wide", "narrow")),
            P(("wide", "narrow")),
            P(None, ("wide", "narrow")),
            P(None, ("wide", "narrow")),
            P(("wide", "narrow")),
            P(("wide", "narrow")),
            P(("wide", "narrow")),
            P(None, ("wide", "narrow")),
            P(("wide", "narrow")),
            P(None, ("wide", "narrow")),
            P(("wide", "narrow")),
            P(("wide", "narrow")),
            P(("wide", "narrow")),
            P(("wide", "narrow"), None, None),
        ),
        out_specs=(
            P(("wide", "narrow"), None, None),
            P(("wide", "narrow"), None, None),
            P(None, ("wide", "narrow")),
            P(("wide", "narrow")),
            P(None, ("wide", "narrow")),
            P(None, ("wide", "narrow")),
            P(("wide", "narrow")),
            P(None, ("wide", "narrow")),
            P(None, ("wide", "narrow")),
            P(("wide", "narrow")),
            P(("wide", "narrow")),
            P(("wide", "narrow")),
            P(None, ("wide", "narrow")),
            P(("wide", "narrow")),
            P(None, ("wide", "narrow")),
            P(("wide", "narrow")),
            P(("wide", "narrow")),
            P(("wide", "narrow")),
        ),
        check_vma=False,
    )
```

```python
import functools

import jax
import jax.numpy as jnp
from jax import lax
from jax.experimental import pallas as pl
from jax.experimental.pallas import tpu as pltpu
from jax.sharding import PartitionSpec as P

BF = jnp.bfloat16
F32 = jnp.float32
HW=64; LM=64; NEWTON=6; GH=12; GW=GH*HW
CHUNK=256
KW=33
SMALL=48
def nt(a,b): return lax.dot_general(a,b,(((1,),(1,)),((),())),preferred_element_type=F32)
def nn(a,b): return lax.dot_general(a,b,(((1,),(0,)),((),())),preferred_element_type=F32)
def split(a):
    hi=a.astype(BF); return hi,(a-hi.astype(F32)).astype(BF)
def wide(a):
    hi,lo=split(a); return jnp.concatenate([hi,hi,lo],axis=1)
def tall(b):
    hi,lo=split(b); return jnp.concatenate([hi,lo,hi],axis=0)
def mm3(a,b): return nn(wide(a),tall(b))
def eye(c):
    row=lax.broadcasted_iota(jnp.int32,(LM,2*LM),0); col=lax.broadcasted_iota(jnp.int32,(LM,2*LM),1)
    return jnp.where((row==col)|(row+LM==col),c,0.0)
def beside(a):
    return [jnp.concatenate([a[i],a[i+1]],axis=1) for i in range(0,len(a),2)]
def blocks(b):
    lane=lax.broadcasted_iota(jnp.int32,(1,2*LM),1)
    first=jnp.where(lane<LM,1.0,0.0).astype(BF); second=jnp.where(lane<LM,0.0,1.0).astype(BF)
    hi,lo=split(b)
    return jnp.concatenate([hi*first,hi*second,lo*first,lo*second,hi*first,hi*second],axis=0)
def mmb(a,b): return nn(wide(a),blocks(b))
def weave(first, second):
    done=0
    for i,step in enumerate(first):
        step()
        upto=(i+1)*len(second)//len(first)
        for other in second[done:upto]: other()
        done=upto
def att_fwd_kernel(x_ref,mean_ref,wq_ref,wk_ref,wv_ref,vec_ref,tok_ref,ldc_ref,ldr_ref,conv_ref,
               q_ref,k_ref,v_ref,k1_ref,k3_ref,inv_ref,stash_ref,small_ref,ctx_ref,
               qlo_ref,klo_ref,score_ref,bias_ref):
    T=x_ref.shape[1]
    heads=range(GH); chunks=[slice(c,c+CHUNK) for c in range(0,T,CHUNK)]
    rows=[slice(h*HW,(h+1)*HW) for h in heads]
    scale=HW**-0.25
    bq=vec_ref[KW:KW+1,:].T; bv=vec_ref[KW+1:KW+2,:].T
    ldc=ldc_ref[0]
    for cs in chunks:
        member=lax.broadcasted_iota(jnp.int32,(LM,CHUNK),0)==tok_ref[0,:,cs]
        doc=jnp.sum(jnp.where(member,ldc,0),axis=0,keepdims=True)
        bias_ref[:,cs]=jnp.where(doc==ldc,0.0,-1e30)
    mean=jnp.concatenate(split(mean_ref[0]),axis=0)
    def land(w_ref):
        both=nt(w_ref[...],mean)
        return both[:,:LM]+both[:,LM:]
    lqt=(land(wq_ref)+bq)*scale; lkt=land(wk_ref)*scale
    lq=[lqt[r].T for r in rows]; lk=[lkt[r].T for r in rows]
    lqw=[wide(a) for a in lq]; lkw=[wide(a) for a in lk]
    allow2=ldc==ldr_ref[0]
    k2=[];zt=[]
    for h in heads:
        sc=jnp.where(allow2,nn(lqw[h],tall(lkt[rows[h]])),-1e30)
        e=jnp.exp(sc-jnp.max(sc,axis=1,keepdims=True))
        k2.append(e/jnp.sum(e,axis=1,keepdims=True))
        zt.append(k2[h]*(1.0/jnp.sum(k2[h]*k2[h])))
    pairs=range(GH//2)
    state={"zt":beside(zt)}
    k2tb=[blocks(a) for a in beside([a.T for a in k2])]
    def newton(n):
        def one():
            state["p"]=[nn(wide(state["zt"][i]),k2tb[i]) for i in pairs]
            state["pw"]=[wide(a) for a in state["p"]]
        def two(): state["b"]=[eye(15.0)-nn(state["pw"][i],blocks(eye(7.0)-state["p"][i])) for i in pairs]
        def three(): state["c"]=[eye(13.0)-nn(state["pw"][i],blocks(state["b"][i])) for i in pairs]
        def four():
            for i in pairs:
                for place,key in enumerate(("p","b","c","zt")): stash_ref[0,i,4*n+place]=state[key][i]
            state["zt"]=[0.25*mmb(state["c"][i],state["zt"][i]) for i in pairs]
        return [one,two,three,four]
    chain=[step for n in range(NEWTON) for step in newton(n)]
    side=[]
    def project(cs):
        x=x_ref[0,cs,:]
        def q():
            a=(nt(wq_ref[...],x)+bq)*scale
            hi,lo=split(a); q_ref[0,:,cs]=hi; qlo_ref[:,cs]=lo
        def k():
            a=nt(wk_ref[...],x)*scale
            hi,lo=split(a); k_ref[0,:,cs]=hi; klo_ref[:,cs]=lo
        def v(): v_ref[0,:,cs]=(nt(wv_ref[...],x)+bv).astype(BF)
        return [q,k,v]
    tops=[None]*GH; sums=[None]*GH; r=[None]*GH
    def lanes(a): return [a[:,i:i+128] for i in range(0,CHUNK,128)]
    def first(h,cs):
        def go():
            hi=q_ref[0,rows[h],cs]
            s=nn(lkw[h],jnp.concatenate([hi,qlo_ref[rows[h],cs],hi],axis=0))+bias_ref[:,cs]
            e=jnp.exp(s-jnp.max(s,axis=0,keepdims=True))
            e=e.astype(BF); k1_ref[0,rows[h],cs]=e
            inv_ref[0,0,h:h+1,cs]=1.0/jnp.sum(e.astype(F32),axis=0,keepdims=True)
        return go
    def third(h,cs):
        def go():
            hi=k_ref[0,rows[h],cs]
            s=nn(lqw[h],jnp.concatenate([hi,klo_ref[rows[h],cs],hi],axis=0))+bias_ref[:,cs]
            score_ref[rows[h],cs]=s
            for a in lanes(s): tops[h]=a if tops[h] is None else jnp.maximum(tops[h],a)
        return go
    def raised(h,cs):
        def go():
            if cs.start==0: tops[h]=jnp.max(tops[h],axis=1,keepdims=True)
            e=jnp.exp(score_ref[rows[h],cs]-tops[h])
            e=e.astype(BF); k3_ref[0,rows[h],cs]=e
            for a in lanes(e.astype(F32)): sums[h]=a if sums[h] is None else sums[h]+a
        return go
    def gathered(h):
        def go():
            sums[h]=1.0/jnp.sum(sums[h],axis=1,keepdims=True)
            r[h]=nt(k3_ref[0,rows[h]],v_ref[0,rows[h]])*sums[h]
        return go
    for cs in chunks: side+=project(cs)
    for h in heads:
        side+=[third(h,cs) for cs in chunks]
        side+=[raised(h,cs) for cs in chunks]+[gathered(h)]
        side+=[first(h,cs) for cs in chunks]
    weave(chain,side)
    uts=[]
    for h in heads:
        zt=state["zt"][h//2][:,h%2*LM:(h%2+1)*LM]
        u=mm3(zt.T,r[h])
        small_ref[0,h,0]=jnp.concatenate([lq[h],lk[h]],axis=1)
        small_ref[0,h,1]=jnp.concatenate([k2[h],zt],axis=1)
        small_ref[0,h,2]=jnp.concatenate([r[h],u],axis=1)
        small_ref[0,h,3]=jnp.broadcast_to(sums[h],(LM,128))
        uts.append(u.T.astype(BF))
    for cs in chunks:
        mixed=jnp.concatenate([nn(uts[h],k1_ref[0,rows[h],cs])*inv_ref[0,0,h:h+1,cs] for h in heads],axis=0)
        ctx_ref[0,cs,:]=(mixed.T+conv_ref[0,cs,:]).astype(BF)
def att_specs(D,T):
    seq=lambda s: pl.BlockSpec((1,)+s,lambda g,b:(b,)+(0,)*len(s))
    wsp=pl.BlockSpec((GW,D),lambda g,b:(g,0)); bsp=pl.BlockSpec((GW,1),lambda g,b:(g,0))
    rows=pl.BlockSpec((1,GW,T),lambda g,b:(b,g,0)); cols=pl.BlockSpec((1,T,GW),lambda g,b:(b,0,g))
    sq=lambda m,n: pl.BlockSpec((1,m,n,LM,2*LM),lambda g,b:(b,g,0,0,0))
    turned=pl.BlockSpec((1,1,-(-GH//8)*8,T),lambda g,b:(b,g,0,0))
    return seq,wsp,bsp,rows,cols,sq,turned
def att_fwd(x,mean,wq,wk,wv,vec,tok,ld,conv):
    B,T,D=x.shape; G=D//GW; H=D//HW
    seq,wsp,bsp,rows,cols,sq,turned=att_specs(D,T)
    sd=jax.ShapeDtypeStruct; big=sd((B,D,T),BF)
    return pl.pallas_call(att_fwd_kernel,grid=(G,B),
        in_specs=[seq((T,D)),seq((LM,D)),wsp,wsp,wsp,pl.BlockSpec((SMALL,GW),lambda g,b:(0,g)),seq((1,T)),seq((LM,1)),seq((1,LM)),cols],
        out_specs=[rows]*5+[turned,sq(GH//2,4*NEWTON),sq(GH,4),cols],
        out_shape=[big]*5+[sd((B,G,-(-GH//8)*8,T),F32),sd((B,H//2,4*NEWTON,LM,2*LM),F32),sd((B,H,4,LM,2*LM),F32),sd((B,T,D),BF)],
        scratch_shapes=[pltpu.VMEM((GW,T),BF)]*2+[pltpu.VMEM((GW,T),F32),pltpu.VMEM((LM,T),F32)],
        compiler_params=pltpu.CompilerParams(vmem_limit_bytes=60*2**20))(
            x,mean,wq,wk,wv,vec,tok[:,None,:],ld[:,:,None],ld[:,None,:],conv)
def att_bwd_kernel(x_ref,al_ref,wo_ref,q_ref,k_ref,v_ref,k1_ref,k3_ref,inv_ref,stash_ref,small_ref,tok_ref,
               dq_ref,dk_ref,dv_ref,gqk_ref,sq_ref,
               g_ref,ds1_ref,ds3_ref,hot_ref):
    T=x_ref.shape[1]
    heads=range(GH); chunks=[slice(c,c+CHUNK) for c in range(0,T,CHUNK)]
    rows=[slice(h*HW,(h+1)*HW) for h in heads]
    scale=HW**-0.25
    for cs in chunks:
        member=lax.broadcasted_iota(jnp.int32,(LM,CHUNK),0)==tok_ref[0,:,cs]
        hot_ref[:,cs]=jnp.where(member,1.0,0.0).astype(BF)
    per=1.0/nt(jnp.ones((8,T),BF),hot_ref[...])[0:1]
    left=lambda i: [small_ref[0,h,i,:,:LM] for h in heads]
    right=lambda i: [small_ref[0,h,i,:,LM:] for h in heads]
    lq,lk,k2,zt,r,u=left(0),right(0),left(1),right(1),left(2),right(2)
    inv=[small_ref[0,h,3,:,:LM] for h in heads]
    ub=[a.astype(BF) for a in u]
    def upstream(cs):
        def go():
            a=nt(wo_ref[...],al_ref[0,cs,:])
            for h in heads: g_ref[rows[h],cs]=(a[rows[h]]*inv_ref[0,0,h:h+1,cs]).astype(BF)
        return go
    def first(h,cs):
        def go():
            k1=k1_ref[0,rows[h],cs].astype(F32)
            t=k1*nn(ub[h],g_ref[rows[h],cs])
            ds1_ref[rows[h],cs]=(t-k1*(jnp.sum(t,axis=0,keepdims=True)*inv_ref[0,0,h:h+1,cs])).astype(BF)
        return go
    for cs in chunks: upstream(cs)()
    du=[nt(k1_ref[0,rows[h]],g_ref[rows[h],:]) for h in heads]
    dr=[mm3(zt[h],du[h]) for h in heads]
    state={"dz":beside([mm3(du[h],r[h].T) for h in heads]),"dk2":[None]*(GH//2)}
    drs=[(dr[h]*inv[h]) for h in heads]
    drb=[a.astype(BF) for a in drs]; drt=[a.T.astype(BF) for a in drs]
    delta=[jnp.sum(drb[h].astype(F32)*r[h],axis=1,keepdims=True) for h in heads]
    dlq=[None]*GH; dlk=[None]*GH
    def third(h,cs):
        def go():
            d=k3_ref[0,rows[h],cs].astype(F32)*(nn(drb[h],v_ref[0,rows[h],cs])-delta[h])
            ds3_ref[rows[h],cs]=d.astype(BF)
        return go
    def values(cs):
        def go():
            a=jnp.concatenate([nn(drt[h],k3_ref[0,rows[h],cs]) for h in heads],axis=0)
            dv_ref[0,:,cs]=a
        return go
    def to_lk(h):
        def go(): dlk[h]=nt(ds1_ref[rows[h],:],q_ref[0,rows[h]])
        return go
    def to_lq(h):
        def go(): dlq[h]=nt(ds3_ref[rows[h],:],k_ref[0,rows[h]])
        return go
    @pl.when(pl.program_id(1)==0)
    def _():
        for ref in (gqk_ref,sq_ref): ref[...]=jnp.zeros_like(ref)
    side=[]
    for h in heads: side+=[third(h,cs) for cs in chunks]+[to_lq(h)]+[first(h,cs) for cs in chunks]+[to_lk(h)]
    side+=[values(cs) for cs in chunks]
    pairs=range(GH//2)
    k2t=[a.T for a in k2]; k2tw=[wide(a) for a in beside(k2t)]
    def newton(n):
        def one():
            state["p"],state["b"],state["c"],state["zt"]=[[stash_ref[0,i,4*n+place] for i in pairs] for place in range(4)]
            state["gz"]=[0.25*d for d in state["dz"]]
            state["dc"]=[mmb(state["zt"][i],state["gz"][i]) for i in pairs]
            state["pw"]=[wide(m) for m in state["p"]]
        def two(): state["db"]=[nn(state["pw"][i],blocks(state["dc"][i])) for i in pairs]
        def three():
            da=[nn(state["pw"][i],blocks(state["db"][i])) for i in pairs]
            state["dp"]=[mmb(state["db"][i],eye(7.0)-state["p"][i])-mmb(state["dc"][i],state["b"][i])-da[i] for i in pairs]
        def four():
            for i in pairs:
                t=mmb(state["dp"][i],state["zt"][i])
                state["dk2"][i]=t if state["dk2"][i] is None else state["dk2"][i]+t
            state["dz"]=[mmb(state["gz"][i],state["c"][i])+nn(k2tw[i],blocks(state["dp"][i])) for i in pairs]
        return [one,two,three,four]
    chain=[step for n in reversed(range(NEWTON)) for step in newton(n)]
    weave(chain,side)
    lhq=[];lhk=[]
    for h in heads:
        half=slice(h%2*LM,(h%2+1)*LM)
        i2=1.0/jnp.sum(k2[h]*k2[h]); dz=state["dz"][h//2][:,half]
        d=state["dk2"][h//2][:,half]+i2*dz.T-k2[h]*(2.0*i2*i2*jnp.sum(dz*k2t[h]))
        d=k2[h]*(d-jnp.sum(k2[h]*d,axis=1,keepdims=True))
        dlqh=dlq[h]+mm3(d,lk[h]); dlkh=dlk[h]+mm3(d.T,lq[h])
        lhq.append(jnp.concatenate([lk[h].T,dlqh.T*per],axis=1).astype(BF))
        lhk.append(jnp.concatenate([lq[h].T,dlkh.T*per],axis=1).astype(BF))
    for cs in chunks:
        hot=hot_ref[:,cs]
        for lh,ds_ref,out_ref in ((lhq,ds1_ref,dq_ref),(lhk,ds3_ref,dk_ref)):
            for h in heads:
                a=nn(lh[h],jnp.concatenate([ds_ref[rows[h],cs],hot],axis=0))
                out_ref[0,rows[h],cs]=(a*scale).astype(BF)
    dq=dq_ref[0]
    gqk_ref[0]+=nn(dq,x_ref[0]); gqk_ref[1]+=nn(dk_ref[0],x_ref[0])
    sq_ref[...]+=jnp.sum(dq.astype(F32),axis=1,keepdims=True)
def att_bwd(x,al,wo,q,k,v,k1,k3,inv,stash,small,tok):
    B,T,D=x.shape; G=D//GW
    seq,wsp,bsp,rows,cols,sq,turned=att_specs(D,T)
    sd=jax.ShapeDtypeStruct; big=sd((B,D,T),BF)
    return pl.pallas_call(att_bwd_kernel,grid=(G,B),
        in_specs=[seq((T,D)),seq((T,D)),wsp]+[rows]*5+[turned,sq(GH//2,4*NEWTON),sq(GH,4),seq((1,T))],
        out_specs=[rows]*3+[pl.BlockSpec((2,GW,D),lambda g,b:(0,g,0)),bsp],
        out_shape=[big,big,sd((B,D,T),F32),sd((2,D,D),F32),sd((D,1),F32)],
        scratch_shapes=[pltpu.VMEM((GW,T),BF)]*3+[pltpu.VMEM((LM,T),BF)],
        compiler_params=pltpu.CompilerParams(vmem_limit_bytes=60*2**20))(
            x,al,wo,q,k,v,k1,k3,inv,stash,small,tok[:,None,:])

HALF=16; DOCS=4; GAP=16
def spread(places, bounds, length, step):
    total=length+GAP*(DOCS+1)
    ids=lax.broadcasted_iota(jnp.int32,(step,128),0)
    for p0 in range(0,total,step):
        size=min(step,total-p0)
        sums=[None]*len(places)
        for d in range(DOCS):
            s0=p0-GAP*(d+1)
            lo=max(s0,0); hi=min(s0+size,length)
            if hi<=lo: continue
            row=ids[:hi-lo]+lo
            inside=(row>=bounds[d])&(row<bounds[d+1])
            for i,(_,get) in enumerate(places):
                part=jnp.where(inside,get(lo,hi-lo),0.0)
                pads=[]
                if lo>s0: pads.append(jnp.zeros((lo-s0,128),F32))
                pads.append(part)
                if s0+size>hi: pads.append(jnp.zeros((s0+size-hi,128),F32))
                part=jnp.concatenate(pads,0) if len(pads)>1 else part
                sums[i]=part if sums[i] is None else sums[i]+part
        for i,(dst,_) in enumerate(places):
            dst[HALF+p0:HALF+p0+size,:]=jnp.zeros((size,128),F32) if sums[i] is None else sums[i]
def collect(src, bounds, lo, size):
    row=lax.broadcasted_iota(jnp.int32,(size,128),0)+lo
    acc=None
    for d in range(DOCS):
        part=src[lo+GAP*(d+1):lo+GAP*(d+1)+size,:]
        acc=part if acc is None else jnp.where(row>=bounds[d],part,acc)
    return acc
BLOCK=64
TALL=128
WIDTH=256
SLABS=range(WIDTH//128)
def taps(ref, base, weight, sign):
    acc=None
    for r in range(8):
        win=ref[pl.ds(base+r,TALL+32),:] if r==0 else ref[pl.ds(base+r,TALL+24),:]
        for a in range(5 if r==0 else 4):
            o=8*a+r
            t=weight(o if sign>0 else 2*HALF-o)*win[8*a:8*a+TALL]
            acc=t if acc is None else acc+t
    return acc

def cut(h): return slice(h*128,(h+1)*128)
def conv_fwd_kernel(bounds_ref, x_ref, wv_ref, w_ref, v_ref, out_ref, pad_ref, res_ref):
    b=pl.program_id(0)
    bounds=[bounds_ref[b,d] for d in range(DOCS+1)]
    length=v_ref.shape[1]; total=length+GAP*(DOCS+1)
    for lo in range(0,length,256):
        v_ref[0,lo:lo+256,:]=nt(x_ref[0,lo:lo+256,:],wv_ref[...])+w_ref[KW+1:KW+2,:]
    for h in SLABS:
        pad_ref[h,0:HALF,:]=jnp.zeros((HALF,128),F32)
        pad_ref[h,HALF+total:,:]=jnp.zeros((pad_ref.shape[1]-HALF-total,128),F32)
    spread([(pad_ref.at[h], lambda lo,n,h=h: v_ref[0,lo:lo+n,cut(h)]) for h in SLABS], bounds, length, BLOCK)
    def block(i,c):
        base=pl.multiple_of(i*TALL,TALL)
        for h in SLABS:
            res_ref[h,pl.ds(base,TALL),:]=taps(pad_ref.at[h], base, lambda s: w_ref[s:s+1,cut(h)], 1)
        return c
    lax.fori_loop(0,-(-total//TALL),block,0)
    for h in SLABS:
        for lo in range(0,length,BLOCK):
            out_ref[0,lo:lo+BLOCK,cut(h)]=collect(res_ref.at[h],bounds,lo,BLOCK)
def padded_rows(length):
    total=length+GAP*(DOCS+1)
    return -(-total//TALL)*TALL

def conv_fwd(bounds, x, w_v, w):
    B,L,D=x.shape
    rows=padded_rows(L)
    slab=pl.BlockSpec((1,L,WIDTH),lambda b,c,_:(b,0,c)); big=jax.ShapeDtypeStruct((B,L,D),F32)
    return pl.pallas_call(conv_fwd_kernel,grid_spec=pltpu.PrefetchScalarGridSpec(num_scalar_prefetch=1,grid=(B,D//WIDTH),
        in_specs=[pl.BlockSpec((1,L,D),lambda b,c,_:(b,0,0)),pl.BlockSpec((WIDTH,D),lambda b,c,_:(c,0)),
            pl.BlockSpec((SMALL,WIDTH),lambda b,c,_:(0,c))],
        out_specs=[slab,slab],
        scratch_shapes=[pltpu.VMEM((WIDTH//128,rows+2*HALF+8,128),F32),pltpu.VMEM((WIDTH//128,rows,128),F32)]),
        out_shape=[big,big],
        compiler_params=pltpu.CompilerParams(vmem_limit_bytes=60*2**20))(bounds,x,w_v,w)
def conv_bwd_kernel(bounds_ref, v_ref, al_ref, wo_ref, w_ref, x_ref, att_ref, q_ref, sums_ref, su_ref, *refs):
    dv_ref, gv_ref, vpad_ref, gpad_ref, res_ref, acc_ref, g_ref, sum_ref = refs[-8:]
    b=pl.program_id(1)
    bounds=[bounds_ref[b,d] for d in range(DOCS+1)]
    length=v_ref.shape[1]; total=length+GAP*(DOCS+1)
    for lo in range(0,length,256):
        g_ref[lo:lo+256,:]=nn(al_ref[0,lo:lo+256,:],wo_ref[...])
    for ref in (vpad_ref,gpad_ref):
        ref[0:HALF,:]=jnp.zeros((HALF,128),F32)
        ref[HALF+total:,:]=jnp.zeros((ref.shape[0]-HALF-total,128),F32)
    spread([(vpad_ref, lambda lo,n: v_ref[0,lo:lo+n,:]), (gpad_ref, lambda lo,n: g_ref[lo:lo+n,:])], bounds, length, BLOCK)
    @pl.when(b==0)
    def _():
        acc_ref[...]=jnp.zeros_like(acc_ref); gv_ref[...]=jnp.zeros_like(gv_ref); sum_ref[...]=jnp.zeros_like(sum_ref)
    def block(i,c):
        base=pl.multiple_of(i*BLOCK,BLOCK)
        here=vpad_ref[pl.ds(base+HALF,BLOCK),:]
        acc=None
        for r in range(8):
            n=5 if r==0 else 4
            win=gpad_ref[pl.ds(base+r,BLOCK+8*(n-1)),:]
            for a in range(n):
                s=2*HALF-(8*a+r)
                x=win[8*a:8*a+BLOCK]
                t=w_ref[s:s+1,:]*x
                acc=t if acc is None else acc+t
                p=(here*x).reshape(BLOCK//8,8,128)
                acc_ref[s]+=jnp.sum(p,axis=0)
        res_ref[pl.ds(base,BLOCK),:]=acc
        return c
    lax.fori_loop(0,-(-total//BLOCK),block,0)
    for lo in range(0,length,BLOCK*2):
        part=collect(res_ref,bounds,lo,BLOCK*2).T+att_ref[0,:,lo:lo+BLOCK*2]
        dv_ref[0,:,lo:lo+BLOCK*2]=part.astype(BF)
    dv=dv_ref[0]; depth=x_ref.shape[2]
    gv_ref[:,:depth]+=nn(dv,x_ref[0])
    sum_ref[...]+=jnp.sum(dv.astype(F32),axis=1,keepdims=True)
    @pl.when(b==pl.num_programs(1)-1)
    def _():
        rows=[jnp.sum(acc_ref[s],axis=0,keepdims=True) for s in range(KW)]
        side=jnp.concatenate(rows+[jnp.zeros((128-KW,128),F32)],axis=0).T
        lane=lax.broadcasted_iota(jnp.int32,(128,128),1)
        lines=su_ref.shape[1]
        side=side+jnp.where(lane==KW,sum_ref[:,:1],0.0)+jnp.where(lane==KW+1,q_ref[...],0.0)
        early=sums_ref[...].T
        for i in range(6): side=side+jnp.where(lane==KW+2+i,early[:,i:i+1],0.0)
        for i in range(lines): side=side+jnp.where(lane==KW+8+i,su_ref[:,i:i+1],0.0)
        gv_ref[:,depth:]=side
def conv_bwd(bounds, v, al, w_o, w, x, att, more, before, slabs, at):
    B,L,D=v.shape
    rows=padded_rows(L)
    sd=jax.ShapeDtypeStruct
    seq=pl.BlockSpec((1,L,D),lambda c,b,_:(b,0,0))
    feats=pl.BlockSpec((1,128,L),lambda c,b,_:(b,at+c,0))
    alias={11:0,12:1} if before else {}
    return pl.pallas_call(conv_bwd_kernel,grid_spec=pltpu.PrefetchScalarGridSpec(num_scalar_prefetch=1,grid=(slabs,B),
        in_specs=[pl.BlockSpec((1,L,128),lambda c,b,_:(b,0,at+c)),seq,
            pl.BlockSpec((D,128),lambda c,b,_:(0,at+c)),pl.BlockSpec((SMALL,128),lambda c,b,_:(0,at+c)),
            seq,feats,pl.BlockSpec((128,1),lambda c,b,_:(at+c,0)),pl.BlockSpec((8,128),lambda c,b,_:(0,at+c)),
            pl.BlockSpec((128,more[2].shape[1]),lambda c,b,_:(at+c,0))]+[pl.BlockSpec(memory_space=pl.ANY)]*len(before),
        out_specs=[feats,pl.BlockSpec((128,D+128),lambda c,b,_:(at+c,0))],
        scratch_shapes=[pltpu.VMEM((rows+2*HALF+8,128),F32)]*2+[pltpu.VMEM((rows,128),F32),pltpu.VMEM((KW,8,128),F32),
            pltpu.VMEM((L,128),F32),pltpu.VMEM((128,128),F32)]),
        out_shape=[sd((B,D,L),BF),sd((D,D+128),F32)],input_output_aliases={i-1:o for i,o in alias.items()},
        compiler_params=pltpu.CompilerParams(vmem_limit_bytes=60*2**20))(bounds,v,al,w_o,w,x,att,*more,*before)

def gelu_parts(x):
    size=jnp.abs(x)
    density=jnp.exp(-0.5*x*x)*0.3989422804014327
    t=1.0/(1.0+0.2316419*size)
    tail=density*(t*(0.319381530+t*(-0.356563782+t*(1.781477937+t*(-1.821255978+t*1.330274429)))))
    dist=jnp.where(x<0.0,tail,1.0-tail)
    return dist, x*density
def norm(v):
    mean=jnp.mean(v,axis=-1,keepdims=True); c=v-mean
    r=lax.rsqrt(jnp.mean(c*c,axis=-1,keepdims=True)+1e-5)
    return c*r, r
def norm_back(up,n,r,g):
    e=up*g
    return r*(e-jnp.mean(e,axis=-1,keepdims=True)-n*jnp.mean(e*n,axis=-1,keepdims=True))
def ffn_kernel(chunks, parts, ctx_ref,x_ref,cot_ref,wo_ref,wu_ref,*refs):
    wd_ref=refs[:chunks]
    (vec_ref,bu_ref,
               out_ref,normed_ref,hidden_ref,down_ref,up_ref,one_ref,att_ref,sums_ref,sumu_ref,slope_ref)=refs[chunks:]
    wu=wu_ref[...].reshape(-1,wu_ref.shape[-1]); width=wu.shape[0]//chunks
    size=x_ref.shape[0]//parts
    @pl.when(pl.program_id(0)==0)
    def _():
        sums_ref[...]=jnp.zeros_like(sums_ref); sumu_ref[...]=jnp.zeros_like(sumu_ref)
    v=lambda i: vec_ref[i:i+1,:]
    b_o,g1,s1,b_d,g2,s2=[v(KW+i) for i in range(2,8)]
    total=lambda a: jnp.sum(a,axis=0,keepdims=True)
    def steps(at):
        rows=slice(at*size,(at+1)*size); st={}
        def attend(): st["one"]=nt(ctx_ref[rows,:],wo_ref[...])
        def norm_one():
            st["n1"],st["r1"]=norm(x_ref[rows,:].astype(F32)+(st["one"]+b_o))
            st["normed"]=st["n1"]*g1+s1
            st["low"]=st["normed"].astype(BF); normed_ref[rows,:]=st["low"]
        def up(k):
            def go():
                if k>0:
                    add=nt(st["hid"],wd_ref[k-1][...]); st["down"]=add if k==1 else st["down"]+add
                if k<chunks: st["pre"]=nt(st["low"],wu[k*width:(k+1)*width,:])
            return go
        def gelu(k):
            part=slice(k*width,(k+1)*width)
            def go():
                pre=st["pre"]+bu_ref[:,part]
                dist,slope=gelu_parts(pre)
                slope_ref[rows,part]=dist+slope
                st["hid"]=(pre*dist).astype(BF); hidden_ref[rows,part]=st["hid"]
            return go
        def norm_two():
            n2,r2=norm(st["normed"]+(st["down"]+b_d))
            out_ref[rows,:]=(n2*g2+s2).astype(BF)
            cot=cot_ref[rows,:].astype(F32)
            st["back"]=norm_back(cot,n2,r2,g2)
            st["low2"]=st["back"].astype(BF); down_ref[rows,:]=st["low2"]
            sums_ref[3:6,:]+=jnp.concatenate([total(st["low2"].astype(F32)),total(cot*n2),total(cot)],axis=0)
        def back(k):
            def go():
                if k>0: st["back"]=st["back"]+nn(st["upl"],wu[(k-1)*width:k*width,:])
                if k<chunks: st["hg"]=nn(st["low2"],wd_ref[k][...])
            return go
        def scale(k):
            part=slice(k*width,(k+1)*width)
            def go():
                upl=(st["hg"]*slope_ref[rows,part]).astype(BF); up_ref[rows,part]=upl; st["upl"]=upl
                sumu_ref[:,part]+=total(upl.astype(F32))
            return go
        def norm_last():
            g_one=norm_back(st["back"],st["n1"],st["r1"],g1)
            one_ref[rows,:]=g_one
            al=g_one.astype(BF); att_ref[rows,:]=al
            sums_ref[0:3,:]+=jnp.concatenate([total(al.astype(F32)),total(st["back"]*st["n1"]),total(st["back"])],axis=0)
        out=[attend,norm_one]
        for k in range(chunks): out+=[up(k),gelu(k)]
        out+=[up(chunks),norm_two]
        for k in range(chunks): out+=[back(k),scale(k)]
        return out+[back(chunks),norm_last]
    lists=[steps(at) for at in range(parts)]
    for i in range(len(lists[0])+parts-1):
        for at in range(parts):
            if 0<=i-at<len(lists[at]): lists[at][i-at]()
def ffn(ctx,x,cot,wo,wu,wd,vec,bu,block=512,parts=2):
    chunks=len(wd)
    T,D=x.shape; F=bu.shape[1]
    row=lambda w: pl.BlockSpec((block,w),lambda i:(i,0))
    full=lambda a: pl.BlockSpec(a.shape,lambda i:(0,)*a.ndim,pipeline_mode=pl.Buffered(1))
    keep=lambda r,w: pl.BlockSpec((r,w),lambda i:(0,0))
    sd=jax.ShapeDtypeStruct
    return pl.pallas_call(functools.partial(ffn_kernel,chunks,parts),grid=(T//block,),
        in_specs=[row(D),row(D),row(D),full(wo),pl.BlockSpec((wu.shape[0],F//wu.shape[0],D),lambda i:(0,0,0),pipeline_mode=pl.Buffered(1)),*[full(a) for a in wd],pl.BlockSpec((SMALL,D),lambda i:(0,0)),full(bu)],
        out_specs=[row(D),row(D),row(F),row(D),row(F),row(D),row(D),keep(8,D),keep(1,F)],
        out_shape=[sd((T,D),BF),sd((T,D),BF),sd((T,F),BF),sd((T,D),BF),sd((T,F),BF),sd((T,D),F32),sd((T,D),BF),sd((8,D),F32),sd((1,F),F32)],
        scratch_shapes=[pltpu.VMEM((block,F),F32)],
        compiler_params=pltpu.CompilerParams(vmem_limit_bytes=60*2**20,dimension_semantics=("arbitrary",)),
    )(ctx,x,cot,wo,wu,*wd,vec,bu)


def across_rows(left_side, right_side):
    return lax.dot_general(left_side, right_side, (((0,), (0,)), ((), ())), preferred_element_type=F32)


def weight_kernel(own, up_ref, normed_ref, hidden_ref, down_ref, att_ref, ctx_ref, out_ref, acc_ref):
    depth=normed_ref.shape[1]; k=pl.program_id(1)
    wide_rows=up_ref.shape[1]; rows=down_ref.shape[1]; parts=hidden_ref.shape[1]//depth
    @pl.when(k==0)
    def _(): acc_ref[...]=jnp.zeros_like(acc_ref)
    for lo in range(0,wide_rows,rows):
        acc_ref[lo:lo+rows]+=across_rows(up_ref[:,lo:lo+rows],normed_ref[...])
    for i in range(parts):
        at=wide_rows+i*rows
        acc_ref[at:at+rows]+=across_rows(down_ref[...],hidden_ref[:,i*depth:(i+1)*depth])
    at=wide_rows+parts*rows
    acc_ref[at:at+rows]+=across_rows(att_ref[...],ctx_ref[...])
    @pl.when(k==pl.num_programs(1)-1)
    def _():
        many=rows//own; lines=wide_rows//many
        out_ref[:,:lines]=acc_ref[:wide_rows].reshape(many,lines,depth).astype(BF)
        narrow=[acc_ref[wide_rows+i*rows:wide_rows+(i+1)*rows].reshape(many,own,depth) for i in range(parts+1)]
        narrow.append(jnp.zeros((many,out_ref.shape[1]-lines-(parts+1)*own,depth),F32))
        out_ref[:,lines:]=jnp.concatenate(narrow,axis=1).astype(BF)
def weight_grads(own, up, normed, hidden, down, att, ctx):
    T,D=normed.shape; F=up.shape[1]; halves=2; many=D//own//halves; block=512
    R=-(-(F//D*2+1)*own//16)*16
    if own%8:
        by=lambda a: a.reshape(D//own,-1,D)
        pieces=[by(across_rows(up,normed))]+[by(across_rows(down,hidden[:,i*D:(i+1)*D])) for i in range(F//D)]
        pieces.append(by(across_rows(att,ctx)))
        pieces.append(jnp.zeros((D//own,R-(F//D*2+1)*own,D),F32))
        return jnp.concatenate(pieces,axis=1).astype(BF)
    col=lambda w: pl.BlockSpec((block,w),lambda h,k:(k,h)); row=lambda w: pl.BlockSpec((block,w),lambda h,k:(k,0))
    return pl.pallas_call(functools.partial(weight_kernel,own),grid=(halves,T//block),
        in_specs=[col(F//halves),row(D),row(F),col(D//halves),col(D//halves),row(D)],
        out_specs=pl.BlockSpec((many,R,D),lambda h,k:(h,0,0)),
        out_shape=jax.ShapeDtypeStruct((D//own,R,D),BF),
        scratch_shapes=[pltpu.VMEM((many*own*(F//D*2+1),D),F32)],
        compiler_params=pltpu.CompilerParams(vmem_limit_bytes=60*2**20))(up,normed,hidden,down,att,ctx)


def digits():
    found = []
    for axis in ("wide", "narrow"):
        stride = lax.axis_size(axis) // 2
        while stride >= 1:
            found.append((axis, stride))
            stride //= 2
    return found


def link_order(number):
    count = len(digits())
    if lax.axis_size("wide") == 8 and lax.axis_size("narrow") == 4:
        return [(4, 2, 3, 1, 0), (4, 3, 1, 2, 0), (4, 1, 2, 3, 0)][number]
    return tuple(range(count - 1, -1, -1))


def exchange(values, axis, stride):
    return lax.ppermute(values, axis, [(i, i ^ stride) for i in range(lax.axis_size(axis))])


def digit_of(axis, stride):
    return (lax.axis_index(axis) // stride) % 2


def gather_rows(shards):
    places = digits()
    held = [shard.reshape((1,) * len(places) + shard.shape) for shard in shards]
    passed = []
    for step in range(len(places)):
        for number, values in enumerate(held):
            dim = link_order(number)[::-1][step]
            mine = digit_of(*places[dim])
            got = exchange(values, *places[dim])
            first = jnp.where(mine == 0, values, got)
            second = jnp.where(mine == 0, got, values)
            held[number] = jnp.concatenate([first, second], dim)
        held = list(lax.optimization_barrier(tuple(held)))
        passed.append(held[0])
    return [values.reshape((-1,) + values.shape[-2:]) for values in held], passed


def scatter_start(whole, own):
    return whole.reshape(whole.shape[:-2] + (2,) * len(digits()) + (own, whole.shape[-1]))


def scatter_step(held, number, step):
    places = digits()
    dim = link_order(number)[step] + held.ndim - 2 - len(places)
    place = places[link_order(number)[step]]
    mine = digit_of(*place)
    keep = lax.dynamic_slice_in_dim(held, mine, 1, dim).astype(F32)
    send = lax.dynamic_slice_in_dim(held, 1 - mine, 1, dim).astype(BF)
    return keep + exchange(send, *place).astype(F32)


def scatter_rest(held, number, step):
    for later in range(step, len(digits())):
        held = scatter_step(held, number, later)
    return held.reshape(held.shape[: held.ndim - 2 - len(digits())] + held.shape[-2:])


def shards(
    inputs,
    tok_landmark,
    landmark_doc,
    w_query,
    b_query,
    w_key,
    w_value,
    b_value,
    conv_weight,
    w_out,
    b_out,
    gain_one,
    shift_one,
    w_up,
    b_up,
    w_down,
    b_down,
    gain_two,
    shift_two,
    cotangent,
):
    batch_rows, sequence_length, feature_width = inputs.shape
    group_count = lax.axis_size("wide") * lax.axis_size("narrow")
    own = feature_width // group_count
    tokens = batch_rows * sequence_length
    lines = b_up.shape[0] // own
    vectors = (b_query, b_value, b_out, gain_one, shift_one, b_down, gain_two, shift_two)
    flat = 0
    for place, vector in enumerate(vectors + (b_up,)):
        before = place * own
        flat = flat + jnp.pad(vector, (before, (8 + lines) * own - before - vector.shape[0]))
    small = jnp.concatenate([conv_weight, flat.reshape(8 + lines, own)])
    small = jnp.pad(small.T, ((0, 0), (0, 128 - small.shape[0])))
    (gathered_v, w_q, w_k), passed = gather_rows(
        [jnp.concatenate([w_value.T, small], axis=1), w_query.T, w_key.T]
    )
    w_q = w_q.reshape(feature_width, feature_width)
    w_k = w_k.reshape(feature_width, feature_width)
    gathered_v = gathered_v.reshape(feature_width, feature_width + 128)
    w_v = gathered_v[:, :feature_width]
    small = gathered_v[:, feature_width:]
    b_u = jnp.moveaxis(small[:, KW + 8 : KW + 8 + lines].reshape(group_count, own, lines), 1, 2)
    b_u = b_u.reshape(1, -1).astype(F32)
    small = small.astype(F32).T
    ff_count = w_down.shape[0] // feature_width
    w_out, w_up, w_down, _ = lax.optimization_barrier((w_out, w_up, w_down, passed[0]))
    shard = jnp.concatenate(
        [w_up.T, w_out.T] + [w_down[i * feature_width : (i + 1) * feature_width].T for i in range(ff_count)]
    )
    gathered = lax.all_gather(shard, ("wide", "narrow"), axis=0)
    w_o = gathered[:, own * lines : own * (1 + lines)].reshape(feature_width, feature_width)
    w_u = gathered if own * lines % 16 == 0 else gathered[:, : own * lines].reshape(1, -1, feature_width)
    w_d = [
        gathered[:, own * (1 + lines + i) : own * (2 + lines + i)].reshape(feature_width, feature_width)
        for i in range(ff_count)
    ]
    member = tok_landmark[:, None, :] == jnp.arange(LM)[None, :, None]
    means = jnp.einsum("bjt,bti->bji", member.astype(BF), inputs, preferred_element_type=F32)
    means = means / jnp.sum(member, axis=2)[..., None].astype(F32)
    doc = jnp.sum(jnp.where(member, landmark_doc[:, :, None], 0), axis=1)
    bounds = jnp.sum(doc[:, None, :] < jnp.arange(DOCS + 1)[None, :, None], axis=2).astype(jnp.int32)
    rows_low = inputs.reshape(tokens, feature_width)
    value_rows, conv_part = conv_fwd(bounds, inputs, w_v, small)
    q, k, v, k1, k3, inv, stash, landmarks, context = att_fwd(
        inputs, means, w_q, w_k, w_v, small, tok_landmark, landmark_doc, conv_part
    )
    context = context.reshape(tokens, feature_width)
    layer_out, normed, hidden, down_low, up_low, grad_one, att_low, sums, sums_up = ffn(
        context, rows_low, cotangent.reshape(tokens, feature_width), w_o, w_u, w_d, small, b_u
    )
    grads = weight_grads(own, up_low, normed, hidden, down_low, att_low, context)
    share = lax.psum_scatter(grads, ("wide", "narrow"), scatter_dimension=0, tiled=True)[0]
    w_plain = w_o.T
    att_low = att_low.reshape(inputs.shape)
    dq, dk, dv, grad_qk, sum_q = att_bwd(
        inputs, att_low, w_plain, q, k, v, k1, k3, inv, stash, landmarks, tok_landmark
    )
    more = (sum_q, sums, sums_up.reshape(feature_width, lines))
    moving = scatter_start(grad_qk, own)
    calls, before = 3, ()
    slabs = feature_width // 128 // calls
    for call in range(calls):
        moved = scatter_step(moving, 1, call)
        before = conv_bwd(
            bounds, value_rows, att_low, w_o, small, inputs, dv, more, before, slabs, call * slabs
        )
        before, att_low, moving = lax.optimization_barrier((tuple(before), att_low, moved))
    dv, grad_v = before
    input_grad = grad_one.reshape(inputs.shape)
    moved = scatter_start(grad_v, own)
    turns = [(dq, w_q), (dk, w_k), (dv, w_v)]
    for number in range(len(digits())):
        moved = scatter_step(moved, 0, number)
        if calls + number < len(digits()):
            moving = scatter_step(moving, 1, calls + number)
        if number < len(turns):
            grad, weight = turns[number]
            moved, moving, grad, input_grad = lax.optimization_barrier((moved, moving, grad, input_grad))
            input_grad = input_grad + jnp.einsum("bot,oi->bti", grad, weight, preferred_element_type=F32)
        elif number == len(digits()) - 2:
            moved, share, input_grad = lax.optimization_barrier((moved, share, input_grad))
    share_qk = moving.reshape(moving.shape[:1] + moving.shape[-2:])
    share_v = moved.reshape(moved.shape[-2:])
    late = share_v[:, feature_width:]
    share = share.astype(F32)
    share_down = share[own * lines : 2 * own * lines].reshape(ff_count, own, feature_width)
    share_out = share[2 * own * lines : 2 * own * lines + own]
    return (
        layer_out.reshape(inputs.shape),
        input_grad,
        share_qk[0].T,
        late[:, KW + 1],
        share_qk[1].T,
        share_v[:, :feature_width].T,
        late[:, KW],
        late[:, :KW].T,
        share_out.T,
        late[:, KW + 2],
        late[:, KW + 3],
        late[:, KW + 4],
        share[: own * lines].T,
        late[:, KW + 8 : KW + 8 + lines].reshape(-1),
        jnp.moveaxis(share_down, 1, 2).reshape(-1, own),
        late[:, KW + 5],
        late[:, KW + 6],
        late[:, KW + 7],
    )


def solution(mesh):
    return jax.shard_map(
        shards,
        mesh=mesh,
        in_specs=(
            P(("wide", "narrow"), None, None),
            P(("wide", "narrow"), None),
            P(("wide", "narrow"), None),
            P(None, ("wide", "narrow")),
            P(("wide", "narrow")),
            P(None, ("wide", "narrow")),
            P(None, ("wide", "narrow")),
            P(("wide", "narrow")),
            P(None, ("wide", "narrow")),
            P(None, ("wide", "narrow")),
            P(("wide", "narrow")),
            P(("wide", "narrow")),
            P(("wide", "narrow")),
            P(None, ("wide", "narrow")),
            P(("wide", "narrow")),
            P(None, ("wide", "narrow")),
            P(("wide", "narrow")),
            P(("wide", "narrow")),
            P(("wide", "narrow")),
            P(("wide", "narrow"), None, None),
        ),
        out_specs=(
            P(("wide", "narrow"), None, None),
            P(("wide", "narrow"), None, None),
            P(None, ("wide", "narrow")),
            P(("wide", "narrow")),
            P(None, ("wide", "narrow")),
            P(None, ("wide", "narrow")),
            P(("wide", "narrow")),
            P(None, ("wide", "narrow")),
            P(None, ("wide", "narrow")),
            P(("wide", "narrow")),
            P(("wide", "narrow")),
            P(("wide", "narrow")),
            P(None, ("wide", "narrow")),
            P(("wide", "narrow")),
            P(None, ("wide", "narrow")),
            P(("wide", "narrow")),
            P(("wide", "narrow")),
            P(("wide", "narrow")),
        ),
        check_vma=False,
    )
```

```python
import functools

import jax
import jax.numpy as jnp
from jax import lax
from jax.experimental import pallas as pl
from jax.experimental.pallas import tpu as pltpu
from jax.sharding import PartitionSpec as P

BF = jnp.bfloat16
F32 = jnp.float32
HW=64; LM=64; NEWTON=6; GH=12; GW=GH*HW
CHUNK=256
KW=33
SMALL=48
def nt(a,b): return lax.dot_general(a,b,(((1,),(1,)),((),())),preferred_element_type=F32)
def nn(a,b): return lax.dot_general(a,b,(((1,),(0,)),((),())),preferred_element_type=F32)
def split(a):
    hi=a.astype(BF); return hi,(a-hi.astype(F32)).astype(BF)
def wide(a):
    hi,lo=split(a); return jnp.concatenate([hi,hi,lo],axis=1)
def tall(b):
    hi,lo=split(b); return jnp.concatenate([hi,lo,hi],axis=0)
def mm3(a,b): return nn(wide(a),tall(b))
def eye(c):
    row=lax.broadcasted_iota(jnp.int32,(LM,2*LM),0); col=lax.broadcasted_iota(jnp.int32,(LM,2*LM),1)
    return jnp.where((row==col)|(row+LM==col),c,0.0)
def beside(a):
    return [jnp.concatenate([a[i],a[i+1]],axis=1) for i in range(0,len(a),2)]
def blocks(b):
    lane=lax.broadcasted_iota(jnp.int32,(1,2*LM),1)
    first=jnp.where(lane<LM,1.0,0.0).astype(BF); second=jnp.where(lane<LM,0.0,1.0).astype(BF)
    hi,lo=split(b)
    return jnp.concatenate([hi*first,hi*second,lo*first,lo*second,hi*first,hi*second],axis=0)
def mmb(a,b): return nn(wide(a),blocks(b))
def weave(first, second):
    done=0
    for i,step in enumerate(first):
        step()
        upto=(i+1)*len(second)//len(first)
        for other in second[done:upto]: other()
        done=upto
def att_fwd_kernel(x_ref,mean_ref,wq_ref,wk_ref,wv_ref,vec_ref,tok_ref,ldc_ref,ldr_ref,conv_ref,
               q_ref,k_ref,v_ref,k1_ref,k3_ref,inv_ref,stash_ref,small_ref,ctx_ref,
               qlo_ref,klo_ref,score_ref,bias_ref):
    T=x_ref.shape[1]
    heads=range(GH); chunks=[slice(c,c+CHUNK) for c in range(0,T,CHUNK)]
    rows=[slice(h*HW,(h+1)*HW) for h in heads]
    scale=HW**-0.25
    bq=vec_ref[KW:KW+1,:].T; bv=vec_ref[KW+1:KW+2,:].T
    ldc=ldc_ref[0]
    for cs in chunks:
        member=lax.broadcasted_iota(jnp.int32,(LM,CHUNK),0)==tok_ref[0,:,cs]
        doc=jnp.sum(jnp.where(member,ldc,0),axis=0,keepdims=True)
        bias_ref[:,cs]=jnp.where(doc==ldc,0.0,-1e30)
    mean=jnp.concatenate(split(mean_ref[0]),axis=0)
    def land(w_ref):
        both=nt(w_ref[...],mean)
        return both[:,:LM]+both[:,LM:]
    lqt=(land(wq_ref)+bq)*scale; lkt=land(wk_ref)*scale
    lq=[lqt[r].T for r in rows]; lk=[lkt[r].T for r in rows]
    lqw=[wide(a) for a in lq]; lkw=[wide(a) for a in lk]
    allow2=ldc==ldr_ref[0]
    k2=[];zt=[]
    for h in heads:
        sc=jnp.where(allow2,nn(lqw[h],tall(lkt[rows[h]])),-1e30)
        e=jnp.exp(sc-jnp.max(sc,axis=1,keepdims=True))
        k2.append(e/jnp.sum(e,axis=1,keepdims=True))
        zt.append(k2[h]*(1.0/jnp.sum(k2[h]*k2[h])))
    pairs=range(GH//2)
    state={"zt":beside(zt)}
    k2tb=[blocks(a) for a in beside([a.T for a in k2])]
    def newton(n):
        def one():
            state["p"]=[nn(wide(state["zt"][i]),k2tb[i]) for i in pairs]
            state["pw"]=[wide(a) for a in state["p"]]
        def two(): state["b"]=[eye(15.0)-nn(state["pw"][i],blocks(eye(7.0)-state["p"][i])) for i in pairs]
        def three(): state["c"]=[eye(13.0)-nn(state["pw"][i],blocks(state["b"][i])) for i in pairs]
        def four():
            for i in pairs:
                for place,key in enumerate(("p","b","c","zt")): stash_ref[0,i,4*n+place]=state[key][i]
            state["zt"]=[0.25*mmb(state["c"][i],state["zt"][i]) for i in pairs]
        return [one,two,three,four]
    chain=[step for n in range(NEWTON) for step in newton(n)]
    side=[]
    def project(cs):
        x=x_ref[0,cs,:]
        def q():
            a=(nt(wq_ref[...],x)+bq)*scale
            hi,lo=split(a); q_ref[0,:,cs]=hi; qlo_ref[:,cs]=lo
        def k():
            a=nt(wk_ref[...],x)*scale
            hi,lo=split(a); k_ref[0,:,cs]=hi; klo_ref[:,cs]=lo
        def v(): v_ref[0,:,cs]=(nt(wv_ref[...],x)+bv).astype(BF)
        return [q,k,v]
    tops=[None]*GH; sums=[None]*GH; r=[None]*GH
    def lanes(a): return [a[:,i:i+128] for i in range(0,CHUNK,128)]
    def first(h,cs):
        def go():
            hi=q_ref[0,rows[h],cs]
            s=nn(lkw[h],jnp.concatenate([hi,qlo_ref[rows[h],cs],hi],axis=0))+bias_ref[:,cs]
            e=jnp.exp(s-jnp.max(s,axis=0,keepdims=True))
            e=e.astype(BF); k1_ref[0,rows[h],cs]=e
            inv_ref[0,0,h:h+1,cs]=1.0/jnp.sum(e.astype(F32),axis=0,keepdims=True)
        return go
    def third(h,cs):
        def go():
            hi=k_ref[0,rows[h],cs]
            s=nn(lqw[h],jnp.concatenate([hi,klo_ref[rows[h],cs],hi],axis=0))+bias_ref[:,cs]
            score_ref[rows[h],cs]=s
            for a in lanes(s): tops[h]=a if tops[h] is None else jnp.maximum(tops[h],a)
        return go
    def raised(h,cs):
        def go():
            if cs.start==0: tops[h]=jnp.max(tops[h],axis=1,keepdims=True)
            e=jnp.exp(score_ref[rows[h],cs]-tops[h])
            e=e.astype(BF); k3_ref[0,rows[h],cs]=e
            for a in lanes(e.astype(F32)): sums[h]=a if sums[h] is None else sums[h]+a
        return go
    def gathered(h):
        def go():
            sums[h]=1.0/jnp.sum(sums[h],axis=1,keepdims=True)
            r[h]=nt(k3_ref[0,rows[h]],v_ref[0,rows[h]])*sums[h]
        return go
    for cs in chunks: side+=project(cs)
    for h in heads:
        side+=[third(h,cs) for cs in chunks]
        side+=[raised(h,cs) for cs in chunks]+[gathered(h)]
        side+=[first(h,cs) for cs in chunks]
    weave(chain,side)
    uts=[]
    for h in heads:
        zt=state["zt"][h//2][:,h%2*LM:(h%2+1)*LM]
        u=mm3(zt.T,r[h])
        small_ref[0,h,0]=jnp.concatenate([lq[h],lk[h]],axis=1)
        small_ref[0,h,1]=jnp.concatenate([k2[h],zt],axis=1)
        small_ref[0,h,2]=jnp.concatenate([r[h],u],axis=1)
        small_ref[0,h,3]=jnp.broadcast_to(sums[h],(LM,128))
        uts.append(u.T.astype(BF))
    for cs in chunks:
        mixed=jnp.concatenate([nn(uts[h],k1_ref[0,rows[h],cs])*inv_ref[0,0,h:h+1,cs] for h in heads],axis=0)
        ctx_ref[0,cs,:]=(mixed.T+conv_ref[0,cs,:]).astype(BF)
def att_specs(D,T):
    seq=lambda s: pl.BlockSpec((1,)+s,lambda g,b:(b,)+(0,)*len(s))
    wsp=pl.BlockSpec((GW,D),lambda g,b:(g,0)); bsp=pl.BlockSpec((GW,1),lambda g,b:(g,0))
    rows=pl.BlockSpec((1,GW,T),lambda g,b:(b,g,0)); cols=pl.BlockSpec((1,T,GW),lambda g,b:(b,0,g))
    sq=lambda m,n: pl.BlockSpec((1,m,n,LM,2*LM),lambda g,b:(b,g,0,0,0))
    turned=pl.BlockSpec((1,1,-(-GH//8)*8,T),lambda g,b:(b,g,0,0))
    return seq,wsp,bsp,rows,cols,sq,turned
def att_fwd(x,mean,wq,wk,wv,vec,tok,ld,conv):
    B,T,D=x.shape; G=D//GW; H=D//HW
    seq,wsp,bsp,rows,cols,sq,turned=att_specs(D,T)
    sd=jax.ShapeDtypeStruct; big=sd((B,D,T),BF)
    return pl.pallas_call(att_fwd_kernel,grid=(G,B),
        in_specs=[seq((T,D)),seq((LM,D)),wsp,wsp,wsp,pl.BlockSpec((SMALL,GW),lambda g,b:(0,g)),seq((1,T)),seq((LM,1)),seq((1,LM)),cols],
        out_specs=[rows]*5+[turned,sq(GH//2,4*NEWTON),sq(GH,4),cols],
        out_shape=[big]*5+[sd((B,G,-(-GH//8)*8,T),F32),sd((B,H//2,4*NEWTON,LM,2*LM),F32),sd((B,H,4,LM,2*LM),F32),sd((B,T,D),BF)],
        scratch_shapes=[pltpu.VMEM((GW,T),BF)]*2+[pltpu.VMEM((GW,T),F32),pltpu.VMEM((LM,T),F32)],
        compiler_params=pltpu.CompilerParams(vmem_limit_bytes=60*2**20))(
            x,mean,wq,wk,wv,vec,tok[:,None,:],ld[:,:,None],ld[:,None,:],conv)
def att_bwd_kernel(x_ref,al_ref,wo_ref,q_ref,k_ref,v_ref,k1_ref,k3_ref,inv_ref,stash_ref,small_ref,tok_ref,
               dq_ref,dk_ref,dv_ref,gqk_ref,sq_ref,
               g_ref,ds1_ref,ds3_ref,hot_ref):
    T=x_ref.shape[1]
    heads=range(GH); chunks=[slice(c,c+CHUNK) for c in range(0,T,CHUNK)]
    rows=[slice(h*HW,(h+1)*HW) for h in heads]
    scale=HW**-0.25
    for cs in chunks:
        member=lax.broadcasted_iota(jnp.int32,(LM,CHUNK),0)==tok_ref[0,:,cs]
        hot_ref[:,cs]=jnp.where(member,1.0,0.0).astype(BF)
    per=1.0/nt(jnp.ones((8,T),BF),hot_ref[...])[0:1]
    left=lambda i: [small_ref[0,h,i,:,:LM] for h in heads]
    right=lambda i: [small_ref[0,h,i,:,LM:] for h in heads]
    lq,lk,k2,zt,r,u=left(0),right(0),left(1),right(1),left(2),right(2)
    inv=[small_ref[0,h,3,:,:LM] for h in heads]
    ub=[a.astype(BF) for a in u]
    def upstream(cs):
        def go():
            a=nt(wo_ref[...],al_ref[0,cs,:])
            for h in heads: g_ref[rows[h],cs]=(a[rows[h]]*inv_ref[0,0,h:h+1,cs]).astype(BF)
        return go
    def first(h,cs):
        def go():
            k1=k1_ref[0,rows[h],cs].astype(F32)
            t=k1*nn(ub[h],g_ref[rows[h],cs])
            ds1_ref[rows[h],cs]=(t-k1*(jnp.sum(t,axis=0,keepdims=True)*inv_ref[0,0,h:h+1,cs])).astype(BF)
        return go
    for cs in chunks: upstream(cs)()
    du=[nt(k1_ref[0,rows[h]],g_ref[rows[h],:]) for h in heads]
    dr=[mm3(zt[h],du[h]) for h in heads]
    state={"dz":beside([mm3(du[h],r[h].T) for h in heads]),"dk2":[None]*(GH//2)}
    drs=[(dr[h]*inv[h]) for h in heads]
    drb=[a.astype(BF) for a in drs]; drt=[a.T.astype(BF) for a in drs]
    delta=[jnp.sum(drb[h].astype(F32)*r[h],axis=1,keepdims=True) for h in heads]
    dlq=[None]*GH; dlk=[None]*GH
    def third(h,cs):
        def go():
            d=k3_ref[0,rows[h],cs].astype(F32)*(nn(drb[h],v_ref[0,rows[h],cs])-delta[h])
            ds3_ref[rows[h],cs]=d.astype(BF)
        return go
    def values(cs):
        def go():
            a=jnp.concatenate([nn(drt[h],k3_ref[0,rows[h],cs]) for h in heads],axis=0)
            dv_ref[0,:,cs]=a
        return go
    def to_lk(h):
        def go(): dlk[h]=nt(ds1_ref[rows[h],:],q_ref[0,rows[h]])
        return go
    def to_lq(h):
        def go(): dlq[h]=nt(ds3_ref[rows[h],:],k_ref[0,rows[h]])
        return go
    @pl.when(pl.program_id(1)==0)
    def _():
        for ref in (gqk_ref,sq_ref): ref[...]=jnp.zeros_like(ref)
    side=[]
    for h in heads: side+=[third(h,cs) for cs in chunks]+[to_lq(h)]+[first(h,cs) for cs in chunks]+[to_lk(h)]
    side+=[values(cs) for cs in chunks]
    pairs=range(GH//2)
    k2t=[a.T for a in k2]; k2tw=[wide(a) for a in beside(k2t)]
    def newton(n):
        def one():
            state["p"],state["b"],state["c"],state["zt"]=[[stash_ref[0,i,4*n+place] for i in pairs] for place in range(4)]
            state["gz"]=[0.25*d for d in state["dz"]]
            state["dc"]=[mmb(state["zt"][i],state["gz"][i]) for i in pairs]
            state["pw"]=[wide(m) for m in state["p"]]
        def two(): state["db"]=[nn(state["pw"][i],blocks(state["dc"][i])) for i in pairs]
        def three():
            da=[nn(state["pw"][i],blocks(state["db"][i])) for i in pairs]
            state["dp"]=[mmb(state["db"][i],eye(7.0)-state["p"][i])-mmb(state["dc"][i],state["b"][i])-da[i] for i in pairs]
        def four():
            for i in pairs:
                t=mmb(state["dp"][i],state["zt"][i])
                state["dk2"][i]=t if state["dk2"][i] is None else state["dk2"][i]+t
            state["dz"]=[mmb(state["gz"][i],state["c"][i])+nn(k2tw[i],blocks(state["dp"][i])) for i in pairs]
        return [one,two,three,four]
    chain=[step for n in reversed(range(NEWTON)) for step in newton(n)]
    weave(chain,side)
    lhq=[];lhk=[]
    for h in heads:
        half=slice(h%2*LM,(h%2+1)*LM)
        i2=1.0/jnp.sum(k2[h]*k2[h]); dz=state["dz"][h//2][:,half]
        d=state["dk2"][h//2][:,half]+i2*dz.T-k2[h]*(2.0*i2*i2*jnp.sum(dz*k2t[h]))
        d=k2[h]*(d-jnp.sum(k2[h]*d,axis=1,keepdims=True))
        dlqh=dlq[h]+mm3(d,lk[h]); dlkh=dlk[h]+mm3(d.T,lq[h])
        lhq.append(jnp.concatenate([lk[h].T,dlqh.T*per],axis=1).astype(BF))
        lhk.append(jnp.concatenate([lq[h].T,dlkh.T*per],axis=1).astype(BF))
    for cs in chunks:
        hot=hot_ref[:,cs]
        for lh,ds_ref,out_ref in ((lhq,ds1_ref,dq_ref),(lhk,ds3_ref,dk_ref)):
            for h in heads:
                a=nn(lh[h],jnp.concatenate([ds_ref[rows[h],cs],hot],axis=0))
                out_ref[0,rows[h],cs]=(a*scale).astype(BF)
    dq=dq_ref[0]
    gqk_ref[0]+=nn(dq,x_ref[0]); gqk_ref[1]+=nn(dk_ref[0],x_ref[0])
    sq_ref[...]+=jnp.sum(dq.astype(F32),axis=1,keepdims=True)
def att_bwd(x,al,wo,q,k,v,k1,k3,inv,stash,small,tok):
    B,T,D=x.shape; G=D//GW
    seq,wsp,bsp,rows,cols,sq,turned=att_specs(D,T)
    sd=jax.ShapeDtypeStruct; big=sd((B,D,T),BF)
    return pl.pallas_call(att_bwd_kernel,grid=(G,B),
        in_specs=[seq((T,D)),seq((T,D)),wsp]+[rows]*5+[turned,sq(GH//2,4*NEWTON),sq(GH,4),seq((1,T))],
        out_specs=[rows]*3+[pl.BlockSpec((2,GW,D),lambda g,b:(0,g,0)),bsp],
        out_shape=[big,big,sd((B,D,T),F32),sd((2,D,D),F32),sd((D,1),F32)],
        scratch_shapes=[pltpu.VMEM((GW,T),BF)]*3+[pltpu.VMEM((LM,T),BF)],
        compiler_params=pltpu.CompilerParams(vmem_limit_bytes=60*2**20))(
            x,al,wo,q,k,v,k1,k3,inv,stash,small,tok[:,None,:])

HALF=16; DOCS=4; GAP=16
def spread(places, bounds, length, step):
    total=length+GAP*(DOCS+1)
    ids=lax.broadcasted_iota(jnp.int32,(step,128),0)
    for p0 in range(0,total,step):
        size=min(step,total-p0)
        sums=[None]*len(places)
        for d in range(DOCS):
            s0=p0-GAP*(d+1)
            lo=max(s0,0); hi=min(s0+size,length)
            if hi<=lo: continue
            row=ids[:hi-lo]+lo
            inside=(row>=bounds[d])&(row<bounds[d+1])
            for i,(_,get) in enumerate(places):
                part=jnp.where(inside,get(lo,hi-lo),0.0)
                pads=[]
                if lo>s0: pads.append(jnp.zeros((lo-s0,128),F32))
                pads.append(part)
                if s0+size>hi: pads.append(jnp.zeros((s0+size-hi,128),F32))
                part=jnp.concatenate(pads,0) if len(pads)>1 else part
                sums[i]=part if sums[i] is None else sums[i]+part
        for i,(dst,_) in enumerate(places):
            dst[HALF+p0:HALF+p0+size,:]=jnp.zeros((size,128),F32) if sums[i] is None else sums[i]
def collect(src, bounds, lo, size):
    row=lax.broadcasted_iota(jnp.int32,(size,128),0)+lo
    acc=None
    for d in range(DOCS):
        part=src[lo+GAP*(d+1):lo+GAP*(d+1)+size,:]
        acc=part if acc is None else jnp.where(row>=bounds[d],part,acc)
    return acc
BLOCK=64
TALL=128
WIDTH=256
SLABS=range(WIDTH//128)
def taps(ref, base, weight, sign):
    acc=None
    for r in range(8):
        win=ref[pl.ds(base+r,TALL+32),:] if r==0 else ref[pl.ds(base+r,TALL+24),:]
        for a in range(5 if r==0 else 4):
            o=8*a+r
            t=weight(o if sign>0 else 2*HALF-o)*win[8*a:8*a+TALL]
            acc=t if acc is None else acc+t
    return acc

def cut(h): return slice(h*128,(h+1)*128)
def conv_fwd_kernel(bounds_ref, x_ref, wv_ref, w_ref, v_ref, out_ref, pad_ref, res_ref):
    b=pl.program_id(0)
    bounds=[bounds_ref[b,d] for d in range(DOCS+1)]
    length=v_ref.shape[1]; total=length+GAP*(DOCS+1)
    for lo in range(0,length,256):
        v_ref[0,lo:lo+256,:]=nt(x_ref[0,lo:lo+256,:],wv_ref[...])+w_ref[KW+1:KW+2,:]
    for h in SLABS:
        pad_ref[h,0:HALF,:]=jnp.zeros((HALF,128),F32)
        pad_ref[h,HALF+total:,:]=jnp.zeros((pad_ref.shape[1]-HALF-total,128),F32)
    spread([(pad_ref.at[h], lambda lo,n,h=h: v_ref[0,lo:lo+n,cut(h)]) for h in SLABS], bounds, length, BLOCK)
    def block(i,c):
        base=pl.multiple_of(i*TALL,TALL)
        for h in SLABS:
            res_ref[h,pl.ds(base,TALL),:]=taps(pad_ref.at[h], base, lambda s: w_ref[s:s+1,cut(h)], 1)
        return c
    lax.fori_loop(0,-(-total//TALL),block,0)
    for h in SLABS:
        for lo in range(0,length,BLOCK):
            out_ref[0,lo:lo+BLOCK,cut(h)]=collect(res_ref.at[h],bounds,lo,BLOCK)
def padded_rows(length):
    total=length+GAP*(DOCS+1)
    return -(-total//TALL)*TALL

def conv_fwd(bounds, x, w_v, w):
    B,L,D=x.shape
    rows=padded_rows(L)
    slab=pl.BlockSpec((1,L,WIDTH),lambda b,c,_:(b,0,c)); big=jax.ShapeDtypeStruct((B,L,D),F32)
    return pl.pallas_call(conv_fwd_kernel,grid_spec=pltpu.PrefetchScalarGridSpec(num_scalar_prefetch=1,grid=(B,D//WIDTH),
        in_specs=[pl.BlockSpec((1,L,D),lambda b,c,_:(b,0,0)),pl.BlockSpec((WIDTH,D),lambda b,c,_:(c,0)),
            pl.BlockSpec((SMALL,WIDTH),lambda b,c,_:(0,c))],
        out_specs=[slab,slab],
        scratch_shapes=[pltpu.VMEM((WIDTH//128,rows+2*HALF+8,128),F32),pltpu.VMEM((WIDTH//128,rows,128),F32)]),
        out_shape=[big,big],
        compiler_params=pltpu.CompilerParams(vmem_limit_bytes=60*2**20))(bounds,x,w_v,w)
def conv_bwd_kernel(bounds_ref, v_ref, al_ref, wo_ref, w_ref, x_ref, att_ref, q_ref, sums_ref, su_ref, *refs):
    dv_ref, gv_ref, vpad_ref, gpad_ref, res_ref, acc_ref, g_ref, sum_ref = refs[-8:]
    b=pl.program_id(1)
    bounds=[bounds_ref[b,d] for d in range(DOCS+1)]
    length=v_ref.shape[1]; total=length+GAP*(DOCS+1)
    for lo in range(0,length,256):
        g_ref[lo:lo+256,:]=nn(al_ref[0,lo:lo+256,:],wo_ref[...])
    for ref in (vpad_ref,gpad_ref):
        ref[0:HALF,:]=jnp.zeros((HALF,128),F32)
        ref[HALF+total:,:]=jnp.zeros((ref.shape[0]-HALF-total,128),F32)
    spread([(vpad_ref, lambda lo,n: v_ref[0,lo:lo+n,:]), (gpad_ref, lambda lo,n: g_ref[lo:lo+n,:])], bounds, length, BLOCK)
    @pl.when(b==0)
    def _():
        acc_ref[...]=jnp.zeros_like(acc_ref); gv_ref[...]=jnp.zeros_like(gv_ref); sum_ref[...]=jnp.zeros_like(sum_ref)
    def block(i,c):
        base=pl.multiple_of(i*BLOCK,BLOCK)
        here=vpad_ref[pl.ds(base+HALF,BLOCK),:]
        acc=None
        for r in range(8):
            n=5 if r==0 else 4
            win=gpad_ref[pl.ds(base+r,BLOCK+8*(n-1)),:]
            for a in range(n):
                s=2*HALF-(8*a+r)
                x=win[8*a:8*a+BLOCK]
                t=w_ref[s:s+1,:]*x
                acc=t if acc is None else acc+t
                p=(here*x).reshape(BLOCK//8,8,128)
                acc_ref[s]+=jnp.sum(p,axis=0)
        res_ref[pl.ds(base,BLOCK),:]=acc
        return c
    lax.fori_loop(0,-(-total//BLOCK),block,0)
    for lo in range(0,length,BLOCK*2):
        part=collect(res_ref,bounds,lo,BLOCK*2).T+att_ref[0,:,lo:lo+BLOCK*2]
        dv_ref[0,:,lo:lo+BLOCK*2]=part.astype(BF)
    dv=dv_ref[0]; depth=x_ref.shape[2]
    gv_ref[:,:depth]+=nn(dv,x_ref[0])
    sum_ref[...]+=jnp.sum(dv.astype(F32),axis=1,keepdims=True)
    @pl.when(b==pl.num_programs(1)-1)
    def _():
        rows=[jnp.sum(acc_ref[s],axis=0,keepdims=True) for s in range(KW)]
        side=jnp.concatenate(rows+[jnp.zeros((128-KW,128),F32)],axis=0).T
        lane=lax.broadcasted_iota(jnp.int32,(128,128),1)
        lines=su_ref.shape[1]
        side=side+jnp.where(lane==KW,sum_ref[:,:1],0.0)+jnp.where(lane==KW+1,q_ref[...],0.0)
        early=sums_ref[...].T
        for i in range(6): side=side+jnp.where(lane==KW+2+i,early[:,i:i+1],0.0)
        for i in range(lines): side=side+jnp.where(lane==KW+8+i,su_ref[:,i:i+1],0.0)
        gv_ref[:,depth:]=side
def conv_bwd(bounds, v, al, w_o, w, x, att, more, before, slabs, at):
    B,L,D=v.shape
    rows=padded_rows(L)
    sd=jax.ShapeDtypeStruct
    seq=pl.BlockSpec((1,L,D),lambda c,b,_:(b,0,0))
    feats=pl.BlockSpec((1,128,L),lambda c,b,_:(b,at+c,0))
    alias={11:0,12:1} if before else {}
    return pl.pallas_call(conv_bwd_kernel,grid_spec=pltpu.PrefetchScalarGridSpec(num_scalar_prefetch=1,grid=(slabs,B),
        in_specs=[pl.BlockSpec((1,L,128),lambda c,b,_:(b,0,at+c)),seq,
            pl.BlockSpec((D,128),lambda c,b,_:(0,at+c)),pl.BlockSpec((SMALL,128),lambda c,b,_:(0,at+c)),
            seq,feats,pl.BlockSpec((128,1),lambda c,b,_:(at+c,0)),pl.BlockSpec((8,128),lambda c,b,_:(0,at+c)),
            pl.BlockSpec((128,more[2].shape[1]),lambda c,b,_:(at+c,0))]+[pl.BlockSpec(memory_space=pl.ANY)]*len(before),
        out_specs=[feats,pl.BlockSpec((128,D+128),lambda c,b,_:(at+c,0))],
        scratch_shapes=[pltpu.VMEM((rows+2*HALF+8,128),F32)]*2+[pltpu.VMEM((rows,128),F32),pltpu.VMEM((KW,8,128),F32),
            pltpu.VMEM((L,128),F32),pltpu.VMEM((128,128),F32)]),
        out_shape=[sd((B,D,L),BF),sd((D,D+128),F32)],input_output_aliases={i-1:o for i,o in alias.items()},
        compiler_params=pltpu.CompilerParams(vmem_limit_bytes=60*2**20))(bounds,v,al,w_o,w,x,att,*more,*before)

def gelu_parts(x):
    size=jnp.abs(x)
    density=jnp.exp(-0.5*x*x)*0.3989422804014327
    t=1.0/(1.0+0.2316419*size)
    tail=density*(t*(0.319381530+t*(-0.356563782+t*(1.781477937+t*(-1.821255978+t*1.330274429)))))
    dist=jnp.where(x<0.0,tail,1.0-tail)
    return dist, x*density
def norm(v):
    mean=jnp.mean(v,axis=-1,keepdims=True); c=v-mean
    r=lax.rsqrt(jnp.mean(c*c,axis=-1,keepdims=True)+1e-5)
    return c*r, r
def norm_back(up,n,r,g):
    e=up*g
    return r*(e-jnp.mean(e,axis=-1,keepdims=True)-n*jnp.mean(e*n,axis=-1,keepdims=True))
def ffn_kernel(chunks, parts, ctx_ref,x_ref,cot_ref,wo_ref,wu_ref,*refs):
    wd_ref=refs[:chunks]
    (vec_ref,bu_ref,
               out_ref,normed_ref,hidden_ref,down_ref,up_ref,one_ref,att_ref,sums_ref,sumu_ref,slope_ref)=refs[chunks:]
    wu=wu_ref[...].reshape(-1,wu_ref.shape[-1]); width=wu.shape[0]//chunks
    size=x_ref.shape[0]//parts
    @pl.when(pl.program_id(0)==0)
    def _():
        sums_ref[...]=jnp.zeros_like(sums_ref); sumu_ref[...]=jnp.zeros_like(sumu_ref)
    v=lambda i: vec_ref[i:i+1,:]
    b_o,g1,s1,b_d,g2,s2=[v(KW+i) for i in range(2,8)]
    total=lambda a: jnp.sum(a,axis=0,keepdims=True)
    def steps(at):
        rows=slice(at*size,(at+1)*size); st={}
        def attend(): st["one"]=nt(ctx_ref[rows,:],wo_ref[...])
        def norm_one():
            st["n1"],st["r1"]=norm(x_ref[rows,:].astype(F32)+(st["one"]+b_o))
            st["normed"]=st["n1"]*g1+s1
            st["low"]=st["normed"].astype(BF); normed_ref[rows,:]=st["low"]
        def up(k):
            def go():
                if k>0:
                    add=nt(st["hid"],wd_ref[k-1][...]); st["down"]=add if k==1 else st["down"]+add
                if k<chunks: st["pre"]=nt(st["low"],wu[k*width:(k+1)*width,:])
            return go
        def gelu(k):
            part=slice(k*width,(k+1)*width)
            def go():
                pre=st["pre"]+bu_ref[:,part]
                dist,slope=gelu_parts(pre)
                slope_ref[rows,part]=dist+slope
                st["hid"]=(pre*dist).astype(BF); hidden_ref[rows,part]=st["hid"]
            return go
        def norm_two():
            n2,r2=norm(st["normed"]+(st["down"]+b_d))
            out_ref[rows,:]=(n2*g2+s2).astype(BF)
            cot=cot_ref[rows,:].astype(F32)
            st["back"]=norm_back(cot,n2,r2,g2)
            st["low2"]=st["back"].astype(BF); down_ref[rows,:]=st["low2"]
            sums_ref[3:6,:]+=jnp.concatenate([total(st["low2"].astype(F32)),total(cot*n2),total(cot)],axis=0)
        def back(k):
            def go():
                if k>0: st["back"]=st["back"]+nn(st["upl"],wu[(k-1)*width:k*width,:])
                if k<chunks: st["hg"]=nn(st["low2"],wd_ref[k][...])
            return go
        def scale(k):
            part=slice(k*width,(k+1)*width)
            def go():
                upl=(st["hg"]*slope_ref[rows,part]).astype(BF); up_ref[rows,part]=upl; st["upl"]=upl
                sumu_ref[:,part]+=total(upl.astype(F32))
            return go
        def norm_last():
            g_one=norm_back(st["back"],st["n1"],st["r1"],g1)
            one_ref[rows,:]=g_one
            al=g_one.astype(BF); att_ref[rows,:]=al
            sums_ref[0:3,:]+=jnp.concatenate([total(al.astype(F32)),total(st["back"]*st["n1"]),total(st["back"])],axis=0)
        out=[attend,norm_one]
        for k in range(chunks): out+=[up(k),gelu(k)]
        out+=[up(chunks),norm_two]
        for k in range(chunks): out+=[back(k),scale(k)]
        return out+[back(chunks),norm_last]
    lists=[steps(at) for at in range(parts)]
    for i in range(len(lists[0])+parts-1):
        for at in range(parts):
            if 0<=i-at<len(lists[at]): lists[at][i-at]()
def ffn(ctx,x,cot,wo,wu,wd,vec,bu,block=512,parts=2):
    chunks=len(wd)
    T,D=x.shape; F=bu.shape[1]
    row=lambda w: pl.BlockSpec((block,w),lambda i:(i,0))
    full=lambda a: pl.BlockSpec(a.shape,lambda i:(0,)*a.ndim,pipeline_mode=pl.Buffered(1))
    keep=lambda r,w: pl.BlockSpec((r,w),lambda i:(0,0))
    sd=jax.ShapeDtypeStruct
    return pl.pallas_call(functools.partial(ffn_kernel,chunks,parts),grid=(T//block,),
        in_specs=[row(D),row(D),row(D),full(wo),pl.BlockSpec((wu.shape[0],F//wu.shape[0],D),lambda i:(0,0,0),pipeline_mode=pl.Buffered(1)),*[full(a) for a in wd],pl.BlockSpec((SMALL,D),lambda i:(0,0)),full(bu)],
        out_specs=[row(D),row(D),row(F),row(D),row(F),row(D),row(D),keep(8,D),keep(1,F)],
        out_shape=[sd((T,D),BF),sd((T,D),BF),sd((T,F),BF),sd((T,D),BF),sd((T,F),BF),sd((T,D),F32),sd((T,D),BF),sd((8,D),F32),sd((1,F),F32)],
        scratch_shapes=[pltpu.VMEM((block,F),F32)],
        compiler_params=pltpu.CompilerParams(vmem_limit_bytes=60*2**20,dimension_semantics=("arbitrary",)),
    )(ctx,x,cot,wo,wu,*wd,vec,bu)


def across_rows(left_side, right_side):
    return lax.dot_general(left_side, right_side, (((0,), (0,)), ((), ())), preferred_element_type=F32)


def weight_kernel(own, up_ref, normed_ref, hidden_ref, down_ref, att_ref, ctx_ref, out_ref, acc_ref):
    depth=normed_ref.shape[1]; k=pl.program_id(1)
    wide_rows=up_ref.shape[1]; rows=down_ref.shape[1]; parts=hidden_ref.shape[1]//depth
    @pl.when(k==0)
    def _(): acc_ref[...]=jnp.zeros_like(acc_ref)
    for lo in range(0,wide_rows,rows):
        acc_ref[lo:lo+rows]+=across_rows(up_ref[:,lo:lo+rows],normed_ref[...])
    for i in range(parts):
        at=wide_rows+i*rows
        acc_ref[at:at+rows]+=across_rows(down_ref[...],hidden_ref[:,i*depth:(i+1)*depth])
    at=wide_rows+parts*rows
    acc_ref[at:at+rows]+=across_rows(att_ref[...],ctx_ref[...])
    @pl.when(k==pl.num_programs(1)-1)
    def _():
        many=rows//own; lines=wide_rows//many
        out_ref[:,:lines]=acc_ref[:wide_rows].reshape(many,lines,depth).astype(BF)
        narrow=[acc_ref[wide_rows+i*rows:wide_rows+(i+1)*rows].reshape(many,own,depth) for i in range(parts+1)]
        narrow.append(jnp.zeros((many,out_ref.shape[1]-lines-(parts+1)*own,depth),F32))
        out_ref[:,lines:]=jnp.concatenate(narrow,axis=1).astype(BF)
def weight_grads(own, up, normed, hidden, down, att, ctx):
    T,D=normed.shape; F=up.shape[1]; halves=2; many=D//own//halves; block=512
    R=-(-(F//D*2+1)*own//16)*16
    if own%8:
        by=lambda a: a.reshape(D//own,-1,D)
        pieces=[by(across_rows(up,normed))]+[by(across_rows(down,hidden[:,i*D:(i+1)*D])) for i in range(F//D)]
        pieces.append(by(across_rows(att,ctx)))
        pieces.append(jnp.zeros((D//own,R-(F//D*2+1)*own,D),F32))
        return jnp.concatenate(pieces,axis=1).astype(BF)
    col=lambda w: pl.BlockSpec((block,w),lambda h,k:(k,h)); row=lambda w: pl.BlockSpec((block,w),lambda h,k:(k,0))
    return pl.pallas_call(functools.partial(weight_kernel,own),grid=(halves,T//block),
        in_specs=[col(F//halves),row(D),row(F),col(D//halves),col(D//halves),row(D)],
        out_specs=pl.BlockSpec((many,R,D),lambda h,k:(h,0,0)),
        out_shape=jax.ShapeDtypeStruct((D//own,R,D),BF),
        scratch_shapes=[pltpu.VMEM((many*own*(F//D*2+1),D),F32)],
        compiler_params=pltpu.CompilerParams(vmem_limit_bytes=60*2**20))(up,normed,hidden,down,att,ctx)


def digits():
    found = []
    for axis in ("wide", "narrow"):
        stride = lax.axis_size(axis) // 2
        while stride >= 1:
            found.append((axis, stride))
            stride //= 2
    return found


def link_order(number):
    count = len(digits())
    if lax.axis_size("wide") == 8 and lax.axis_size("narrow") == 4:
        return [(4, 2, 3, 1, 0), (4, 3, 1, 2, 0), (4, 1, 2, 3, 0)][number]
    return tuple(range(count - 1, -1, -1))


def exchange(values, axis, stride):
    return lax.ppermute(values, axis, [(i, i ^ stride) for i in range(lax.axis_size(axis))])


def digit_of(axis, stride):
    return (lax.axis_index(axis) // stride) % 2


def gather_rows(shards, others):
    places = digits()
    held = [shard.reshape((1,) * len(places) + shard.shape) for shard in shards]
    passed = []
    for step in range(len(places)):
        for number, values in enumerate(held):
            dim = link_order(number)[::-1][step]
            mine = digit_of(*places[dim])
            got = exchange(values, *places[dim])
            first = jnp.where(mine == 0, values, got)
            second = jnp.where(mine == 0, got, values)
            held[number] = jnp.concatenate([first, second], dim)
        if step == 2:
            held, others = lax.optimization_barrier((held, others))
        else:
            held = lax.optimization_barrier(held)
        passed.append(held[0])
    return [values.reshape((-1,) + values.shape[-2:]) for values in held], passed, others


def scatter_start(whole, own):
    return whole.reshape(whole.shape[:-2] + (2,) * len(digits()) + (own, whole.shape[-1]))


def scatter_step(held, number, step):
    places = digits()
    dim = link_order(number)[step] + held.ndim - 2 - len(places)
    place = places[link_order(number)[step]]
    mine = digit_of(*place)
    keep = lax.dynamic_slice_in_dim(held, mine, 1, dim).astype(F32)
    send = lax.dynamic_slice_in_dim(held, 1 - mine, 1, dim).astype(BF)
    return keep + exchange(send, *place).astype(F32)


def scatter_rest(held, number, step):
    for later in range(step, len(digits())):
        held = scatter_step(held, number, later)
    return held.reshape(held.shape[: held.ndim - 2 - len(digits())] + held.shape[-2:])


def shards(
    inputs,
    tok_landmark,
    landmark_doc,
    w_query,
    b_query,
    w_key,
    w_value,
    b_value,
    conv_weight,
    w_out,
    b_out,
    gain_one,
    shift_one,
    w_up,
    b_up,
    w_down,
    b_down,
    gain_two,
    shift_two,
    cotangent,
):
    batch_rows, sequence_length, feature_width = inputs.shape
    group_count = lax.axis_size("wide") * lax.axis_size("narrow")
    own = feature_width // group_count
    tokens = batch_rows * sequence_length
    lines = b_up.shape[0] // own
    vectors = (b_query, b_value, b_out, gain_one, shift_one, b_down, gain_two, shift_two)
    flat = 0
    for place, vector in enumerate(vectors + (b_up,)):
        before = place * own
        flat = flat + jnp.pad(vector, (before, (8 + lines) * own - before - vector.shape[0]))
    small = jnp.concatenate([conv_weight, flat.reshape(8 + lines, own)])
    small = jnp.pad(small.T, ((0, 0), (0, 128 - small.shape[0])))
    member = tok_landmark[:, None, :] == jnp.arange(LM)[None, :, None]
    means = jnp.einsum("bjt,bti->bji", member.astype(BF), inputs, preferred_element_type=F32)
    means = means / jnp.sum(member, axis=2)[..., None].astype(F32)
    doc = jnp.sum(jnp.where(member, landmark_doc[:, :, None], 0), axis=1)
    bounds = jnp.sum(doc[:, None, :] < jnp.arange(DOCS + 1)[None, :, None], axis=2).astype(jnp.int32)
    (gathered_v, w_q, w_k), passed, (means, bounds) = gather_rows(
        [jnp.concatenate([w_value.T, small], axis=1), w_query.T, w_key.T], (means, bounds)
    )
    w_q = w_q.reshape(feature_width, feature_width)
    w_k = w_k.reshape(feature_width, feature_width)
    gathered_v = gathered_v.reshape(feature_width, feature_width + 128)
    w_v = gathered_v[:, :feature_width]
    small = gathered_v[:, feature_width:]
    b_u = jnp.moveaxis(small[:, KW + 8 : KW + 8 + lines].reshape(group_count, own, lines), 1, 2)
    b_u = b_u.reshape(1, -1).astype(F32)
    small = small.astype(F32).T
    ff_count = w_down.shape[0] // feature_width
    w_out, w_up, w_down, _ = lax.optimization_barrier((w_out, w_up, w_down, passed[0]))
    shard = jnp.concatenate(
        [w_up.T, w_out.T] + [w_down[i * feature_width : (i + 1) * feature_width].T for i in range(ff_count)]
    )
    gathered = lax.all_gather(shard, ("wide", "narrow"), axis=0)
    w_o = gathered[:, own * lines : own * (1 + lines)].reshape(feature_width, feature_width)
    w_u = gathered if own * lines % 16 == 0 else gathered[:, : own * lines].reshape(1, -1, feature_width)
    w_d = [
        gathered[:, own * (1 + lines + i) : own * (2 + lines + i)].reshape(feature_width, feature_width)
        for i in range(ff_count)
    ]
    rows_low = inputs.reshape(tokens, feature_width)
    value_rows, conv_part = conv_fwd(bounds, inputs, w_v, small)
    q, k, v, k1, k3, inv, stash, landmarks, context = att_fwd(
        inputs, means, w_q, w_k, w_v, small, tok_landmark, landmark_doc, conv_part
    )
    context = context.reshape(tokens, feature_width)
    layer_out, normed, hidden, down_low, up_low, grad_one, att_low, sums, sums_up = ffn(
        context, rows_low, cotangent.reshape(tokens, feature_width), w_o, w_u, w_d, small, b_u
    )
    grads = weight_grads(own, up_low, normed, hidden, down_low, att_low, context)
    share = lax.psum_scatter(grads, ("wide", "narrow"), scatter_dimension=0, tiled=True)[0]
    w_plain = w_o.T
    att_low = att_low.reshape(inputs.shape)
    dq, dk, dv, grad_qk, sum_q = att_bwd(
        inputs, att_low, w_plain, q, k, v, k1, k3, inv, stash, landmarks, tok_landmark
    )
    more = (sum_q, sums, sums_up.reshape(feature_width, lines))
    moving = scatter_start(grad_qk, own)
    calls, before = 3, ()
    slabs = feature_width // 128 // calls
    for call in range(calls):
        moved = scatter_step(moving, 1, call)
        before = conv_bwd(
            bounds, value_rows, att_low, w_o, small, inputs, dv, more, before, slabs, call * slabs
        )
        before, att_low, moving = lax.optimization_barrier((tuple(before), att_low, moved))
    dv, grad_v = before
    moved = scatter_start(grad_v, own)

    def through(grad, weight):
        return jnp.einsum("bot,oi->bti", grad, weight, preferred_element_type=F32)

    parts = ()
    for number in range(len(digits())):
        moved = scatter_step(moved, 0, number)
        if calls + number < len(digits()):
            moving = scatter_step(moving, 1, calls + number)
        if number == 0:
            moved, moving, dq = lax.optimization_barrier((moved, moving, dq))
            parts = (through(dq, w_q),)
        elif number == 1:
            moved, moving, dk, parts = lax.optimization_barrier((moved, moving, dk, parts))
            parts = parts + (through(dk, w_k),)
        elif number == 2:
            moved, dv, parts = lax.optimization_barrier((moved, dv, parts))
            input_grad = grad_one.reshape(inputs.shape) + parts[0] + parts[1] + through(dv, w_v)
        elif number == len(digits()) - 2:
            moved, share, input_grad = lax.optimization_barrier((moved, share, input_grad))
    share_qk = moving.reshape(moving.shape[:1] + moving.shape[-2:])
    share_v = moved.reshape(moved.shape[-2:])
    late = share_v[:, feature_width:]
    share = share.astype(F32)
    share_down = share[own * lines : 2 * own * lines].reshape(ff_count, own, feature_width)
    share_out = share[2 * own * lines : 2 * own * lines + own]
    return (
        layer_out.reshape(inputs.shape),
        input_grad,
        share_qk[0].T,
        late[:, KW + 1],
        share_qk[1].T,
        share_v[:, :feature_width].T,
        late[:, KW],
        late[:, :KW].T,
        share_out.T,
        late[:, KW + 2],
        late[:, KW + 3],
        late[:, KW + 4],
        share[: own * lines].T,
        late[:, KW + 8 : KW + 8 + lines].reshape(-1),
        jnp.moveaxis(share_down, 1, 2).reshape(-1, own),
        late[:, KW + 5],
        late[:, KW + 6],
        late[:, KW + 7],
    )


def solution(mesh):
    return jax.shard_map(
        shards,
        mesh=mesh,
        in_specs=(
            P(("wide", "narrow"), None, None),
            P(("wide", "narrow"), None),
            P(("wide", "narrow"), None),
            P(None, ("wide", "narrow")),
            P(("wide", "narrow")),
            P(None, ("wide", "narrow")),
            P(None, ("wide", "narrow")),
            P(("wide", "narrow")),
            P(None, ("wide", "narrow")),
            P(None, ("wide", "narrow")),
            P(("wide", "narrow")),
            P(("wide", "narrow")),
            P(("wide", "narrow")),
            P(None, ("wide", "narrow")),
            P(("wide", "narrow")),
            P(None, ("wide", "narrow")),
            P(("wide", "narrow")),
            P(("wide", "narrow")),
            P(("wide", "narrow")),
            P(("wide", "narrow"), None, None),
        ),
        out_specs=(
            P(("wide", "narrow"), None, None),
            P(("wide", "narrow"), None, None),
            P(None, ("wide", "narrow")),
            P(("wide", "narrow")),
            P(None, ("wide", "narrow")),
            P(None, ("wide", "narrow")),
            P(("wide", "narrow")),
            P(None, ("wide", "narrow")),
            P(None, ("wide", "narrow")),
            P(("wide", "narrow")),
            P(("wide", "narrow")),
            P(("wide", "narrow")),
            P(None, ("wide", "narrow")),
            P(("wide", "narrow")),
            P(None, ("wide", "narrow")),
            P(("wide", "narrow")),
            P(("wide", "narrow")),
            P(("wide", "narrow")),
        ),
        check_vma=False,
    )
```

```python
import functools

import jax
import jax.numpy as jnp
from jax import lax
from jax.experimental import pallas as pl
from jax.experimental.pallas import tpu as pltpu
from jax.sharding import PartitionSpec as P

BF = jnp.bfloat16
F32 = jnp.float32
HW=64; LM=64; NEWTON=6; GH=12; GW=GH*HW
CHUNK=256
KW=33
SMALL=48
def nt(a,b): return lax.dot_general(a,b,(((1,),(1,)),((),())),preferred_element_type=F32)
def nn(a,b): return lax.dot_general(a,b,(((1,),(0,)),((),())),preferred_element_type=F32)
def split(a):
    hi=a.astype(BF); return hi,(a-hi.astype(F32)).astype(BF)
def wide(a):
    hi,lo=split(a); return jnp.concatenate([hi,hi,lo],axis=1)
def tall(b):
    hi,lo=split(b); return jnp.concatenate([hi,lo,hi],axis=0)
def mm3(a,b): return nn(wide(a),tall(b))
def eye(c):
    row=lax.broadcasted_iota(jnp.int32,(LM,2*LM),0); col=lax.broadcasted_iota(jnp.int32,(LM,2*LM),1)
    return jnp.where((row==col)|(row+LM==col),c,0.0)
def beside(a):
    return [jnp.concatenate([a[i],a[i+1]],axis=1) for i in range(0,len(a),2)]
def blocks(b):
    lane=lax.broadcasted_iota(jnp.int32,(1,2*LM),1)
    first=jnp.where(lane<LM,1.0,0.0).astype(BF); second=jnp.where(lane<LM,0.0,1.0).astype(BF)
    hi,lo=split(b)
    return jnp.concatenate([hi*first,hi*second,lo*first,lo*second,hi*first,hi*second],axis=0)
def mmb(a,b): return nn(wide(a),blocks(b))
def weave(first, second):
    done=0
    for i,step in enumerate(first):
        step()
        upto=(i+1)*len(second)//len(first)
        for other in second[done:upto]: other()
        done=upto
def att_fwd_kernel(x_ref,mean_ref,wq_ref,wk_ref,wv_ref,vec_ref,tok_ref,ldc_ref,ldr_ref,conv_ref,
               q_ref,k_ref,v_ref,k1_ref,k3_ref,inv_ref,stash_ref,small_ref,ctx_ref,
               qlo_ref,klo_ref,score_ref,bias_ref):
    T=x_ref.shape[1]
    heads=range(GH); chunks=[slice(c,c+CHUNK) for c in range(0,T,CHUNK)]
    rows=[slice(h*HW,(h+1)*HW) for h in heads]
    scale=HW**-0.25
    bq=vec_ref[KW:KW+1,:].T; bv=vec_ref[KW+1:KW+2,:].T
    ldc=ldc_ref[0]
    for cs in chunks:
        member=lax.broadcasted_iota(jnp.int32,(LM,CHUNK),0)==tok_ref[0,:,cs]
        doc=jnp.sum(jnp.where(member,ldc,0),axis=0,keepdims=True)
        bias_ref[:,cs]=jnp.where(doc==ldc,0.0,-1e30)
    mean=jnp.concatenate(split(mean_ref[0]),axis=0)
    def land(w_ref):
        both=nt(w_ref[...],mean)
        return both[:,:LM]+both[:,LM:]
    lqt=(land(wq_ref)+bq)*scale; lkt=land(wk_ref)*scale
    lq=[lqt[r].T for r in rows]; lk=[lkt[r].T for r in rows]
    lqw=[wide(a) for a in lq]; lkw=[wide(a) for a in lk]
    allow2=ldc==ldr_ref[0]
    k2=[];zt=[]
    for h in heads:
        sc=jnp.where(allow2,nn(lqw[h],tall(lkt[rows[h]])),-1e30)
        e=jnp.exp(sc-jnp.max(sc,axis=1,keepdims=True))
        k2.append(e/jnp.sum(e,axis=1,keepdims=True))
        zt.append(k2[h]*(1.0/jnp.sum(k2[h]*k2[h])))
    pairs=range(GH//2)
    state={"zt":beside(zt)}
    k2tb=[blocks(a) for a in beside([a.T for a in k2])]
    def newton(n):
        def one():
            state["p"]=[nn(wide(state["zt"][i]),k2tb[i]) for i in pairs]
            state["pw"]=[wide(a) for a in state["p"]]
        def two(): state["b"]=[eye(15.0)-nn(state["pw"][i],blocks(eye(7.0)-state["p"][i])) for i in pairs]
        def three(): state["c"]=[eye(13.0)-nn(state["pw"][i],blocks(state["b"][i])) for i in pairs]
        def four():
            for i in pairs:
                for place,key in enumerate(("p","b","c","zt")): stash_ref[0,i,4*n+place]=state[key][i]
            state["zt"]=[0.25*mmb(state["c"][i],state["zt"][i]) for i in pairs]
        return [one,two,three,four]
    chain=[step for n in range(NEWTON) for step in newton(n)]
    side=[]
    def project(cs):
        x=x_ref[0,cs,:]
        def q():
            a=(nt(wq_ref[...],x)+bq)*scale
            hi,lo=split(a); q_ref[0,:,cs]=hi; qlo_ref[:,cs]=lo
        def k():
            a=nt(wk_ref[...],x)*scale
            hi,lo=split(a); k_ref[0,:,cs]=hi; klo_ref[:,cs]=lo
        def v(): v_ref[0,:,cs]=(nt(wv_ref[...],x)+bv).astype(BF)
        return [q,k,v]
    tops=[None]*GH; sums=[None]*GH; r=[None]*GH
    def lanes(a): return [a[:,i:i+128] for i in range(0,CHUNK,128)]
    def first(h,cs):
        def go():
            hi=q_ref[0,rows[h],cs]
            s=nn(lkw[h],jnp.concatenate([hi,qlo_ref[rows[h],cs],hi],axis=0))+bias_ref[:,cs]
            e=jnp.exp(s-jnp.max(s,axis=0,keepdims=True))
            e=e.astype(BF); k1_ref[0,rows[h],cs]=e
            inv_ref[0,0,h:h+1,cs]=1.0/jnp.sum(e.astype(F32),axis=0,keepdims=True)
        return go
    def third(h,cs):
        def go():
            hi=k_ref[0,rows[h],cs]
            s=nn(lqw[h],jnp.concatenate([hi,klo_ref[rows[h],cs],hi],axis=0))+bias_ref[:,cs]
            score_ref[rows[h],cs]=s
            for a in lanes(s): tops[h]=a if tops[h] is None else jnp.maximum(tops[h],a)
        return go
    def raised(h,cs):
        def go():
            if cs.start==0: tops[h]=jnp.max(tops[h],axis=1,keepdims=True)
            e=jnp.exp(score_ref[rows[h],cs]-tops[h])
            e=e.astype(BF); k3_ref[0,rows[h],cs]=e
            for a in lanes(e.astype(F32)): sums[h]=a if sums[h] is None else sums[h]+a
        return go
    def gathered(h):
        def go():
            sums[h]=1.0/jnp.sum(sums[h],axis=1,keepdims=True)
            r[h]=nt(k3_ref[0,rows[h]],v_ref[0,rows[h]])*sums[h]
        return go
    for cs in chunks: side+=project(cs)
    for h in heads:
        side+=[third(h,cs) for cs in chunks]
        side+=[raised(h,cs) for cs in chunks]+[gathered(h)]
        side+=[first(h,cs) for cs in chunks]
    weave(chain,side)
    uts=[]
    for h in heads:
        zt=state["zt"][h//2][:,h%2*LM:(h%2+1)*LM]
        u=mm3(zt.T,r[h])
        small_ref[0,h,0]=jnp.concatenate([lq[h],lk[h]],axis=1)
        small_ref[0,h,1]=jnp.concatenate([k2[h],zt],axis=1)
        small_ref[0,h,2]=jnp.concatenate([r[h],u],axis=1)
        small_ref[0,h,3]=jnp.broadcast_to(sums[h],(LM,128))
        uts.append(u.T.astype(BF))
    for cs in chunks:
        mixed=jnp.concatenate([nn(uts[h],k1_ref[0,rows[h],cs])*inv_ref[0,0,h:h+1,cs] for h in heads],axis=0)
        ctx_ref[0,cs,:]=(mixed.T+conv_ref[0,cs,:]).astype(BF)
def att_specs(D,T):
    seq=lambda s: pl.BlockSpec((1,)+s,lambda g,b:(b,)+(0,)*len(s))
    wsp=pl.BlockSpec((GW,D),lambda g,b:(g,0)); bsp=pl.BlockSpec((GW,1),lambda g,b:(g,0))
    rows=pl.BlockSpec((1,GW,T),lambda g,b:(b,g,0)); cols=pl.BlockSpec((1,T,GW),lambda g,b:(b,0,g))
    sq=lambda m,n: pl.BlockSpec((1,m,n,LM,2*LM),lambda g,b:(b,g,0,0,0))
    turned=pl.BlockSpec((1,1,-(-GH//8)*8,T),lambda g,b:(b,g,0,0))
    return seq,wsp,bsp,rows,cols,sq,turned
def att_fwd(x,mean,wq,wk,wv,vec,tok,ld,conv):
    B,T,D=x.shape; G=D//GW; H=D//HW
    seq,wsp,bsp,rows,cols,sq,turned=att_specs(D,T)
    sd=jax.ShapeDtypeStruct; big=sd((B,D,T),BF)
    return pl.pallas_call(att_fwd_kernel,grid=(G,B),
        in_specs=[seq((T,D)),seq((LM,D)),wsp,wsp,wsp,pl.BlockSpec((SMALL,GW),lambda g,b:(0,g)),seq((1,T)),seq((LM,1)),seq((1,LM)),cols],
        out_specs=[rows]*5+[turned,sq(GH//2,4*NEWTON),sq(GH,4),cols],
        out_shape=[big]*5+[sd((B,G,-(-GH//8)*8,T),F32),sd((B,H//2,4*NEWTON,LM,2*LM),F32),sd((B,H,4,LM,2*LM),F32),sd((B,T,D),BF)],
        scratch_shapes=[pltpu.VMEM((GW,T),BF)]*2+[pltpu.VMEM((GW,T),F32),pltpu.VMEM((LM,T),F32)],
        compiler_params=pltpu.CompilerParams(vmem_limit_bytes=60*2**20))(
            x,mean,wq,wk,wv,vec,tok[:,None,:],ld[:,:,None],ld[:,None,:],conv)
def att_bwd_kernel(x_ref,al_ref,wo_ref,q_ref,k_ref,v_ref,k1_ref,k3_ref,inv_ref,stash_ref,small_ref,tok_ref,
               dq_ref,dk_ref,dv_ref,gqk_ref,sq_ref,
               g_ref,ds1_ref,ds3_ref,hot_ref):
    T=x_ref.shape[1]
    heads=range(GH); chunks=[slice(c,c+CHUNK) for c in range(0,T,CHUNK)]
    rows=[slice(h*HW,(h+1)*HW) for h in heads]
    scale=HW**-0.25
    for cs in chunks:
        member=lax.broadcasted_iota(jnp.int32,(LM,CHUNK),0)==tok_ref[0,:,cs]
        hot_ref[:,cs]=jnp.where(member,1.0,0.0).astype(BF)
    per=1.0/nt(jnp.ones((8,T),BF),hot_ref[...])[0:1]
    left=lambda i: [small_ref[0,h,i,:,:LM] for h in heads]
    right=lambda i: [small_ref[0,h,i,:,LM:] for h in heads]
    lq,lk,k2,zt,r,u=left(0),right(0),left(1),right(1),left(2),right(2)
    inv=[small_ref[0,h,3,:,:LM] for h in heads]
    ub=[a.astype(BF) for a in u]
    def upstream(cs):
        def go():
            a=nt(wo_ref[...],al_ref[0,cs,:])
            for h in heads: g_ref[rows[h],cs]=(a[rows[h]]*inv_ref[0,0,h:h+1,cs]).astype(BF)
        return go
    def first(h,cs):
        def go():
            k1=k1_ref[0,rows[h],cs].astype(F32)
            t=k1*nn(ub[h],g_ref[rows[h],cs])
            ds1_ref[rows[h],cs]=(t-k1*(jnp.sum(t,axis=0,keepdims=True)*inv_ref[0,0,h:h+1,cs])).astype(BF)
        return go
    for cs in chunks: upstream(cs)()
    du=[nt(k1_ref[0,rows[h]],g_ref[rows[h],:]) for h in heads]
    dr=[mm3(zt[h],du[h]) for h in heads]
    state={"dz":beside([mm3(du[h],r[h].T) for h in heads]),"dk2":[None]*(GH//2)}
    drs=[(dr[h]*inv[h]) for h in heads]
    drb=[a.astype(BF) for a in drs]; drt=[a.T.astype(BF) for a in drs]
    delta=[jnp.sum(drb[h].astype(F32)*r[h],axis=1,keepdims=True) for h in heads]
    dlq=[None]*GH; dlk=[None]*GH
    def third(h,cs):
        def go():
            d=k3_ref[0,rows[h],cs].astype(F32)*(nn(drb[h],v_ref[0,rows[h],cs])-delta[h])
            ds3_ref[rows[h],cs]=d.astype(BF)
        return go
    def values(cs):
        def go():
            a=jnp.concatenate([nn(drt[h],k3_ref[0,rows[h],cs]) for h in heads],axis=0)
            dv_ref[0,:,cs]=a
        return go
    def to_lk(h):
        def go(): dlk[h]=nt(ds1_ref[rows[h],:],q_ref[0,rows[h]])
        return go
    def to_lq(h):
        def go(): dlq[h]=nt(ds3_ref[rows[h],:],k_ref[0,rows[h]])
        return go
    @pl.when(pl.program_id(1)==0)
    def _():
        for ref in (gqk_ref,sq_ref): ref[...]=jnp.zeros_like(ref)
    side=[]
    for h in heads: side+=[third(h,cs) for cs in chunks]+[to_lq(h)]+[first(h,cs) for cs in chunks]+[to_lk(h)]
    side+=[values(cs) for cs in chunks]
    pairs=range(GH//2)
    k2t=[a.T for a in k2]; k2tw=[wide(a) for a in beside(k2t)]
    def newton(n):
        def one():
            state["p"],state["b"],state["c"],state["zt"]=[[stash_ref[0,i,4*n+place] for i in pairs] for place in range(4)]
            state["gz"]=[0.25*d for d in state["dz"]]
            state["dc"]=[mmb(state["zt"][i],state["gz"][i]) for i in pairs]
            state["pw"]=[wide(m) for m in state["p"]]
        def two(): state["db"]=[nn(state["pw"][i],blocks(state["dc"][i])) for i in pairs]
        def three():
            da=[nn(state["pw"][i],blocks(state["db"][i])) for i in pairs]
            state["dp"]=[mmb(state["db"][i],eye(7.0)-state["p"][i])-mmb(state["dc"][i],state["b"][i])-da[i] for i in pairs]
        def four():
            for i in pairs:
                t=mmb(state["dp"][i],state["zt"][i])
                state["dk2"][i]=t if state["dk2"][i] is None else state["dk2"][i]+t
            state["dz"]=[mmb(state["gz"][i],state["c"][i])+nn(k2tw[i],blocks(state["dp"][i])) for i in pairs]
        return [one,two,three,four]
    chain=[step for n in reversed(range(NEWTON)) for step in newton(n)]
    weave(chain,side)
    lhq=[];lhk=[]
    for h in heads:
        half=slice(h%2*LM,(h%2+1)*LM)
        i2=1.0/jnp.sum(k2[h]*k2[h]); dz=state["dz"][h//2][:,half]
        d=state["dk2"][h//2][:,half]+i2*dz.T-k2[h]*(2.0*i2*i2*jnp.sum(dz*k2t[h]))
        d=k2[h]*(d-jnp.sum(k2[h]*d,axis=1,keepdims=True))
        dlqh=dlq[h]+mm3(d,lk[h]); dlkh=dlk[h]+mm3(d.T,lq[h])
        lhq.append(jnp.concatenate([lk[h].T,dlqh.T*per],axis=1).astype(BF))
        lhk.append(jnp.concatenate([lq[h].T,dlkh.T*per],axis=1).astype(BF))
    for cs in chunks:
        hot=hot_ref[:,cs]
        for lh,ds_ref,out_ref in ((lhq,ds1_ref,dq_ref),(lhk,ds3_ref,dk_ref)):
            for h in heads:
                a=nn(lh[h],jnp.concatenate([ds_ref[rows[h],cs],hot],axis=0))
                out_ref[0,rows[h],cs]=(a*scale).astype(BF)
    dq=dq_ref[0]
    gqk_ref[0]+=nn(dq,x_ref[0]); gqk_ref[1]+=nn(dk_ref[0],x_ref[0])
    sq_ref[...]+=jnp.sum(dq.astype(F32),axis=1,keepdims=True)
def att_bwd(x,al,wo,q,k,v,k1,k3,inv,stash,small,tok):
    B,T,D=x.shape; G=D//GW
    seq,wsp,bsp,rows,cols,sq,turned=att_specs(D,T)
    sd=jax.ShapeDtypeStruct; big=sd((B,D,T),BF)
    return pl.pallas_call(att_bwd_kernel,grid=(G,B),
        in_specs=[seq((T,D)),seq((T,D)),wsp]+[rows]*5+[turned,sq(GH//2,4*NEWTON),sq(GH,4),seq((1,T))],
        out_specs=[rows]*3+[pl.BlockSpec((2,GW,D),lambda g,b:(0,g,0)),bsp],
        out_shape=[big,big,sd((B,D,T),F32),sd((2,D,D),F32),sd((D,1),F32)],
        scratch_shapes=[pltpu.VMEM((GW,T),BF)]*3+[pltpu.VMEM((LM,T),BF)],
        compiler_params=pltpu.CompilerParams(vmem_limit_bytes=60*2**20))(
            x,al,wo,q,k,v,k1,k3,inv,stash,small,tok[:,None,:])

HALF=16; DOCS=4; GAP=16
def spread(places, bounds, length, step):
    total=length+GAP*(DOCS+1)
    ids=lax.broadcasted_iota(jnp.int32,(step,128),0)
    for p0 in range(0,total,step):
        size=min(step,total-p0)
        sums=[None]*len(places)
        for d in range(DOCS):
            s0=p0-GAP*(d+1)
            lo=max(s0,0); hi=min(s0+size,length)
            if hi<=lo: continue
            row=ids[:hi-lo]+lo
            inside=(row>=bounds[d])&(row<bounds[d+1])
            for i,(_,get) in enumerate(places):
                part=jnp.where(inside,get(lo,hi-lo),0.0)
                pads=[]
                if lo>s0: pads.append(jnp.zeros((lo-s0,128),F32))
                pads.append(part)
                if s0+size>hi: pads.append(jnp.zeros((s0+size-hi,128),F32))
                part=jnp.concatenate(pads,0) if len(pads)>1 else part
                sums[i]=part if sums[i] is None else sums[i]+part
        for i,(dst,_) in enumerate(places):
            dst[HALF+p0:HALF+p0+size,:]=jnp.zeros((size,128),F32) if sums[i] is None else sums[i]
def collect(src, bounds, lo, size):
    row=lax.broadcasted_iota(jnp.int32,(size,128),0)+lo
    acc=None
    for d in range(DOCS):
        part=src[lo+GAP*(d+1):lo+GAP*(d+1)+size,:]
        acc=part if acc is None else jnp.where(row>=bounds[d],part,acc)
    return acc
BLOCK=64
TALL=128
WIDTH=256
SLABS=range(WIDTH//128)
def taps(ref, base, weight, sign):
    acc=None
    for r in range(8):
        win=ref[pl.ds(base+r,TALL+32),:] if r==0 else ref[pl.ds(base+r,TALL+24),:]
        for a in range(5 if r==0 else 4):
            o=8*a+r
            t=weight(o if sign>0 else 2*HALF-o)*win[8*a:8*a+TALL]
            acc=t if acc is None else acc+t
    return acc

def cut(h): return slice(h*128,(h+1)*128)
def conv_fwd_kernel(bounds_ref, x_ref, wv_ref, w_ref, v_ref, out_ref, pad_ref, res_ref):
    b=pl.program_id(0)
    bounds=[bounds_ref[b,d] for d in range(DOCS+1)]
    length=v_ref.shape[1]; total=length+GAP*(DOCS+1)
    for lo in range(0,length,256):
        v_ref[0,lo:lo+256,:]=nt(x_ref[0,lo:lo+256,:],wv_ref[...])+w_ref[KW+1:KW+2,:]
    for h in SLABS:
        pad_ref[h,0:HALF,:]=jnp.zeros((HALF,128),F32)
        pad_ref[h,HALF+total:,:]=jnp.zeros((pad_ref.shape[1]-HALF-total,128),F32)
    spread([(pad_ref.at[h], lambda lo,n,h=h: v_ref[0,lo:lo+n,cut(h)]) for h in SLABS], bounds, length, BLOCK)
    def block(i,c):
        base=pl.multiple_of(i*TALL,TALL)
        for h in SLABS:
            res_ref[h,pl.ds(base,TALL),:]=taps(pad_ref.at[h], base, lambda s: w_ref[s:s+1,cut(h)], 1)
        return c
    lax.fori_loop(0,-(-total//TALL),block,0)
    for h in SLABS:
        for lo in range(0,length,BLOCK):
            out_ref[0,lo:lo+BLOCK,cut(h)]=collect(res_ref.at[h],bounds,lo,BLOCK)
def padded_rows(length):
    total=length+GAP*(DOCS+1)
    return -(-total//TALL)*TALL

def conv_fwd(bounds, x, w_v, w):
    B,L,D=x.shape
    rows=padded_rows(L)
    slab=pl.BlockSpec((1,L,WIDTH),lambda b,c,_:(b,0,c)); big=jax.ShapeDtypeStruct((B,L,D),F32)
    return pl.pallas_call(conv_fwd_kernel,grid_spec=pltpu.PrefetchScalarGridSpec(num_scalar_prefetch=1,grid=(B,D//WIDTH),
        in_specs=[pl.BlockSpec((1,L,D),lambda b,c,_:(b,0,0)),pl.BlockSpec((WIDTH,D),lambda b,c,_:(c,0)),
            pl.BlockSpec((SMALL,WIDTH),lambda b,c,_:(0,c))],
        out_specs=[slab,slab],
        scratch_shapes=[pltpu.VMEM((WIDTH//128,rows+2*HALF+8,128),F32),pltpu.VMEM((WIDTH//128,rows,128),F32)]),
        out_shape=[big,big],
        compiler_params=pltpu.CompilerParams(vmem_limit_bytes=60*2**20))(bounds,x,w_v,w)
def conv_bwd_kernel(bounds_ref, v_ref, al_ref, wo_ref, w_ref, x_ref, att_ref, q_ref, sums_ref, su_ref, *refs):
    dv_ref, gv_ref, vpad_ref, gpad_ref, res_ref, acc_ref, g_ref, sum_ref = refs[-8:]
    b=pl.program_id(1)
    bounds=[bounds_ref[b,d] for d in range(DOCS+1)]
    length=v_ref.shape[1]; total=length+GAP*(DOCS+1)
    for lo in range(0,length,256):
        g_ref[lo:lo+256,:]=nn(al_ref[0,lo:lo+256,:],wo_ref[...])
    for ref in (vpad_ref,gpad_ref):
        ref[0:HALF,:]=jnp.zeros((HALF,128),F32)
        ref[HALF+total:,:]=jnp.zeros((ref.shape[0]-HALF-total,128),F32)
    spread([(vpad_ref, lambda lo,n: v_ref[0,lo:lo+n,:]), (gpad_ref, lambda lo,n: g_ref[lo:lo+n,:])], bounds, length, BLOCK)
    @pl.when(b==0)
    def _():
        acc_ref[...]=jnp.zeros_like(acc_ref); gv_ref[...]=jnp.zeros_like(gv_ref); sum_ref[...]=jnp.zeros_like(sum_ref)
    def block(i,c):
        base=pl.multiple_of(i*BLOCK,BLOCK)
        here=vpad_ref[pl.ds(base+HALF,BLOCK),:]
        acc=None
        for r in range(8):
            n=5 if r==0 else 4
            win=gpad_ref[pl.ds(base+r,BLOCK+8*(n-1)),:]
            for a in range(n):
                s=2*HALF-(8*a+r)
                x=win[8*a:8*a+BLOCK]
                t=w_ref[s:s+1,:]*x
                acc=t if acc is None else acc+t
                p=(here*x).reshape(BLOCK//8,8,128)
                acc_ref[s]+=jnp.sum(p,axis=0)
        res_ref[pl.ds(base,BLOCK),:]=acc
        return c
    lax.fori_loop(0,-(-total//BLOCK),block,0)
    for lo in range(0,length,BLOCK*2):
        part=collect(res_ref,bounds,lo,BLOCK*2).T+att_ref[0,:,lo:lo+BLOCK*2]
        dv_ref[0,:,lo:lo+BLOCK*2]=part.astype(BF)
    dv=dv_ref[0]; depth=x_ref.shape[2]
    gv_ref[:,:depth]+=nn(dv,x_ref[0])
    sum_ref[...]+=jnp.sum(dv.astype(F32),axis=1,keepdims=True)
    @pl.when(b==pl.num_programs(1)-1)
    def _():
        rows=[jnp.sum(acc_ref[s],axis=0,keepdims=True) for s in range(KW)]
        side=jnp.concatenate(rows+[jnp.zeros((128-KW,128),F32)],axis=0).T
        lane=lax.broadcasted_iota(jnp.int32,(128,128),1)
        lines=su_ref.shape[1]
        side=side+jnp.where(lane==KW,sum_ref[:,:1],0.0)+jnp.where(lane==KW+1,q_ref[...],0.0)
        early=sums_ref[...].T
        for i in range(6): side=side+jnp.where(lane==KW+2+i,early[:,i:i+1],0.0)
        for i in range(lines): side=side+jnp.where(lane==KW+8+i,su_ref[:,i:i+1],0.0)
        gv_ref[:,depth:]=side
def conv_bwd(bounds, v, al, w_o, w, x, att, more, before, slabs, at):
    B,L,D=v.shape
    rows=padded_rows(L)
    sd=jax.ShapeDtypeStruct
    seq=pl.BlockSpec((1,L,D),lambda c,b,_:(b,0,0))
    feats=pl.BlockSpec((1,128,L),lambda c,b,_:(b,at+c,0))
    alias={11:0,12:1} if before else {}
    return pl.pallas_call(conv_bwd_kernel,grid_spec=pltpu.PrefetchScalarGridSpec(num_scalar_prefetch=1,grid=(slabs,B),
        in_specs=[pl.BlockSpec((1,L,128),lambda c,b,_:(b,0,at+c)),seq,
            pl.BlockSpec((D,128),lambda c,b,_:(0,at+c)),pl.BlockSpec((SMALL,128),lambda c,b,_:(0,at+c)),
            seq,feats,pl.BlockSpec((128,1),lambda c,b,_:(at+c,0)),pl.BlockSpec((8,128),lambda c,b,_:(0,at+c)),
            pl.BlockSpec((128,more[2].shape[1]),lambda c,b,_:(at+c,0))]+[pl.BlockSpec(memory_space=pl.ANY)]*len(before),
        out_specs=[feats,pl.BlockSpec((128,D+128),lambda c,b,_:(at+c,0))],
        scratch_shapes=[pltpu.VMEM((rows+2*HALF+8,128),F32)]*2+[pltpu.VMEM((rows,128),F32),pltpu.VMEM((KW,8,128),F32),
            pltpu.VMEM((L,128),F32),pltpu.VMEM((128,128),F32)]),
        out_shape=[sd((B,D,L),BF),sd((D,D+128),F32)],input_output_aliases={i-1:o for i,o in alias.items()},
        compiler_params=pltpu.CompilerParams(vmem_limit_bytes=60*2**20))(bounds,v,al,w_o,w,x,att,*more,*before)

def gelu_parts(x):
    size=jnp.abs(x)
    density=jnp.exp(-0.5*x*x)*0.3989422804014327
    t=1.0/(1.0+0.2316419*size)
    tail=density*(t*(0.319381530+t*(-0.356563782+t*(1.781477937+t*(-1.821255978+t*1.330274429)))))
    dist=jnp.where(x<0.0,tail,1.0-tail)
    return dist, x*density
def norm(v):
    mean=jnp.mean(v,axis=-1,keepdims=True); c=v-mean
    r=lax.rsqrt(jnp.mean(c*c,axis=-1,keepdims=True)+1e-5)
    return c*r, r
def norm_back(up,n,r,g):
    e=up*g
    return r*(e-jnp.mean(e,axis=-1,keepdims=True)-n*jnp.mean(e*n,axis=-1,keepdims=True))
def ffn_kernel(chunks, parts, ctx_ref,x_ref,cot_ref,wo_ref,wu_ref,*refs):
    wd_ref=refs[:chunks]
    (vec_ref,bu_ref,
               out_ref,normed_ref,hidden_ref,down_ref,up_ref,one_ref,att_ref,sums_ref,sumu_ref,slope_ref)=refs[chunks:]
    wu=wu_ref[...].reshape(-1,wu_ref.shape[-1]); width=wu.shape[0]//chunks
    size=x_ref.shape[0]//parts
    @pl.when(pl.program_id(0)==0)
    def _():
        sums_ref[...]=jnp.zeros_like(sums_ref); sumu_ref[...]=jnp.zeros_like(sumu_ref)
    v=lambda i: vec_ref[i:i+1,:]
    b_o,g1,s1,b_d,g2,s2=[v(KW+i) for i in range(2,8)]
    total=lambda a: jnp.sum(a,axis=0,keepdims=True)
    def steps(at):
        rows=slice(at*size,(at+1)*size); st={}
        def attend(): st["one"]=nt(ctx_ref[rows,:],wo_ref[...])
        def norm_one():
            st["n1"],st["r1"]=norm(x_ref[rows,:].astype(F32)+(st["one"]+b_o))
            st["normed"]=st["n1"]*g1+s1
            st["low"]=st["normed"].astype(BF); normed_ref[rows,:]=st["low"]
        def up(k):
            def go():
                if k>0:
                    add=nt(st["hid"],wd_ref[k-1][...]); st["down"]=add if k==1 else st["down"]+add
                if k<chunks: st["pre"]=nt(st["low"],wu[k*width:(k+1)*width,:])
            return go
        def gelu(k):
            part=slice(k*width,(k+1)*width)
            def go():
                pre=st["pre"]+bu_ref[:,part]
                dist,slope=gelu_parts(pre)
                slope_ref[rows,part]=dist+slope
                st["hid"]=(pre*dist).astype(BF); hidden_ref[rows,part]=st["hid"]
            return go
        def norm_two():
            n2,r2=norm(st["normed"]+(st["down"]+b_d))
            out_ref[rows,:]=(n2*g2+s2).astype(BF)
            cot=cot_ref[rows,:].astype(F32)
            st["back"]=norm_back(cot,n2,r2,g2)
            st["low2"]=st["back"].astype(BF); down_ref[rows,:]=st["low2"]
            sums_ref[3:6,:]+=jnp.concatenate([total(st["low2"].astype(F32)),total(cot*n2),total(cot)],axis=0)
        def back(k):
            def go():
                if k>0: st["back"]=st["back"]+nn(st["upl"],wu[(k-1)*width:k*width,:])
                if k<chunks: st["hg"]=nn(st["low2"],wd_ref[k][...])
            return go
        def scale(k):
            part=slice(k*width,(k+1)*width)
            def go():
                upl=(st["hg"]*slope_ref[rows,part]).astype(BF); up_ref[rows,part]=upl; st["upl"]=upl
                sumu_ref[:,part]+=total(upl.astype(F32))
            return go
        def norm_last():
            g_one=norm_back(st["back"],st["n1"],st["r1"],g1)
            one_ref[rows,:]=g_one
            al=g_one.astype(BF); att_ref[rows,:]=al
            sums_ref[0:3,:]+=jnp.concatenate([total(al.astype(F32)),total(st["back"]*st["n1"]),total(st["back"])],axis=0)
        out=[attend,norm_one]
        for k in range(chunks): out+=[up(k),gelu(k)]
        out+=[up(chunks),norm_two]
        for k in range(chunks): out+=[back(k),scale(k)]
        return out+[back(chunks),norm_last]
    lists=[steps(at) for at in range(parts)]
    for i in range(len(lists[0])+parts-1):
        for at in range(parts):
            if 0<=i-at<len(lists[at]): lists[at][i-at]()
def ffn(ctx,x,cot,wo,wu,wd,vec,bu,block=512,parts=2):
    chunks=len(wd)
    T,D=x.shape; F=bu.shape[1]
    row=lambda w: pl.BlockSpec((block,w),lambda i:(i,0))
    full=lambda a: pl.BlockSpec(a.shape,lambda i:(0,)*a.ndim,pipeline_mode=pl.Buffered(1))
    keep=lambda r,w: pl.BlockSpec((r,w),lambda i:(0,0))
    sd=jax.ShapeDtypeStruct
    return pl.pallas_call(functools.partial(ffn_kernel,chunks,parts),grid=(T//block,),
        in_specs=[row(D),row(D),row(D),full(wo),pl.BlockSpec((wu.shape[0],F//wu.shape[0],D),lambda i:(0,0,0),pipeline_mode=pl.Buffered(1)),*[full(a) for a in wd],pl.BlockSpec((SMALL,D),lambda i:(0,0)),full(bu)],
        out_specs=[row(D),row(D),row(F),row(D),row(F),row(D),row(D),keep(8,D),keep(1,F)],
        out_shape=[sd((T,D),BF),sd((T,D),BF),sd((T,F),BF),sd((T,D),BF),sd((T,F),BF),sd((T,D),F32),sd((T,D),BF),sd((8,D),F32),sd((1,F),F32)],
        scratch_shapes=[pltpu.VMEM((block,F),F32)],
        compiler_params=pltpu.CompilerParams(vmem_limit_bytes=60*2**20,dimension_semantics=("arbitrary",)),
    )(ctx,x,cot,wo,wu,*wd,vec,bu)


def across_rows(left_side, right_side):
    return lax.dot_general(left_side, right_side, (((0,), (0,)), ((), ())), preferred_element_type=F32)


def weight_kernel(own, up_ref, normed_ref, hidden_ref, down_ref, att_ref, ctx_ref, out_ref, acc_ref):
    depth=normed_ref.shape[1]; k=pl.program_id(1)
    wide_rows=up_ref.shape[1]; rows=down_ref.shape[1]; parts=hidden_ref.shape[1]//depth
    @pl.when(k==0)
    def _(): acc_ref[...]=jnp.zeros_like(acc_ref)
    for lo in range(0,wide_rows,rows):
        acc_ref[lo:lo+rows]+=across_rows(up_ref[:,lo:lo+rows],normed_ref[...])
    for i in range(parts):
        at=wide_rows+i*rows
        acc_ref[at:at+rows]+=across_rows(down_ref[...],hidden_ref[:,i*depth:(i+1)*depth])
    at=wide_rows+parts*rows
    acc_ref[at:at+rows]+=across_rows(att_ref[...],ctx_ref[...])
    @pl.when(k==pl.num_programs(1)-1)
    def _():
        many=rows//own; lines=wide_rows//many
        out_ref[:,:lines]=acc_ref[:wide_rows].reshape(many,lines,depth).astype(BF)
        narrow=[acc_ref[wide_rows+i*rows:wide_rows+(i+1)*rows].reshape(many,own,depth) for i in range(parts+1)]
        narrow.append(jnp.zeros((many,out_ref.shape[1]-lines-(parts+1)*own,depth),F32))
        out_ref[:,lines:]=jnp.concatenate(narrow,axis=1).astype(BF)
def weight_grads(own, up, normed, hidden, down, att, ctx):
    T,D=normed.shape; F=up.shape[1]; halves=2; many=D//own//halves; block=512
    R=-(-(F//D*2+1)*own//16)*16
    if own%8:
        by=lambda a: a.reshape(D//own,-1,D)
        pieces=[by(across_rows(up,normed))]+[by(across_rows(down,hidden[:,i*D:(i+1)*D])) for i in range(F//D)]
        pieces.append(by(across_rows(att,ctx)))
        pieces.append(jnp.zeros((D//own,R-(F//D*2+1)*own,D),F32))
        return jnp.concatenate(pieces,axis=1).astype(BF)
    col=lambda w: pl.BlockSpec((block,w),lambda h,k:(k,h)); row=lambda w: pl.BlockSpec((block,w),lambda h,k:(k,0))
    return pl.pallas_call(functools.partial(weight_kernel,own),grid=(halves,T//block),
        in_specs=[col(F//halves),row(D),row(F),col(D//halves),col(D//halves),row(D)],
        out_specs=pl.BlockSpec((many,R,D),lambda h,k:(h,0,0)),
        out_shape=jax.ShapeDtypeStruct((D//own,R,D),BF),
        scratch_shapes=[pltpu.VMEM((many*own*(F//D*2+1),D),F32)],
        compiler_params=pltpu.CompilerParams(vmem_limit_bytes=60*2**20))(up,normed,hidden,down,att,ctx)


def digits():
    found = []
    for axis in ("wide", "narrow"):
        stride = lax.axis_size(axis) // 2
        while stride >= 1:
            found.append((axis, stride))
            stride //= 2
    return found


def link_order(number):
    count = len(digits())
    if lax.axis_size("wide") == 8 and lax.axis_size("narrow") == 4:
        return [(4, 2, 3, 1, 0), (4, 3, 1, 2, 0), (4, 1, 2, 3, 0)][number]
    return tuple(range(count - 1, -1, -1))


def exchange(values, axis, stride):
    return lax.ppermute(values, axis, [(i, i ^ stride) for i in range(lax.axis_size(axis))])


def digit_of(axis, stride):
    return (lax.axis_index(axis) // stride) % 2


def gather_rows(shards, others):
    places = digits()
    held = [shard.reshape((1,) * len(places) + shard.shape) for shard in shards]
    passed = []
    for step in range(len(places)):
        for number, values in enumerate(held):
            dim = link_order(number)[::-1][step]
            mine = digit_of(*places[dim])
            got = exchange(values, *places[dim])
            first = jnp.where(mine == 0, values, got)
            second = jnp.where(mine == 0, got, values)
            held[number] = jnp.concatenate([first, second], dim)
        if step == 2:
            held, others = lax.optimization_barrier((held, others))
        else:
            held = lax.optimization_barrier(held)
        passed.append(held[0])
    return [values.reshape((-1,) + values.shape[-2:]) for values in held], passed, others


def scatter_start(whole, own):
    return whole.reshape(whole.shape[:-2] + (2,) * len(digits()) + (own, whole.shape[-1]))


def scatter_step(held, number, step):
    places = digits()
    dim = link_order(number)[step] + held.ndim - 2 - len(places)
    place = places[link_order(number)[step]]
    mine = digit_of(*place)
    keep = lax.dynamic_slice_in_dim(held, mine, 1, dim).astype(F32)
    send = lax.dynamic_slice_in_dim(held, 1 - mine, 1, dim).astype(BF)
    return keep + exchange(send, *place).astype(F32)


def scatter_rest(held, number, step):
    for later in range(step, len(digits())):
        held = scatter_step(held, number, later)
    return held.reshape(held.shape[: held.ndim - 2 - len(digits())] + held.shape[-2:])


def shards(
    inputs,
    tok_landmark,
    landmark_doc,
    w_query,
    b_query,
    w_key,
    w_value,
    b_value,
    conv_weight,
    w_out,
    b_out,
    gain_one,
    shift_one,
    w_up,
    b_up,
    w_down,
    b_down,
    gain_two,
    shift_two,
    cotangent,
):
    batch_rows, sequence_length, feature_width = inputs.shape
    group_count = lax.axis_size("wide") * lax.axis_size("narrow")
    own = feature_width // group_count
    tokens = batch_rows * sequence_length
    lines = b_up.shape[0] // own
    vectors = (b_query, b_value, b_out, gain_one, shift_one, b_down, gain_two, shift_two)
    flat = 0
    for place, vector in enumerate(vectors + (b_up,)):
        before = place * own
        flat = flat + jnp.pad(vector, (before, (8 + lines) * own - before - vector.shape[0]))
    small = jnp.concatenate([conv_weight, flat.reshape(8 + lines, own)])
    small = jnp.pad(small.T, ((0, 0), (0, 128 - small.shape[0])))
    member = tok_landmark[:, None, :] == jnp.arange(LM)[None, :, None]
    means = jnp.einsum("bjt,bti->bji", member.astype(BF), inputs, preferred_element_type=F32)
    means = means / jnp.sum(member, axis=2)[..., None].astype(F32)
    doc = jnp.sum(jnp.where(member, landmark_doc[:, :, None], 0), axis=1)
    bounds = jnp.sum(doc[:, None, :] < jnp.arange(DOCS + 1)[None, :, None], axis=2).astype(jnp.int32)
    (gathered_v, w_q, w_k), passed, (means, bounds) = gather_rows(
        [jnp.concatenate([w_value.T, small], axis=1), w_query.T, w_key.T], (means, bounds)
    )
    w_q = w_q.reshape(feature_width, feature_width)
    w_k = w_k.reshape(feature_width, feature_width)
    gathered_v = gathered_v.reshape(feature_width, feature_width + 128)
    w_v = gathered_v[:, :feature_width]
    small = gathered_v[:, feature_width:]
    b_u = jnp.moveaxis(small[:, KW + 8 : KW + 8 + lines].reshape(group_count, own, lines), 1, 2)
    b_u = b_u.reshape(1, -1).astype(F32)
    small = small.astype(F32).T
    ff_count = w_down.shape[0] // feature_width
    w_out, w_up, w_down, _ = lax.optimization_barrier((w_out, w_up, w_down, passed[0]))
    shard = jnp.concatenate(
        [w_up.T, w_out.T] + [w_down[i * feature_width : (i + 1) * feature_width].T for i in range(ff_count)]
    )
    gathered = lax.all_gather(shard, ("wide", "narrow"), axis=0)
    w_o = gathered[:, own * lines : own * (1 + lines)].reshape(feature_width, feature_width)
    w_u = gathered if own * lines % 16 == 0 else gathered[:, : own * lines].reshape(1, -1, feature_width)
    w_d = [
        gathered[:, own * (1 + lines + i) : own * (2 + lines + i)].reshape(feature_width, feature_width)
        for i in range(ff_count)
    ]
    rows_low = inputs.reshape(tokens, feature_width)
    value_rows, conv_part = conv_fwd(bounds, inputs, w_v, small)
    q, k, v, k1, k3, inv, stash, landmarks, context = att_fwd(
        inputs, means, w_q, w_k, w_v, small, tok_landmark, landmark_doc, conv_part
    )
    context = context.reshape(tokens, feature_width)
    layer_out, normed, hidden, down_low, up_low, grad_one, att_low, sums, sums_up = ffn(
        context, rows_low, cotangent.reshape(tokens, feature_width), w_o, w_u, w_d, small, b_u
    )
    grads = weight_grads(own, up_low, normed, hidden, down_low, att_low, context)
    share = lax.psum_scatter(grads, ("wide", "narrow"), scatter_dimension=0, tiled=True)[0]
    w_plain = w_o.T
    att_low = att_low.reshape(inputs.shape)
    dq, dk, dv, grad_qk, sum_q = att_bwd(
        inputs, att_low, w_plain, q, k, v, k1, k3, inv, stash, landmarks, tok_landmark
    )
    more = (sum_q, sums, sums_up.reshape(feature_width, lines))
    moving = scatter_start(grad_qk, own)
    calls, before = 2, ()
    slabs = feature_width // 128 // calls
    for call in range(calls):
        moved = scatter_step(moving, 1, call)
        before = conv_bwd(
            bounds, value_rows, att_low, w_o, small, inputs, dv, more, before, slabs, call * slabs
        )
        before, att_low, moving = lax.optimization_barrier((tuple(before), att_low, moved))
    dv, grad_v = before
    moved = scatter_start(grad_v, own)

    def through(grad, weight):
        return jnp.einsum("bot,oi->bti", grad, weight, preferred_element_type=F32)

    parts = ()
    for number in range(len(digits())):
        moved = scatter_step(moved, 0, number)
        if calls + number < len(digits()):
            moving = scatter_step(moving, 1, calls + number)
        if number == 0:
            moved, moving, dq = lax.optimization_barrier((moved, moving, dq))
            parts = (through(dq, w_q),)
        elif number == 1:
            moved, moving, dk, parts = lax.optimization_barrier((moved, moving, dk, parts))
            parts = parts + (through(dk, w_k),)
        elif number == 2:
            moved, dv, parts = lax.optimization_barrier((moved, dv, parts))
            input_grad = grad_one.reshape(inputs.shape) + parts[0] + parts[1] + through(dv, w_v)
        elif number == len(digits()) - 2:
            moved, share, input_grad = lax.optimization_barrier((moved, share, input_grad))
    share_qk = moving.reshape(moving.shape[:1] + moving.shape[-2:])
    share_v = moved.reshape(moved.shape[-2:])
    late = share_v[:, feature_width:]
    share = share.astype(F32)
    share_down = share[own * lines : 2 * own * lines].reshape(ff_count, own, feature_width)
    share_out = share[2 * own * lines : 2 * own * lines + own]
    return (
        layer_out.reshape(inputs.shape),
        input_grad,
        share_qk[0].T,
        late[:, KW + 1],
        share_qk[1].T,
        share_v[:, :feature_width].T,
        late[:, KW],
        late[:, :KW].T,
        share_out.T,
        late[:, KW + 2],
        late[:, KW + 3],
        late[:, KW + 4],
        share[: own * lines].T,
        late[:, KW + 8 : KW + 8 + lines].reshape(-1),
        jnp.moveaxis(share_down, 1, 2).reshape(-1, own),
        late[:, KW + 5],
        late[:, KW + 6],
        late[:, KW + 7],
    )


def solution(mesh):
    return jax.shard_map(
        shards,
        mesh=mesh,
        in_specs=(
            P(("wide", "narrow"), None, None),
            P(("wide", "narrow"), None),
            P(("wide", "narrow"), None),
            P(None, ("wide", "narrow")),
            P(("wide", "narrow")),
            P(None, ("wide", "narrow")),
            P(None, ("wide", "narrow")),
            P(("wide", "narrow")),
            P(None, ("wide", "narrow")),
            P(None, ("wide", "narrow")),
            P(("wide", "narrow")),
            P(("wide", "narrow")),
            P(("wide", "narrow")),
            P(None, ("wide", "narrow")),
            P(("wide", "narrow")),
            P(None, ("wide", "narrow")),
            P(("wide", "narrow")),
            P(("wide", "narrow")),
            P(("wide", "narrow")),
            P(("wide", "narrow"), None, None),
        ),
        out_specs=(
            P(("wide", "narrow"), None, None),
            P(("wide", "narrow"), None, None),
            P(None, ("wide", "narrow")),
            P(("wide", "narrow")),
            P(None, ("wide", "narrow")),
            P(None, ("wide", "narrow")),
            P(("wide", "narrow")),
            P(None, ("wide", "narrow")),
            P(None, ("wide", "narrow")),
            P(("wide", "narrow")),
            P(("wide", "narrow")),
            P(("wide", "narrow")),
            P(None, ("wide", "narrow")),
            P(("wide", "narrow")),
            P(None, ("wide", "narrow")),
            P(("wide", "narrow")),
            P(("wide", "narrow")),
            P(("wide", "narrow")),
        ),
        check_vma=False,
    )
```
